32 devices in a mesh: dp: 8 (over z, core), fsdp: 4 (over y, x).
Axes of the slice: x: 2, y: 2, z: 4, core: 2. Of those that a mesh axis runs over, the one named last changes fastest.
Arguments:
- hidden: bfloat16 [128, 512, 768], P(('dp', 'fsdp')), may hold values from -6 to 6
- lengths: int32 [128], P(('dp', 'fsdp')), may hold values from 40 to 512, as said below
- key_mask: int32 [128, 512], P(('dp', 'fsdp')), may hold values from 0 to 1, as said below
- cotangent: bfloat16 [128, 256, 768], P(('dp', 'fsdp')), may hold values from -6 to 6
- attention_weight: float32 [5, 768, 768], P(None, ('dp', 'fsdp')), may hold values from -0.3125 to 0.3125
- expand_weight: float32 [768, 3072], P(('dp', 'fsdp')), may hold values from -0.21875 to 0.21875
- contract_weight: float32 [3072, 768], P(('dp', 'fsdp')), may hold values from -0.109375 to 0.109375
- small_params: float32 [13, 768], P(None, ('dp', 'fsdp')), may hold values from -1.5 to 1.5, as said below
- mean_attention: float32 [5, 768, 768], P(None, ('dp', 'fsdp')), may hold values from -192 to 192
- mean_expand: float32 [768, 3072], P(('dp', 'fsdp')), may hold values from -192 to 192
- mean_contract: float32 [3072, 768], P(('dp', 'fsdp')), may hold values from -192 to 192
- mean_small: float32 [13, 768], P(None, ('dp', 'fsdp')), may hold values from -192 to 192
- square_attention: float32 [5, 768, 768], P(None, ('dp', 'fsdp')), may hold values from 512 to 8192
- square_expand: float32 [768, 3072], P(('dp', 'fsdp')), may hold values from 512 to 8192
- square_contract: float32 [3072, 768], P(('dp', 'fsdp')), may hold values from 512 to 8192
- square_small: float32 [13, 768], P(None, ('dp', 'fsdp')), may hold values from 512 to 8192
- update_step: int32 [1], replicated, may hold values from 1 to 19
- update_rates: float32 [4], replicated, may hold values from 0.05 to 0.95, as said below
Outputs:
- pooled_out: bfloat16 [128, 256, 768], P(('dp', 'fsdp'))
- input_grad: bfloat16 [128, 512, 768], P(('dp', 'fsdp'))
- attention_grad: float32 [5, 768, 768], P(None, ('dp', 'fsdp'))
- expand_grad: float32 [768, 3072], P(('dp', 'fsdp'))
- contract_grad: float32 [3072, 768], P(('dp', 'fsdp'))
- small_grad: float32 [13, 768], P(None, ('dp', 'fsdp'))
- attention_next: float32 [5, 768, 768], P(None, ('dp', 'fsdp'))
- expand_next: float32 [768, 3072], P(('dp', 'fsdp'))
- contract_next: float32 [3072, 768], P(('dp', 'fsdp'))
- small_next: float32 [13, 768], P(None, ('dp', 'fsdp'))
- attention_mean: float32 [5, 768, 768], P(None, ('dp', 'fsdp'))
- expand_mean: float32 [768, 3072], P(('dp', 'fsdp'))
- contract_mean: float32 [3072, 768], P(('dp', 'fsdp'))
- small_mean: float32 [13, 768], P(None, ('dp', 'fsdp'))
- attention_square: float32 [5, 768, 768], P(None, ('dp', 'fsdp'))
- expand_square: float32 [768, 3072], P(('dp', 'fsdp'))
- contract_square: float32 [3072, 768], P(('dp', 'fsdp'))
- small_square: float32 [13, 768], P(None, ('dp', 'fsdp'))
The draws below stay inside these ranges and needn't reach their ends.
Inputs may be any that keep to these rules, and one draw needn't show every extreme that they name: `lengths`: in every aligned block of 8 sequences at least one has 512 tokens; every sequence has at least 40. `key_mask`: position 0 of every sequence is 1. `small_params`: rows 4 and 7 lie between 0.55 and 1.45. `update_rates`: learning rate first, then the two moment decays, then weight decay.
All inputs are finite; a program needn't handle non-finite values.
Results may differ from the reference program's by a relative error of at most 0.015.
The reference program's roundings to bfloat16 on the way count: a program that leaves them out, or rounds other values in their place, can miss the bound.
Values may be sent and summed in bfloat16 or wider, within the bound.
No kernel may reach another device: no remote copies, remote signals or barrier semaphores. Data moves between devices by JAX's collectives and lax.ppermute only.
A program may use at most 256 MiB of HBM per device.

```python
import math
import jax
import jax.numpy as jnp
from jax import lax

D = 768
HEADS = 12
HEAD = 64
FF = 3072
SEQ = 512
POOLED = 256
ROWS = 128
VEC = 13


def draw_lengths(key, part):
    drawn = jax.random.randint(jax.random.fold_in(key, 11), (ROWS,), SEQ // 13 + 1, SEQ + 1, dtype=jnp.int32)
    chosen = jax.random.randint(jax.random.fold_in(key, 12), (ROWS // 8,), 0, 8, dtype=jnp.int32)
    places = jnp.arange(ROWS, dtype=jnp.int32)
    full_rows = places % 8 == jnp.repeat(chosen, 8)
    return jnp.where(full_rows, SEQ, drawn).astype(jnp.int32)


def draw_key_mask(key, part):
    coins = jax.random.randint(jax.random.fold_in(key, 21), (ROWS, SEQ), 0, 20, dtype=jnp.int32)
    kept = (coins < 17).astype(jnp.int32)
    return kept.at[:, 0].set(1)


def draw_small_params(key, part):
    rows_total = 9 + FF // D
    noise = jax.random.normal(jax.random.fold_in(key, 31), (rows_total, D), jnp.float32)
    noise = jnp.clip(noise, -3.0, 3.0)
    index = jnp.arange(rows_total, dtype=jnp.int32)[:, None]
    scales = jnp.where(index < 2, 0.5, 0.3).astype(jnp.float32)
    gains = (index == 4) | (index == 7)
    return jnp.where(gains, 1.0 + 0.15 * noise, scales * noise).astype(jnp.float32)


def draw_update_rates(key, part):
    learning = jax.random.uniform(jax.random.fold_in(key, 41), (1,), jnp.float32, 0.1, 0.25)
    first_decay = jax.random.uniform(jax.random.fold_in(key, 42), (1,), jnp.float32, 0.8, 0.95)
    second_decay = jax.random.uniform(jax.random.fold_in(key, 43), (1,), jnp.float32, 0.5, 0.8)
    weight_decay = jax.random.uniform(jax.random.fold_in(key, 44), (1,), jnp.float32, 0.05, 0.2)
    return jnp.concatenate([learning, first_decay, second_decay, weight_decay]).astype(jnp.float32)


def block_scale(key, dims, shards, least, top_value):
    gain = 1.0
    for axis_at, parts in shards:
        draws = jax.random.uniform(jax.random.fold_in(jax.random.fold_in(key, 6), axis_at), (parts,), jnp.float32, least / len(shards), top_value / len(shards))
        gain = gain * jnp.repeat(jnp.exp(draws), dims[axis_at] // parts).reshape((-1,) + (1,) * (len(dims) - 1 - axis_at))
    return gain


def bell_draw(stream_key, shape, scale, bound, pieces=(), kind=jnp.bfloat16):
    values = scale * jax.random.normal(stream_key, shape, jnp.float32)
    if pieces:
        values = values * block_scale(stream_key, shape, pieces, -0.22, 0.18)
    return jnp.clip(values, -bound, bound).astype(kind)


def setup_inputs(seed: int = 0) -> dict:
    seeds = jax.random.split(jax.random.key(seed), 19)
    return {
        "hidden": bell_draw(seeds[0], (ROWS, SEQ, D), 1.0, 6.0, ((0, 32),)),
        "lengths": draw_lengths(jax.random.fold_in(seeds[18], 71), 0),
        "key_mask": draw_key_mask(jax.random.fold_in(seeds[18], 71), 0),
        "cotangent": bell_draw(seeds[3], (ROWS, POOLED, D), 1.0, 6.0, ((0, 32),)),
        "attention_weight": bell_draw(seeds[4], (5, D, D), (D // 2) ** -0.5, 0.3125, ((1, 32),), jnp.float32),
        "expand_weight": bell_draw(seeds[5], (D, FF), D ** -0.5, 0.21875, ((0, 32),), jnp.float32),
        "contract_weight": bell_draw(seeds[6], (FF, D), FF ** -0.5, 0.109375, ((0, 32),), jnp.float32),
        "small_params": draw_small_params(jax.random.fold_in(seeds[18], 71), 0),
        "mean_attention": bell_draw(seeds[8], (5, D, D), ((ROWS * SEQ // 64) ** 0.5), 192.0, ((1, 32),), jnp.float32),
        "mean_expand": bell_draw(seeds[9], (D, FF), ((ROWS * SEQ // 64) ** 0.5), 192.0, ((0, 32),), jnp.float32),
        "mean_contract": bell_draw(seeds[10], (FF, D), ((ROWS * SEQ // 64) ** 0.5), 192.0, ((0, 32),), jnp.float32),
        "mean_small": bell_draw(seeds[11], (VEC, D), ((ROWS * SEQ // 64) ** 0.5), 192.0, ((1, 32),), jnp.float32),
        "square_attention": jnp.clip(jnp.exp(math.log(8192.0) - 2.7725887 * jax.random.uniform(seeds[12], (5, D, D), jnp.float32) ** block_scale(seeds[12], (5, D, D), ((1, 32),), -0.2, 0.2)), 512.0, 8192.0),
        "square_expand": jnp.clip(jnp.exp(math.log(8192.0) - 2.7725887 * jax.random.uniform(seeds[13], (D, FF), jnp.float32) ** block_scale(seeds[13], (D, FF), ((0, 32),), -0.2, 0.2)), 512.0, 8192.0),
        "square_contract": jnp.clip(jnp.exp(math.log(8192.0) - 2.7725887 * jax.random.uniform(seeds[14], (FF, D), jnp.float32) ** block_scale(seeds[14], (FF, D), ((0, 32),), -0.2, 0.2)), 512.0, 8192.0),
        "square_small": jnp.clip(jnp.exp(math.log(8192.0) - 2.7725887 * jax.random.uniform(seeds[15], (VEC, D), jnp.float32) ** block_scale(seeds[15], (VEC, D), ((1, 32),), -0.2, 0.2)), 512.0, 8192.0),
        "update_step": jax.random.randint(seeds[16], (1,), 1, 20).astype(jnp.int32),
        "update_rates": draw_update_rates(jax.random.fold_in(seeds[18], 71), 0),
    }


EPSILON = 1e-06
SCORE_SCALE = 0.125
MASK_FILL = -1000000000.0

@jax.custom_vjp
def low(v):
    return lax.optimization_barrier(v.astype(jnp.bfloat16)).astype(jnp.float32)

@jax.custom_vjp
def low_back(v):
    return v

def low_keep(v):
    return (low(v), None)

def low_pass(kept, grad):
    return (grad,)

def back_keep(v):
    return (v, None)

def back_low(kept, grad):
    return (low(grad),)
low.defvjp(low_keep, low_pass)
low_back.defvjp(back_keep, back_low)

def rel_table(length, width):
    places = length - jnp.arange(2 * length, dtype=jnp.float32)
    half_width = width // 2
    frequency = jnp.exp(jnp.arange(half_width, dtype=jnp.float32) * (-2.0 * math.log(10000.0) / width))
    angles = places[:, None] * frequency[None, :]
    return jnp.concatenate([jnp.sin(angles), jnp.cos(angles)], axis=1)

def shift_rel(table_scores, length):
    leading = table_scores.shape[:-2]
    rows_here = table_scores.shape[-2]
    flat = table_scores.reshape(leading + (rows_here * 2 * length,))
    middle = lax.slice_in_dim(flat, length, length + rows_here * (2 * length - 2), axis=flat.ndim - 1)
    return middle.reshape(leading + (rows_here, 2 * length - 2))[..., :length]

def normalize(values):
    center = values - lax.optimization_barrier(jnp.mean(values, axis=-1, keepdims=True))
    spread = lax.optimization_barrier(jnp.mean(center * center, axis=-1, keepdims=True))
    return center * lax.rsqrt(spread + EPSILON)

def layer(hidden_rows, attention, expand, contract, small_vals, key_bias, pooled_mask, rel_place):
    rows_count, length, width = hidden_rows.shape
    pooled_len = length // 2
    highest = lax.Precision.HIGHEST
    pooled = lax.optimization_barrier(jnp.mean(hidden_rows.reshape(rows_count, pooled_len, 2, width), axis=2))
    query = low_back(jnp.einsum('bpd,de->bpe', low(pooled), attention[0], precision=highest))
    keys_low = low(low_back(jnp.einsum('bsd,de->bse', hidden_rows, attention[1], precision=highest)))
    values_low = low(low_back(jnp.einsum('bsd,de->bse', hidden_rows, attention[2], precision=highest)) + small_vals[2])
    rel_heads = low(jnp.dot(low(rel_place), attention[3], precision=highest)).reshape(2 * length, HEADS, HEAD)
    query_content = low(query + small_vals[0])
    query_place = low(query + small_vals[1])

    def attend(inputs):
        content_row, place_row, keys_row, values_row, bias_row = inputs
        content_heads = content_row.reshape(pooled_len, HEADS, HEAD)
        place_heads = place_row.reshape(pooled_len, HEADS, HEAD)
        keys_heads = keys_row.reshape(length, HEADS, HEAD)
        values_heads = values_row.reshape(length, HEADS, HEAD)
        content = jnp.einsum('phe,she->hps', content_heads, keys_heads, precision=highest)
        placed = jnp.einsum('phe,mhe->hpm', place_heads, rel_heads, precision=highest)
        raw = low_back(content + shift_rel(placed, length))
        scores = raw * SCORE_SCALE + bias_row[None, None, :]
        probs = jax.nn.softmax(scores, axis=-1)
        context = jnp.einsum('hps,she->phe', low(probs), values_heads, precision=highest)
        return low(low_back(context)).reshape(pooled_len, width)
    context_low = lax.map(jax.checkpoint(attend), (query_content, query_place, keys_low, values_low, key_bias))
    branch = low_back(jnp.einsum('bpe,ed->bpd', context_low, attention[4], precision=highest)) + small_vals[3]
    first_out = normalize(pooled + branch) * small_vals[4] + small_vals[5]
    inner = low_back(jnp.einsum('bpd,df->bpf', low(first_out), expand, precision=highest)) + small_vals[9:].reshape(-1)
    activated = jax.nn.gelu(inner, approximate=False)
    second = first_out + low_back(jnp.einsum('bpf,fd->bpd', low(activated), contract, precision=highest)) + small_vals[6]
    return (normalize(second) * small_vals[7] + small_vals[8]) * pooled_mask[:, :, None]

def adamw(weight, moment, second, gradient, step_value, rates):
    new_moment = rates[1] * moment + (1.0 - rates[1]) * gradient
    new_second = rates[2] * second + (1.0 - rates[2]) * gradient * gradient
    moment_hat = new_moment / (1.0 - jnp.power(rates[1], step_value))
    second_hat = new_second / (1.0 - jnp.power(rates[2], step_value))
    new_weight = weight - rates[0] * (moment_hat / (jnp.sqrt(second_hat) + 1e-08) + rates[3] * weight)
    return (new_weight, new_moment, new_second)

def reference(hidden, lengths, key_mask, cotangent, attention_weight, expand_weight, contract_weight, small_params, mean_attention, mean_expand, mean_contract, mean_small, square_attention, square_expand, square_contract, square_small, update_step, update_rates):
    masters = (attention_weight, expand_weight, contract_weight, small_params)
    params = tuple((master.astype(jnp.bfloat16).astype(jnp.float32) for master in masters))
    positions = jnp.arange(SEQ, dtype=jnp.int32)
    valid_keys = (key_mask == 1) & (positions[None, :] < lengths[:, None])
    key_bias = jnp.where(valid_keys, 0.0, MASK_FILL).astype(jnp.float32)
    pooled_mask = lax.optimization_barrier(jnp.max(valid_keys.astype(jnp.float32).reshape(ROWS, SEQ // 2, 2), axis=2))
    rel_place = rel_table(SEQ, D)
    group_rows = math.gcd(ROWS, max(1, 4096 // SEQ))
    group_count = ROWS // group_rows
    blocks_in = (hidden.astype(jnp.float32).reshape(group_count, group_rows, SEQ, D), key_bias.reshape(group_count, group_rows, SEQ), pooled_mask.reshape(group_count, group_rows, SEQ // 2), cotangent.astype(jnp.float32).reshape(group_count, group_rows, SEQ // 2, D))

    def one_group(totals, blocks):
        hidden_block, bias_block, mask_block, cot_block = blocks

        def forward(hidden_rows, attention, expand, contract, small_vals):
            return layer(hidden_rows, attention, expand, contract, small_vals, bias_block, mask_block, rel_place)
        result, pullback = jax.vjp(forward, hidden_block, params[0], params[1], params[2], params[3])
        gradients = pullback(cot_block)
        totals = tuple((total + gradient for total, gradient in zip(totals, gradients[1:])))
        return (totals, (result.astype(jnp.bfloat16), gradients[0].astype(jnp.bfloat16)))
    initial = tuple((jnp.zeros(param.shape, jnp.float32) for param in params))
    totals, (outputs, inward) = lax.scan(one_group, initial, blocks_in)
    pooled_out = outputs.reshape(ROWS, SEQ // 2, D)
    input_grad = inward.reshape(ROWS, SEQ, D)
    step_value = update_step[0].astype(jnp.float32)
    moments = (mean_attention, mean_expand, mean_contract, mean_small)
    seconds = (square_attention, square_expand, square_contract, square_small)
    updated = [adamw(masters[index], moments[index], seconds[index], totals[index], step_value, update_rates) for index in range(4)]
    return (pooled_out, input_grad, totals[0], totals[1], totals[2], totals[3], updated[0][0], updated[1][0], updated[2][0], updated[3][0], updated[0][1], updated[1][1], updated[2][1], updated[3][1], updated[0][2], updated[1][2], updated[2][2], updated[3][2])
```

```python
import functools
import math

import jax
import jax.numpy as jnp
from jax import lax
from jax.experimental import pallas as pl
from jax.experimental.pallas import tpu as pltpu
from jax.sharding import PartitionSpec as P

HEAD = 64
GC = 256
GH = GC // HEAD
FC = 768
EPSILON = 1e-06
MASK_FILL = -1000000000.0
ALL = ("dp", "fsdp")
F32 = jnp.float32
BF = jnp.bfloat16
VMEM = 58 << 20
NT = (((1,), (1,)), ((), ()))
TN = (((0,), (0,)), ((), ()))


def dot(a, b):
    return jnp.dot(a, b, preferred_element_type=F32)


def dot_nt(a, b):
    return lax.dot_general(a, b, NT, preferred_element_type=F32)


def dot_tn(a, b):
    return lax.dot_general(a, b, TN, preferred_element_type=F32)


def sds(shape, dtype):
    return jax.ShapeDtypeStruct(shape, dtype)


def seqs(*tail):
    return pl.BlockSpec((1,) + tail, lambda s, *_: (s,) + (0,) * len(tail))


def whole(*shape):
    return pl.BlockSpec(shape, lambda *_: (0,) * len(shape), pipeline_mode=pl.Buffered(1))


def params():
    return pltpu.CompilerParams(vmem_limit_bytes=VMEM)


def cost(macs, moved, exps=0):
    return pl.CostEstimate(flops=int(2 * macs), bytes_accessed=int(moved), transcendentals=int(exps))


def rel_table(length, width):
    places = length - jnp.arange(2 * length, dtype=F32)
    half_width = width // 2
    frequency = jnp.exp(jnp.arange(half_width, dtype=F32) * (-2.0 * math.log(10000.0) / width))
    angles = places[:, None] * frequency[None, :]
    return jnp.concatenate([jnp.sin(angles), jnp.cos(angles)], axis=1)


X, Y, CORE, Z = 1, 2, 4, 8
HALVES = ((X, Y), (Y, X))


def pairs(bit):
    return [(d, d ^ bit) for d in range(32)]


def swap(a, bit):
    return lax.ppermute(a, ALL, pairs(bit))


def flat_of(rel, half):
    low, high = HALVES[half]
    return (rel & 3) * Z + (rel >> 2 & 1) * low + (rel >> 3 & 1) * high + (rel >> 4 & 1) * CORE


def after(x, *earlier):
    return lax.optimization_barrier((x, earlier))[0]


def assemble_kernel(stacked, me_ref, *refs):
    ins, outs = refs[:8], refs[8:]
    for half in range(2):
        for rel in range(32):
            k = jnp.bitwise_xor(me_ref[0], flat_of(rel, half))
            src = ins[4 * half + rel // 8]
            n, r = src.shape[1], src.shape[2]
            for i in range(n):
                if stacked:
                    outs[half][i, k] = src[rel % 8, i]
                else:
                    outs[0][k, half * r : (half + 1) * r, :] = src[rel % 8, i]


def gather(me, part, split, stacked=True, gate=None):
    n, r, c = part.shape
    along = [part] + [swap(part, k * Z) for k in range(1, 4)]
    halves = [jnp.stack([p[:split] for p in along]), jnp.stack([p[split:] for p in along])]
    token = halves[0]
    firsts = [jnp.concatenate([h, swap(h, HALVES[i][0])], axis=0) for i, h in enumerate(halves)]
    seconds = [swap(h, HALVES[i][1]) for i, h in enumerate(firsts)]
    ins = []
    for f, s in zip(firsts, seconds):
        ins += [f, s, swap(f, CORE), swap(s, CORE)]
    shapes = [(split, 32, r, c), (n - split, 32, r, c)] if stacked else [(32, n * r, c)]
    out = pl.pallas_call(
        functools.partial(assemble_kernel, stacked),
        in_specs=[pl.BlockSpec(memory_space=pltpu.SMEM)] + [pl.BlockSpec(memory_space=pltpu.VMEM)] * 8,
        out_specs=[pl.BlockSpec(memory_space=pltpu.VMEM)] * len(shapes),
        out_shape=[sds(shape, part.dtype) for shape in shapes],
        cost_estimate=cost(0, 4 * 32 * n * r * c),
        compiler_params=params(),
    )(me, *ins)
    if stacked:
        return token, [o.reshape(o.shape[0], 32 * r, c) for o in out]
    return token, out[0].reshape(32 * n * r, c)


def merge_kernel(counts, last, *refs):
    pairs_in = 2 * sum(counts)
    ins, outs = refs[:pairs_in], refs[pairs_in:]
    at = 0
    block = 0
    for half, count in enumerate(counts):
        mine = 0
        for _ in range(count):
            kept, got = ins[at], ins[at + 1]
            at += 2
            n, m = kept.shape[0], kept.shape[1]
            for j in range(n):
                v = (kept[j].astype(F32) + got[j].astype(F32)).astype(BF)
                if last:
                    outs[j][block : block + m] = v
                else:
                    outs[2 * half + (j >= n // 2)][j % (n // 2), mine : mine + m] = v
            mine += m
            block += m


def merge(parts, last):
    counts = [len(p) for p in parts]
    flat = [a for p in parts for pair in p for a in pair]
    n, _, r, c = flat[0].shape
    blocks = [sum(pair[0].shape[1] for pair in p) for p in parts]
    if last:
        shapes = [(sum(blocks), r, c)] * n
    else:
        shapes = [(n // 2, m, r, c) for m in blocks for _ in range(2)]
    return pl.pallas_call(
        functools.partial(merge_kernel, counts, last),
        in_specs=[pl.BlockSpec(memory_space=pltpu.VMEM)] * len(flat),
        out_specs=[pl.BlockSpec(memory_space=pltpu.VMEM)] * len(shapes),
        out_shape=[sds(shape, BF) for shape in shapes],
        cost_estimate=cost(0, 6 * n * sum(blocks) * r * c),
        compiler_params=params(),
    )(*flat)


class Reduction:
    def __init__(self, *halves):
        self.parts = [[(k, swap(s, CORE)) for k, s in half] for half in halves]
        self.stage = 0

    def step(self, *earlier):
        parts = self.parts
        if earlier:
            parts = after(parts, *earlier)
        if self.stage < 2:
            k0, s0, k1, s1 = merge(parts, False)
            self.parts = [[(k, swap(s, HALVES[i][1 - self.stage]))] for i, (k, s) in enumerate(((k0, s0), (k1, s1)))]
            self.token = (k0, k1)
        else:
            sums = merge(parts, True)
            self.terms = [sums[0]] + [swap(sums[k], k * Z) for k in range(1, 4)]
            self.token = (sums[0],)
        self.stage += 1
        return self


def prepare_kernel(hidden_ref, pooled_ref, low_ref, hidt_ref, lowt_ref, wide):
    hid = hidden_ref[0]
    half = pooled_ref.shape[1]
    hidt_ref[0] = hid.T
    columns = []
    for i in range(wide.shape[0]):
        wide[i] = hid[:, i * 128 : (i + 1) * 128].astype(F32)
        columns.append((wide[i, pl.ds(0, half, stride=2), :] + wide[i, pl.ds(1, half, stride=2), :]) * 0.5)
    pooled = jnp.concatenate(columns, axis=1)
    pooled_ref[0] = pooled
    low = pooled.astype(BF)
    low_ref[0] = low
    lowt_ref[0] = low.T


def prepare(hidden):
    B, L, D = hidden.shape
    R = L // 2
    return pl.pallas_call(
        prepare_kernel,
        grid=(B,),
        in_specs=[seqs(L, D)],
        out_specs=[seqs(R, D), seqs(R, D), seqs(D, L), seqs(D, R)],
        out_shape=[sds((B, R, D), F32), sds((B, R, D), BF), sds((B, D, L), BF), sds((B, D, R), BF)],
        scratch_shapes=[pltpu.VMEM((D // 128, L, 128), F32)],
        cost_estimate=cost(0, 8 * B * L * D),
        compiler_params=params(),
    )(hidden)


def attend_kernel(hidden_ref, pooled_ref, wq_ref, wk_ref, wv_ref, wr_ref, table_ref, small_ref, bias_ref,
                  ctx_ref, probs_ref, qu_ref, qw_ref, keys_ref, values_ref, rel_ref, rel_scr):
    half = hidden_ref.shape[1] // 2
    blk = half // 2

    @pl.when(pl.program_id(1) == 0)
    def _():
        rel = dot(table_ref[...], wr_ref[0]).astype(BF)
        rel_scr[...] = rel
        rel_ref[...] = rel

    hid = hidden_ref[0]
    q = dot(pooled_ref[0], wq_ref[0])
    qu = (q + small_ref[0:1, :]).astype(BF)
    qw = (q + small_ref[1:2, :]).astype(BF)
    qu_ref[0] = qu
    qw_ref[0] = qw
    keys_ref[0] = dot(hid, wk_ref[0]).astype(BF)
    values_ref[0] = (dot(hid, wv_ref[0]) + small_ref[2:3, :]).astype(BF)
    bias = bias_ref[0]
    lane = lax.broadcasted_iota(jnp.int32, (1, GC), 1)
    for b in range(2):
        rows = slice(b * blk, (b + 1) * blk)
        m0 = half * (1 - b)
        total = None
        for h in range(GH):
            mine = (lane >= h * HEAD) & (lane < (h + 1) * HEAD)
            quh = jnp.where(mine, qu[rows].astype(F32) * 0.125, 0.0).astype(BF)
            qwh = jnp.where(mine, qw[rows].astype(F32) * 0.125, 0.0).astype(BF)
            content = dot_nt(quh, keys_ref[0])
            placed = dot_nt(qwh, rel_scr[m0 : m0 + 3 * half, :])
            moved = pltpu.roll(placed, 0, 1, stride=2, stride_axis=0)[:, half:]
            s = content + moved + bias
            top = jnp.max(s, axis=-1, keepdims=True)
            e = jnp.exp(s - top)
            p = e * (1.0 / jnp.sum(e, axis=-1, keepdims=True))
            probs_ref[0, 0, h, rows, :] = p
            c = dot(p.astype(BF), values_ref[0])
            total = c if total is None else jnp.where(mine, c, total)
        ctx_ref[0, rows, :] = total.astype(BF)


def attend(hidden, pooled_low, weights_qk, weights_vr, table, small, bias):
    B, L, D = hidden.shape
    R = L // 2
    G = D // GC
    seq = lambda r: pl.BlockSpec((1, r, D), lambda g, s: (s, 0, 0))
    mat = lambda m: pl.BlockSpec((1, D, GC), lambda g, s: (m * G + g, 0, 0))
    so = lambda r: pl.BlockSpec((1, r, GC), lambda g, s: (s, 0, g))
    col = lambda r: pl.BlockSpec((r, GC), lambda g, s: (0, g))
    return pl.pallas_call(
        attend_kernel,
        grid=(G, B),
        in_specs=[seq(L), seq(R), mat(0), mat(1), mat(0), mat(1),
                  pl.BlockSpec((2 * L, D), lambda g, s: (0, 0)), col(small.shape[0]),
                  pl.BlockSpec((1, 1, L), lambda g, s: (s, 0, 0))],
        out_specs=[so(R), pl.BlockSpec((1, 1, GH, R, L), lambda g, s: (s, g, 0, 0, 0)),
                   so(R), so(R), so(L), so(L), col(2 * L)],
        out_shape=[sds((B, R, D), BF), sds((B, G, GH, R, L), F32), sds((B, R, D), BF), sds((B, R, D), BF),
                   sds((B, L, D), BF), sds((B, L, D), BF), sds((2 * L, D), BF)],
        scratch_shapes=[pltpu.VMEM((2 * L, GC), BF)],
        cost_estimate=cost(12e9, 60e6, B * G * GH * R * L),
        compiler_params=params(),
    )(hidden, pooled_low, weights_qk, weights_qk, weights_vr, weights_vr, table, small, bias[:, None, :])


def phi_and_slope(z):
    e = jnp.exp(z * z * (-0.5))
    t = 1.0 / (1.0 + (0.3275911 * 0.7071067811865476) * jnp.abs(z))
    poly = t * (0.127414796 + t * (-0.142248368 + t * (0.7107068705 + t * (-0.7265760135 + t * 0.5307027145))))
    tail = poly * e
    phi = jnp.where(z >= 0, 1.0 - tail, tail)
    return phi, phi + z * e * 0.3989422804014327


def norm(x):
    center = x - jnp.mean(x, axis=-1, keepdims=True)
    inv = lax.rsqrt(jnp.mean(center * center, axis=-1, keepdims=True) + EPSILON)
    return center * inv, inv


def norm_back(e, n, inv):
    return inv * (e - jnp.mean(e, axis=-1, keepdims=True) - n * jnp.mean(e * n, axis=-1, keepdims=True))


def add_rows(ref, *values):
    for k, v in enumerate(values):
        ref[k : k + 1, :] += jnp.sum(v, axis=0, keepdims=True)


def mlp_kernel(ctx_ref, pooled_ref, cot_ref, mask_ref, exp_ref, more_ref, w2_ref, small_ref, b1_ref,
               out_ref, y1_ref, n1_ref, s1_ref, inner_ref, slope_ref, dx2_ref, e2_ref, sums_ref):
    @pl.when(pl.program_id(0) == 0)
    def _():
        sums_ref[...] = jnp.zeros_like(sums_ref)

    row = lambda k: small_ref[k : k + 1, :]
    here = exp_ref.shape[0] - 1
    chunks = here + more_ref.shape[0]
    x1 = pooled_ref[0] + dot(ctx_ref[0], exp_ref[here]) + row(3)
    n1, inv1 = norm(x1)
    n1_ref[0] = n1
    s1_ref[0] = inv1
    y1 = n1 * row(4) + row(5)
    y1l = y1.astype(BF)
    y1_ref[0] = y1l
    x2 = y1 + row(6)
    for c in range(chunks):
        cs = slice(c * FC, (c + 1) * FC)
        z = dot(y1l, exp_ref[c] if c < here else more_ref[c - here]) + b1_ref[:, cs]
        phi, slope = phi_and_slope(z)
        inner = (z * phi).astype(BF)
        inner_ref[0, :, cs] = inner
        slope_ref[0, :, cs] = slope
        x2 += dot(inner, w2_ref[cs, :])
    n2, inv2 = norm(x2)
    m = mask_ref[0]
    out_ref[0] = ((n2 * row(7) + row(8)) * m).astype(BF)
    dy2 = cot_ref[0].astype(F32) * m
    dx2 = norm_back(dy2 * row(7), n2, inv2)
    dx2_ref[0] = dx2
    e2_ref[0] = dx2.astype(BF)
    add_rows(sums_ref, dx2, dy2 * n2, dy2)


def mlp(ctx, pooled, cot, mask, expand, more, w2, small, b1):
    B, R, D = pooled.shape
    F = w2.shape[0]
    return pl.pallas_call(
        mlp_kernel,
        grid=(B,),
        in_specs=[seqs(R, D), seqs(R, D), seqs(R, D), seqs(R, 1), whole(*expand.shape), whole(*more.shape), whole(F, D),
                  whole(*small.shape), whole(1, F)],
        out_specs=[seqs(R, D), seqs(R, D), seqs(R, D), seqs(R, 1), seqs(R, F), seqs(R, F), seqs(R, D), seqs(R, D),
                   pl.BlockSpec((8, D), lambda s: (0, 0))],
        out_shape=[sds((B, R, D), BF), sds((B, R, D), BF), sds((B, R, D), F32), sds((B, R, 1), F32), sds((B, R, F), BF),
                   sds((B, R, F), F32), sds((B, R, D), F32), sds((B, R, D), BF), sds((8, D), F32)],
        cost_estimate=cost(10e9, 40e6, 2 * B * R * F),
        compiler_params=params(),
    )(ctx, pooled, cot, mask, expand, more, w2, small, b1)


def mlp_back_kernel(dx2_ref, e2_ref, slope_ref, n1_ref, s1_ref, exp_ref, more_ref, w2_ref, small_ref,
                    e1_ref, dx1_ref, ea_ref, dctx_ref, sums_ref, db1_ref):
    @pl.when(pl.program_id(0) == 0)
    def _():
        sums_ref[...] = jnp.zeros_like(sums_ref)
        db1_ref[...] = jnp.zeros_like(db1_ref)

    here = exp_ref.shape[0] - 1
    chunks = here + more_ref.shape[0]
    e2 = e2_ref[0]
    dy1 = dx2_ref[0]
    for c in range(chunks):
        cs = slice(c * FC, (c + 1) * FC)
        dz = dot_nt(e2, w2_ref[cs, :]) * slope_ref[0, :, cs]
        db1_ref[:, cs] += jnp.sum(dz, axis=0, keepdims=True)
        e1 = dz.astype(BF)
        e1_ref[0, :, cs] = e1
        dy1 += dot_nt(e1, exp_ref[c] if c < here else more_ref[c - here])
    n1 = n1_ref[0]
    dx1 = norm_back(dy1 * small_ref[4:5, :], n1, s1_ref[0])
    dx1_ref[0] = dx1
    ea = dx1.astype(BF)
    ea_ref[0] = ea
    dctx_ref[0] = dot_nt(ea, exp_ref[here]).astype(BF)
    add_rows(sums_ref, dx1, dy1 * n1, dy1)


def mlp_back(dx2, e2, slope, n1, s1, expand, more, w2, small):
    B, R, D = dx2.shape
    F = w2.shape[0]
    return pl.pallas_call(
        mlp_back_kernel,
        grid=(B,),
        in_specs=[seqs(R, D), seqs(R, D), seqs(R, F), seqs(R, D), seqs(R, 1), whole(*expand.shape), whole(*more.shape), whole(F, D),
                  whole(*small.shape)],
        out_specs=[seqs(R, F), seqs(R, D), seqs(R, D), seqs(R, D), pl.BlockSpec((8, D), lambda s: (0, 0)),
                   pl.BlockSpec((1, F), lambda s: (0, 0))],
        out_shape=[sds((B, R, F), BF), sds((B, R, D), F32), sds((B, R, D), BF), sds((B, R, D), BF), sds((8, D), F32),
                   sds((1, F), F32)],
        cost_estimate=cost(7e9, 50e6),
        compiler_params=params(),
    )(dx2, e2, slope, n1, s1, expand, more, w2, small)


def deal(half, me, total_ref, put):
    r = total_ref.shape[0] // 32
    for rel in range(32):
        k = jnp.bitwise_xor(me, flat_of(rel, half))
        put(rel // 16, rel % 16, total_ref[pl.ds(pl.multiple_of(k * r, 8), r), :].astype(BF))


def outer_kernel(half, me_ref, a_ref, b_ref, keep_ref, send_ref, turned, total):
    B, R, M = a_ref.shape

    @pl.when(pl.program_id(0) == 0)
    def _():
        turned[...] = a_ref[...].reshape(B * R, M).T

    total[...] = dot(turned[...], b_ref[...].reshape(B * R, b_ref.shape[2]))

    def put(sent, i, v):
        (send_ref if sent else keep_ref)[i, 0] = v

    deal(half, me_ref[0], total, put)


def outer_plain_kernel(a_ref, b_ref, out_ref):
    B, R, M = a_ref.shape
    out_ref[...] = dot_tn(a_ref[...].reshape(B * R, M), b_ref[...].reshape(B * R, b_ref.shape[2]))


def outer(me, a, b, cols, half=None, blocks=None):
    B, R, M = a.shape
    N = b.shape[2]
    first, count = blocks or (0, N // cols)
    specs = [pl.BlockSpec((B, R, M), lambda j: (0, 0, 0)), pl.BlockSpec((B, R, cols), lambda j: (0, 0, first + j))]
    price = cost(1.5 * B * R * M * cols * count, 2 * (B * R * (M + cols * count) + M * cols * count))
    if half is None:
        return pl.pallas_call(
            outer_plain_kernel, grid=(count,), in_specs=specs,
            out_specs=pl.BlockSpec((M, cols), lambda j: (0, j)),
            out_shape=sds((M, N), F32), cost_estimate=price, compiler_params=params())(a, b)
    return pl.pallas_call(
        functools.partial(outer_kernel, half),
        grid=(count,),
        in_specs=[pl.BlockSpec(memory_space=pltpu.SMEM)] + specs,
        out_specs=[pl.BlockSpec((16, 1, M // 32, cols), lambda j: (0, j, 0, 0))] * 2,
        out_shape=[sds((16, count, M // 32, cols), BF)] * 2,
        scratch_shapes=[pltpu.VMEM((M, B * R), BF), pltpu.VMEM((M, cols), F32)],
        cost_estimate=price,
        compiler_params=params(),
    )(me, a, b)


def tall_outer_kernel(steps, me_ref, a_ref, b_ref, keep0_ref, send0_ref, keep1_ref, send1_ref, total):
    B, R, M = a_ref.shape
    i = pl.program_id(0)
    v = dot_tn(a_ref[...].reshape(B * R, M), b_ref[...].reshape(B * R, b_ref.shape[2]))
    total[pl.ds(pl.multiple_of(i * M, 8), M), :] = v

    @pl.when(i == steps - 1)
    def _():
        r = keep0_ref.shape[2]
        for half, refs in enumerate(((keep0_ref, send0_ref), (keep1_ref, send1_ref))):
            for rel in range(32):
                k = jnp.bitwise_xor(me_ref[0], flat_of(rel, half))
                at = pl.multiple_of(k * (2 * r) + half * r, 8)
                refs[rel // 16][rel % 16, 0] = total[pl.ds(at, r), :].astype(BF)


def tall_outer(me, a, b, rows):
    B, R, M = a.shape
    N = b.shape[2]
    r = M // 64
    out = pl.pallas_call(
        functools.partial(tall_outer_kernel, M // rows),
        grid=(M // rows,),
        in_specs=[pl.BlockSpec(memory_space=pltpu.SMEM), pl.BlockSpec((B, R, rows), lambda i: (0, 0, i)), whole(B, R, N)],
        out_specs=[whole(16, 1, r, N)] * 4,
        out_shape=[sds((16, 1, r, N), BF)] * 4,
        scratch_shapes=[pltpu.VMEM((M, N), F32)],
        cost_estimate=cost(1.5 * B * R * M * N, 2 * (B * R * (M + N) + M * N)),
        compiler_params=params(),
    )(me, a, b)
    return (out[0], out[1]), (out[2], out[3])


def small_deal_kernel(me_ref, *refs):
    sums, (sums1, sums2, db1, keep_ref, send_ref, total, turned) = refs[:-7], refs[-7:]
    D = sums1.shape[1]
    total[...] = jnp.zeros_like(total)
    for g, s in enumerate(sums):
        total[0:3, g * GC : (g + 1) * GC] = s[0:3, :]
    total[3:6, :] = sums1[0:3, :]
    total[6:9, :] = sums2[0:3, :]
    for i in range(db1.shape[1] // D):
        total[9 + i : 10 + i, :] = db1[0:1, i * D : (i + 1) * D]
    turned[...] = jnp.concatenate([total[...].T, jnp.zeros((D, GC - total.shape[0]), F32)], axis=1)

    def put(sent, i, v):
        (send_ref if sent else keep_ref)[i, 0] = v

    deal(0, me_ref[0], turned, put)


def small_deal(me, sums, sums1, sums2, db1):
    D = sums1.shape[1]
    n = 4 + len(sums)
    return pl.pallas_call(
        small_deal_kernel,
        in_specs=[pl.BlockSpec(memory_space=pltpu.SMEM)] + [pl.BlockSpec(memory_space=pltpu.VMEM)] * (n - 1),
        out_specs=[pl.BlockSpec(memory_space=pltpu.VMEM)] * 2,
        out_shape=[sds((16, 1, D // 32, GC), BF)] * 2,
        scratch_shapes=[pltpu.VMEM((128, D), F32), pltpu.VMEM((D, GC), F32)],
        cost_estimate=cost(0, 4e6),
        compiler_params=params(),
    )(me, *sums, sums1, sums2, db1)


def attend_back_kernel(plan, *refs):
    (me_ref, probs_ref, dctx_ref, qu_ref, qw_ref, keys_ref, values_ref, rel_ref, hidt_ref, lowt_ref, tablet_ref) = refs[:11]
    outs = refs[11 : 14]
    dq_ref, dk_ref, dv_ref = outs
    grads = refs[14 : -8]
    sums_ref = refs[-8]
    acc_q, acc_k, acc_v, acc_r, acc_dv, dkt, dvt = refs[-7:]
    step = pl.program_id(0)
    half, L = probs_ref.shape[3], probs_ref.shape[4]
    blk = half // 2

    @pl.when(step == 0)
    def _():
        for a in (acc_q, acc_k, acc_v, acc_r, acc_dv, sums_ref):
            a[...] = jnp.zeros_like(a)

    across = lax.broadcasted_iota(jnp.int32, (half, half), 0) + lax.broadcasted_iota(jnp.int32, (half, half), 1)
    flip = (across == half - 1).astype(F32).astype(BF)
    lane = lax.broadcasted_iota(jnp.int32, (1, GC), 1)
    dctx = dctx_ref[0]
    dctx_t = dctx.T
    qu_t = qu_ref[0].T
    qwr_t = dot(flip, qw_ref[0]).astype(BF).T
    keys = keys_ref[0]
    values = values_ref[0]
    dqu = dqw = None
    for h in range(GH):
        mine = (lane >= h * HEAD) & (lane < (h + 1) * HEAD)
        sel = slice(h * HEAD, (h + 1) * HEAD)
        p = probs_ref[0, 0, h]
        dp = dot_nt(jnp.where(mine, dctx.astype(F32), 0.0).astype(BF), values)
        t = p * dp
        draw = (t - p * jnp.sum(t, axis=-1, keepdims=True)).astype(BF)
        dvt[sel, :] = dot(dctx_t[sel], p.astype(BF))
        both = dot(jnp.concatenate([qu_t[sel], flip], axis=0), draw)
        dkt[sel, :] = both[:HEAD] * 0.125
        back = both[HEAD:]
        a = dot(back.astype(BF), keys)
        tables = []
        for b in range(2):
            x = jnp.concatenate([back[b * blk : (b + 1) * blk], jnp.zeros((blk, half), F32)], axis=1)
            x = pltpu.roll(x, 2, 1, stride=2, stride_axis=0).astype(BF)
            m0 = half * b
            tables.append(dot(x, rel_ref[m0 : m0 + 3 * half, :]))
            acc_r[sel, m0 : m0 + 3 * half] += dot(qwr_t[sel, b * blk : (b + 1) * blk], x)
        c = jnp.concatenate(tables, axis=0)
        dqu, dqw = (a, c) if dqu is None else (jnp.where(mine, a, dqu), jnp.where(mine, c, dqw))
    dqu = dqu * 0.125
    dqw = dqw * 0.125
    dq = dot(flip, (dqu + dqw).astype(BF)).astype(BF)
    dk = dkt[...].astype(BF).T
    dvf = dvt[...]
    dv = dvf.astype(BF).T
    dq_ref[0] = dq
    dk_ref[0] = dk
    dv_ref[0] = dv
    acc_dv[...] += dvf
    add_rows(sums_ref, dqu, dqw)
    acc_q[...] += dot(lowt_ref[0], dq)
    acc_k[...] += dot(hidt_ref[0], dk)
    acc_v[...] += dot(hidt_ref[0], dv)

    @pl.when(step == pl.num_programs(0) - 1)
    def _():
        sums_ref[2:3, :] = jnp.sum(acc_dv[...].T, axis=0, keepdims=True)
        dr = acc_r[...] * 0.125
        hi = dr.astype(BF)
        lo = (dr - hi.astype(F32)).astype(BF)
        tt = tablet_ref[...]
        if plan is None:
            for i, a in enumerate((acc_q, acc_k, acc_v)):
                grads[0][i] = a[...]
            grads[0][3] = dot_nt(tt, hi) + dot_nt(tt, lo)
        else:
            for i in range(4):
                half = plan[i]
                at = plan[:i].count(half)
                base = 2 * sorted(set(plan)).index(half)
                acc = (acc_q, acc_k, acc_v, acc_q)[i]
                if i == 3:
                    acc_q[...] = dot_nt(tt, hi) + dot_nt(tt, lo)

                def put(sent, j, v):
                    grads[base + sent][j, at] = v

                deal(half, me_ref[0], acc, put)


def attend_back(me, g, probs, dctx, qu, qw, keys, values, rel, hid_t, low_t, table_t, plan=None):
    B, R, D = qu.shape
    L = 2 * R
    so = lambda r: pl.BlockSpec((1, r, GC), lambda s: (s, 0, g))
    if plan is None:
        grad_specs = [pl.BlockSpec((4, D, GC), lambda s: (0, 0, 0))]
        grad_shapes = [sds((4, D, GC), F32)]
    else:
        sizes = [(16, plan.count(h), D // 32, GC) for h in sorted(set(plan)) for _ in range(2)]
        grad_specs = [whole(*size) for size in sizes]
        grad_shapes = [sds(size, BF) for size in sizes]
    return pl.pallas_call(
        functools.partial(attend_back_kernel, plan),
        grid=(B,),
        in_specs=[pl.BlockSpec(memory_space=pltpu.SMEM),
                  pl.BlockSpec((1, 1, GH, R, L), lambda s: (s, g, 0, 0, 0)), so(R), so(R), so(R), so(L), so(L),
                  pl.BlockSpec((2 * L, GC), lambda s: (0, g)), seqs(D, L), seqs(D, R), whole(D, 2 * L)],
        out_specs=[seqs(R, GC), seqs(L, GC), seqs(L, GC)] + grad_specs + [pl.BlockSpec((8, GC), lambda s: (0, 0))],
        out_shape=[sds((B, R, GC), BF), sds((B, L, GC), BF), sds((B, L, GC), BF)] + grad_shapes + [sds((8, GC), F32)],
        scratch_shapes=[pltpu.VMEM((D, GC), F32)] * 3 + [pltpu.VMEM((GC, 2 * L), F32)] + [pltpu.VMEM((GC, L), F32)] * 3,
        cost_estimate=cost(10e9, 30e6),
        compiler_params=params(),
    )(me, probs, dctx, qu, qw, keys, values, rel, hid_t, low_t, table_t)


def input_grad_kernel(groups, *refs):
    dqs, dks, dvs = refs[:groups], refs[groups : 2 * groups], refs[2 * groups : 3 * groups]
    dx1_ref, wa_ref, wb_ref, out_ref, wide = refs[3 * groups :]
    half = dx1_ref.shape[1]
    shared = dx1_ref[0]
    total = None
    for g in range(groups):
        shared += dot_nt(dqs[g][0], wa_ref[g])
        t = dot_nt(dks[g][0], wa_ref[groups + g]) + dot_nt(dvs[g][0], wb_ref[g])
        total = t if total is None else total + t
    shared = shared * 0.5
    for i in range(wide.shape[0]):
        cs = slice(i * 128, (i + 1) * 128)
        wide[i, pl.ds(0, half, stride=2), :] = shared[:, cs]
        wide[i, pl.ds(1, half, stride=2), :] = shared[:, cs]
        out_ref[0, :, cs] = (total[:, cs] + wide[i]).astype(BF)


def input_grad(dqs, dks, dvs, dx1, weights_qk, weights_vr):
    B, R, D = dx1.shape
    L = 2 * R
    G = len(dqs)
    return pl.pallas_call(
        functools.partial(input_grad_kernel, G),
        grid=(B,),
        in_specs=[seqs(R, GC)] * G + [seqs(L, GC)] * (2 * G) + [seqs(R, D), whole(2 * G, D, GC), whole(G, D, GC)],
        out_specs=seqs(L, D),
        out_shape=sds((B, L, D), BF),
        scratch_shapes=[pltpu.VMEM((D // 128, L, 128), F32)],
        cost_estimate=cost(5e9, 20e6),
        compiler_params=params(),
    )(*dqs, *dks, *dvs, dx1, weights_qk, weights_vr)


def adamw(weight, moment, second, gradient, rates):
    new_moment = rates[1] * moment + (1.0 - rates[1]) * gradient
    new_second = rates[2] * second + (1.0 - rates[2]) * gradient * gradient
    moment_hat = new_moment / rates[4]
    second_hat = new_second / rates[5]
    new_weight = weight - rates[0] * (moment_hat / (jnp.sqrt(second_hat) + 1e-08) + rates[3] * weight)
    return (new_weight, new_moment, new_second)


def update_kernel(plan, rates_ref, w_ref, m_ref, v_ref, *refs):
    terms, (grad_ref, w_out, m_out, v_out) = refs[:-4], refs[-4:]
    rates = [rates_ref[i] for i in range(6)]
    for first, count, block, dest in plan:
        g = None
        for t in terms[first : first + count]:
            v = (t[...] if block is None else t[block]).astype(F32)
            g = v if g is None else g + v
        grad_ref[dest] = g
        w_out[dest], m_out[dest], v_out[dest] = adamw(w_ref[dest], m_ref[dest], v_ref[dest], g, rates)


def update(rates, w, m, v, terms, plan=None):
    plan = plan or [(0, len(terms), None, (slice(None),) * w.ndim)]
    return pl.pallas_call(
        functools.partial(update_kernel, plan),
        in_specs=[pl.BlockSpec(memory_space=pltpu.SMEM)] + [pl.BlockSpec(memory_space=pltpu.VMEM)] * (3 + len(terms)),
        out_specs=[pl.BlockSpec(memory_space=pltpu.VMEM)] * 4,
        out_shape=[sds(w.shape, F32)] * 4,
        cost_estimate=cost(0, 36 * w.size),
        compiler_params=params(),
    )(rates, w, m, v, *terms)


def shards(fast, hidden, lengths, key_mask, cotangent, attention_weight, expand_weight, contract_weight, small_params,
           mean_attention, mean_expand, mean_contract, mean_small,
           square_attention, square_expand, square_contract, square_small, update_step, update_rates):
    B, L, D = hidden.shape
    R = L // 2
    F = expand_weight.shape[1]
    G = D // GC
    C = F // FC
    H = C // 2
    r = attention_weight.shape[1]
    V = small_params.shape[0]
    me = (lax.axis_index("dp") * lax.axis_size("fsdp") + lax.axis_index("fsdp")).astype(jnp.int32).reshape(1)

    cut = lambda a, c: a.astype(BF).reshape(r, -1, c).transpose(1, 0, 2)
    small_t = jnp.pad(small_params.T, ((0, 0), (0, GC - V))).astype(BF)[None]
    a_low = attention_weight
    first = jnp.concatenate([cut(a_low[0], GC), cut(a_low[1], GC), small_t, cut(a_low[2], GC), cut(a_low[3], GC)], axis=0)
    e_cut = cut(expand_weight, FC)
    second = jnp.concatenate([e_cut[:H], cut(a_low[4], FC), e_cut[H:]], axis=0)
    if fast:
        token, (w_qk, w_vr) = gather(me, first, 2 * G + 1)
        token, (w_eo, w_e) = gather(me, after(second, token), H + 1)
        third = contract_weight.astype(BF).reshape(2, -1, D)
        token, w2 = gather(me, after(third, token), 1, stacked=False)
    else:
        full = lambda a: lax.all_gather(a, ALL, axis=1, tiled=True)
        first, second = full(first), full(second)
        w_qk, w_vr = first[: 2 * G + 1], first[2 * G + 1 :]
        w_eo, w_e = second[: H + 1], second[H + 1 :]
        w2 = lax.all_gather(contract_weight.astype(BF), ALL, axis=0, tiled=True)
    small = w_qk[2 * G, :, :16].astype(F32).T
    b1 = small[9:V].reshape(1, F)

    positions = jnp.arange(L, dtype=jnp.int32)
    valid = (key_mask == 1) & (positions[None, :] < lengths[:, None])
    bias = jnp.where(valid, 0.0, MASK_FILL).astype(F32)
    mask = jnp.max(valid.astype(F32).reshape(B, R, 2), axis=2)[:, :, None]
    table = rel_table(L, D).astype(BF)
    table_t = table.T
    step = update_step[0].astype(F32)
    rates = jnp.concatenate([update_rates, 1.0 - jnp.power(update_rates[1:3], step)])

    pooled, pooled_low, hid_t, low_t = prepare(hidden)
    ctx, probs, qu, qw, keys, values, rel = attend(hidden, pooled_low, w_qk, w_vr, table, small, bias)
    out, y1, n1, s1, inner, slope, dx2, e2, sums2 = mlp(ctx, pooled, cotangent, mask, w_eo, w_e, w2, small, b1)

    def backward(g, dctx, plan=None):
        return attend_back(me, g, probs, dctx, qu, qw, keys, values, rel, hid_t, low_t, table_t, plan)

    if not fast:
        scatter = lambda a, d: lax.psum_scatter(a, ALL, scatter_dimension=d, tiled=True)
        e1, dx1, ea, dctx, sums1, db1 = mlp_back(dx2, e2, slope, n1, s1, w_eo, w_e, w2, small)
        back = [backward(g, dctx) for g in range(G)]
        in_grad = input_grad([b[0] for b in back], [b[1] for b in back], [b[2] for b in back], dx1, w_qk, w_vr)
        d_att = jnp.concatenate([b[3] for b in back], axis=2)
        d_att = jnp.concatenate([d_att, outer(me, ctx, ea, 384)[None]], axis=0)
        d_small = jnp.concatenate([b[-1][0:3] for b in back], axis=1)
        d_small = jnp.concatenate([d_small, sums1[0:3], sums2[0:3], db1.reshape(-1, D)], axis=0)
        attention_terms, attention_plan = [scatter(d_att, 1)], None
        expand_terms, expand_plan = [scatter(outer(me, y1, e1, FC), 0)], None
        contract_terms, contract_plan = [scatter(outer(me, inner, e2, 384), 0)], None
        small_grad = scatter(d_small, 1)
    else:
        half0, half1 = tall_outer(me, inner, e2, 768)
        red1 = Reduction([half0], [half1])
        e1, dx1, ea, dctx, sums1, db1 = mlp_back(dx2, after(e2, half0, half1), slope, n1, s1, w_eo, w_e, w2, small)
        red1.step(e1)
        y1, ctx = after((y1, ctx), red1.token)
        d_e0 = outer(me, y1, e1, FC, 0, (0, H))
        d_e1 = outer(me, y1, e1, FC, 1, (H, C - H))
        d_o = outer(me, ctx, ea, FC, 0)
        red2 = Reduction([d_e0, d_o], [d_e1])
        back = [backward(0, after(dctx, d_e0, d_e1, d_o), (0, 0, 0, 0))]
        red1.step(back[0][0])
        red2.step(back[0][0])
        back.append(backward(1, after(dctx, red1.token, red2.token), (1, 1, 1, 1)))
        red3 = Reduction([tuple(back[0][3:5])], [tuple(back[1][3:5])])
        red1.step(back[1][0])
        red2.step(back[1][0])
        back.append(backward(2, after(dctx, red1.token, red2.token), (0, 0, 1, 1)))
        last = back[2]
        d_small = small_deal(me, [b[-1] for b in back], sums1, sums2, db1)
        red4 = Reduction([tuple(last[3:5]), tuple(d_small)], [tuple(last[5:7])])
        red2.step(last[0])
        red3.step(last[0])
        red4.step()
        dx1 = after(dx1, red2.token, red3.token, red4.token)
        in_grad = input_grad([b[0] for b in back], [b[1] for b in back], [b[2] for b in back], dx1, w_qk, w_vr)
        red3.step(in_grad)
        red4.step(in_grad)
        red3.step()
        red4.step()
        whole_rows = slice(None)
        r2 = contract_weight.shape[0] // 2
        contract_terms = red1.terms
        contract_plan = [(0, 4, i, (slice(i * r2, (i + 1) * r2), whole_rows)) for i in range(2)]
        expand_terms = red2.terms
        expand_plan = [(0, 4, i + (i >= H), (whole_rows, slice(i * FC, (i + 1) * FC))) for i in range(C)]
        attention_terms = red3.terms + red4.terms + red2.terms
        place = lambda m, g: (m, whole_rows, slice(g * GC, (g + 1) * GC))
        attention_plan = [(0, 4, 4 * g + m, place(m, g)) for g in range(2) for m in range(4)]
        attention_plan += [(4, 4, m + (m > 1), place(m, 2)) for m in range(4)]
        attention_plan += [(8, 4, H, (4, whole_rows, whole_rows))]
        small_grad = sum(t[2, :, :V].astype(F32) for t in red4.terms).T
    contract_up = update(rates, contract_weight, mean_contract, square_contract, contract_terms, contract_plan)
    expand_up = update(rates, expand_weight, mean_expand, square_expand, expand_terms, expand_plan)
    attention_up = update(rates, attention_weight, mean_attention, square_attention, attention_terms, attention_plan)
    small_up = update(rates, small_params, mean_small, square_small, [small_grad])
    ups = (attention_up, expand_up, contract_up, small_up)
    return (out, in_grad) + tuple(u[i] for i in range(4) for u in ups)


def solution(mesh):
    outer_rows = P(ALL, None)
    middle = P(None, ALL, None)
    inner_cols = P(None, ALL)
    table = (middle, outer_rows, outer_rows, inner_cols)
    tokens = P(ALL, None, None)
    in_specs = (tokens, P(ALL), outer_rows, tokens) + table * 3 + (P(), P())
    out_specs = (tokens, tokens) + table * 4
    fast = mesh.shape["dp"] == 8 and mesh.shape["fsdp"] == 4
    return jax.shard_map(
        functools.partial(shards, fast), mesh=mesh, in_specs=in_specs, out_specs=out_specs, check_vma=False
    )
```

```python
import functools
import math

import jax
import jax.numpy as jnp
import ml_dtypes
import numpy as np
from jax import lax
from jax.experimental import pallas as pl
from jax.experimental.pallas import tpu as pltpu
from jax.sharding import PartitionSpec as P

HEAD = 64
GC = 256
GH = GC // HEAD
FC = 768
EPSILON = 1e-06
MASK_FILL = -1000000000.0
ALL = ("dp", "fsdp")
F32 = jnp.float32
BF = jnp.bfloat16
NT = (((1,), (1,)), ((), ()))
TN = (((0,), (0,)), ((), ()))


def dot(a, b):
    return jnp.dot(a, b, preferred_element_type=F32)


def dot_nt(a, b):
    return lax.dot_general(a, b, NT, preferred_element_type=F32)


def dot_tn(a, b):
    return lax.dot_general(a, b, TN, preferred_element_type=F32)


def sds(shape, dtype):
    return jax.ShapeDtypeStruct(shape, dtype)


def seqs(*tail):
    return pl.BlockSpec((1,) + tail, lambda s, *_: (s,) + (0,) * len(tail))


def whole(*shape):
    return pl.BlockSpec(shape, lambda *_: (0,) * len(shape), pipeline_mode=pl.Buffered(1))


def turned_small(width):
    return pl.BlockSpec((1, width, GC), lambda s: (2 * width // GC, 0, 0), pipeline_mode=pl.Buffered(1))


def params(mib):
    return pltpu.CompilerParams(vmem_limit_bytes=mib << 20)


def cost(us):
    return pl.CostEstimate(flops=int(us * 1.1e9), bytes_accessed=int(us * 3.5e6), transcendentals=0)


def rel_table(length, width):
    places = length - np.arange(2 * length, dtype=np.float32)
    half_width = width // 2
    frequency = np.exp(np.arange(half_width, dtype=np.float32) * np.float32(-2.0 * math.log(10000.0) / width))
    angles = places[:, None] * frequency[None, :]
    return np.concatenate([np.sin(angles), np.cos(angles)], axis=1).astype(ml_dtypes.bfloat16)


X, Y, CORE, Z = 1, 2, 4, 8
HALVES = ((X, Y), (Y, X))


def pairs(bit):
    return [(d, d ^ bit) for d in range(32)]


def swap(a, bit):
    return lax.ppermute(a, ALL, pairs(bit))


def flat_of(rel, half):
    low, high = HALVES[half]
    return (rel & 3) * Z + (rel >> 2 & 1) * low + (rel >> 3 & 1) * high + (rel >> 4 & 1) * CORE


def after(x, *earlier):
    return lax.optimization_barrier((x, earlier))[0]


def assemble_kernel(stacked, me_ref, *refs):
    ins, outs = refs[:8], refs[8:]
    for half in range(2):
        for rel in range(32):
            k = jnp.bitwise_xor(me_ref[0], flat_of(rel, half))
            src = ins[4 * half + rel // 8]
            for i in range(src.shape[1]):
                if stacked[half]:
                    outs[half][i, k] = src[rel % 8, i]
                else:
                    outs[half][k, i] = src[rel % 8, i]


def small_call(body, shapes, dtype, *ins, mib=32):
    return pl.pallas_call(
        body,
        in_specs=[pl.BlockSpec(memory_space=pltpu.VMEM)] * len(ins),
        out_specs=[pl.BlockSpec(memory_space=pltpu.VMEM)] * len(shapes),
        out_shape=[sds(shape, dtype) for shape in shapes],
        cost_estimate=cost(2),
        compiler_params=params(mib),
    )(*ins)


def halve(parts, split):
    n, r, c = parts[0].shape

    def body(*refs):
        first, second = refs[-2:]
        for k, ref in enumerate(refs[:-2]):
            first[k] = ref[:split]
            second[k] = ref[split:]

    return small_call(body, [(len(parts), split, r, c), (len(parts), n - split, r, c)], parts[0].dtype, *parts)


def double(halves, got):
    def body(a, b, a_got, b_got, a_out, b_out):
        for mine, other, out in ((a, a_got, a_out), (b, b_got, b_out)):
            m = mine.shape[0]
            out[:m] = mine[...]
            out[m:] = other[...]

    shapes = [(2 * h.shape[0],) + h.shape[1:] for h in halves]
    return small_call(body, shapes, halves[0].dtype, *halves, *got)


def parcel(attention, expand, contract, small):
    r, F = expand.shape
    V = small.shape[0]
    C = F // FC
    G = attention.shape[2] // GC

    def body(att_ref, exp_ref, con_ref, small_ref, first, third, pad):
        pad[...] = jnp.zeros_like(pad)
        pad[0:V, 0:r] = small_ref[...]
        turned = pad[...].T
        narrow = lambda m, g: att_ref[m, :, g * GC : (g + 1) * GC].astype(BF)
        for g in range(G):
            for i, m in ((0, 0), (G, 1), (2 * G + 1, 2), (3 * G + 1, 3)):
                first[i + g] = narrow(m, g)
        first[2 * G] = jnp.concatenate([turned[0:r, :], jnp.zeros((r, GC - 128), F32)], axis=1).astype(BF)
        for i in range(C):
            third[i] = exp_ref[:, i * FC : (i + 1) * FC].astype(BF)
        third[C] = att_ref[4].astype(BF)
        for i in range(C):
            third[C + 1 + i] = con_ref[i * r : (i + 1) * r, :].astype(BF)

    shapes = [(4 * G + 1, r, GC), (2 * C + 1, r, FC)]
    return pl.pallas_call(
        body,
        in_specs=[pl.BlockSpec(memory_space=pltpu.VMEM)] * 4,
        out_specs=[pl.BlockSpec(memory_space=pltpu.VMEM)] * 2,
        out_shape=[sds(shape, BF) for shape in shapes],
        scratch_shapes=[pltpu.VMEM((128, 128), F32)],
        cost_estimate=cost(2),
        compiler_params=params(58),
    )(attention, expand, contract, small)


class Gather:
    def __init__(self, me, part, split, stacked=(True, True)):
        self.me, self.part, self.split, self.stacked = me, part, split, stacked
        self.along = [part]

    def far(self, *ks, then=()):
        part = after(self.part, then) if then else self.part
        self.along += [swap(part, k * Z) for k in ks]
        return self.along[-1]

    def plane(self, *earlier):
        along = after(self.along, *earlier) if earlier else self.along
        self.halves = halve(along, self.split)
        self.got = [swap(h, HALVES[i][0]) for i, h in enumerate(self.halves)]
        return self.halves

    def plane_again(self, *earlier):
        halves, got = after((self.halves, self.got), *earlier) if earlier else (self.halves, self.got)
        self.firsts = double(halves, got)
        self.seconds = [swap(h, HALVES[i][1]) for i, h in enumerate(self.firsts)]
        return self.firsts

    def cores(self, *earlier):
        firsts, seconds = after((self.firsts, self.seconds), *earlier) if earlier else (self.firsts, self.seconds)
        self.pieces = []
        for f, s in zip(firsts, seconds):
            self.pieces += [f, s, swap(f, CORE), swap(s, CORE)]
        return firsts, seconds

    def result(self, *earlier):
        pieces = after(self.pieces, *earlier) if earlier else self.pieces
        n, r, c = self.part.shape
        wide = min(c, 384)
        counts = [self.split, n - self.split]
        specs = [pl.BlockSpec((8, m, r, wide), lambda j: (0, 0, 0, j)) for m in counts for _ in range(4)]
        shapes, outs = [], []
        for m, stacked in zip(counts, self.stacked):
            lead = (m, 32) if stacked else (32, m)
            shapes.append(sds(lead + (r, c), self.part.dtype))
            outs.append(pl.BlockSpec(lead + (r, wide), lambda j: (0, 0, 0, j)))
        out = pl.pallas_call(
            functools.partial(assemble_kernel, self.stacked),
            grid=(c // wide,),
            in_specs=[pl.BlockSpec(memory_space=pltpu.SMEM)] + specs,
            out_specs=outs,
            out_shape=shapes,
            cost_estimate=cost(4),
            compiler_params=params(58 if c > GC else 40),
        )(self.me, *pieces)
        return [o.reshape(m, 32 * r, c) if stacked else o.reshape(32 * m * r, c) for o, m, stacked in zip(out, counts, self.stacked)]


def join_kernel(plan, *refs):
    n = 1 + max(w for blocks in plan for _, terms in blocks for w, _ in terms)
    ins, outs = refs[:n], refs[n:]
    for out, blocks in zip(outs, plan):
        for place, terms in blocks:
            total = None
            for w, at in terms:
                v = ins[w][at].astype(F32)
                total = v if total is None else total + v
            out[place] = total.astype(BF)


def join(plan, shapes, ins):
    return pl.pallas_call(
        functools.partial(join_kernel, plan),
        in_specs=[pl.BlockSpec(memory_space=pltpu.VMEM)] * len(ins),
        out_specs=[pl.BlockSpec(memory_space=pltpu.VMEM)] * len(shapes),
        out_shape=[sds(shape, BF) for shape in shapes],
        cost_estimate=cost(1),
        compiler_params=params(32),
    )(*ins)


def settle(terms):
    def body(*refs):
        total = refs[0][...].astype(F32)
        for ref in refs[1:-1]:
            total += ref[...].astype(F32)
        refs[-1][...] = total

    return small_call(body, [terms[0].shape], F32, *terms)[0]


class Reduction:
    def __init__(self, *halves):
        self.halves = []
        for h, parts in enumerate(halves):
            self.halves.append([(k, swap(s, CORE)) for k, s in parts])
        self.token = None

    def add(self, *halves):
        for mine, parts in zip(self.halves, halves):
            mine += [(k, swap(s, CORE)) for k, s in parts]

    def flat(self, earlier):
        halves = after(self.halves, *earlier) if earlier else self.halves
        ins, at = [], []
        for parts in halves:
            blocks = []
            for terms in parts:
                blocks += [[(len(ins) + t, b) for t in range(len(terms))] for b in range(terms[0].shape[1])]
                ins += terms
            at.append(blocks)
        return ins, at, ins[0].shape[2:]

    def cross(self, *earlier):
        ins, at, tail = self.flat(earlier)
        n = ins[0].shape[0] // 2
        bit = 1 if n == 8 else 0
        plan, shapes = [], []
        for blocks in at:
            for far in range(2):
                plan.append([((j, b), [(w, (far * n + j, i)) for w, i in terms]) for j in range(n) for b, terms in enumerate(blocks)])
                shapes.append((n, len(blocks)) + tail)
        out = join(plan, shapes, ins)
        self.halves = [[(out[2 * h], swap(out[2 * h + 1], HALVES[h][bit]))] for h in range(2)]
        self.token = out

    def direct(self, *earlier):
        ins, at, tail = self.flat(earlier)
        count = sum(len(blocks) for blocks in at)
        plan = []
        for q in range(4):
            places = []
            b = 0
            for h, blocks in enumerate(at):
                lead = 4 * (q if h == 0 else (q >> 1) + 2 * (q & 1))
                for terms in blocks:
                    places += [((j, b), [(w, (lead + j, i)) for w, i in terms]) for j in range(4)]
                    b += 1
            plan.append(places)
        out = join(plan, [(4, count) + tail] * 4, ins)
        self.halves = [[tuple([out[0]] + [swap(out[q], (q & 1) * X + (q >> 1) * Y) for q in range(1, 4)])]]
        self.token = out

    def along(self, *earlier, also=()):
        groups = [r.flat(earlier) for r in (self,) + tuple(also)]
        ins, places, tail = [], [[] for _ in range(4)], groups[0][2]
        b = 0
        for more, at, _ in groups:
            base = len(ins)
            ins += more
            for blocks in at:
                for terms in blocks:
                    for k in range(4):
                        places[k].append((b, [(base + w, (k, i)) for w, i in terms]))
                    b += 1
        out = join(places, [(b,) + tail] * 4, ins)
        self.terms = [out[0]] + [swap(out[k], k * Z) for k in range(1, 4)]
        self.token = out


def prepare_kernel(lengths_ref, hidden_ref, key_ref, pooled_ref, low_ref, hidt_ref, lowt_ref, bias_ref, mask_ref, wide):
    hid = hidden_ref[0]
    half, L = pooled_ref.shape[1], hid.shape[0]
    hidt_ref[0] = hid.T
    columns = []
    for i in range(wide.shape[0]):
        wide[i] = hid[:, i * 128 : (i + 1) * 128].astype(F32)
        columns.append((wide[i, pl.ds(0, half, stride=2), :] + wide[i, pl.ds(1, half, stride=2), :]) * 0.5)
    pooled = jnp.concatenate(columns, axis=1)
    pooled_ref[0] = pooled
    low = pooled.astype(BF)
    low_ref[0] = low
    lowt_ref[0] = low.T
    place = lax.broadcasted_iota(jnp.int32, (1, L), 1)
    valid = (key_ref[pl.ds(pl.program_id(0), 1), :] == 1) & (place < lengths_ref[pl.program_id(0)])
    bias_ref[0] = jnp.where(valid, 0.0, MASK_FILL)
    twice = 2 * lax.broadcasted_iota(jnp.int32, (half, L), 0)
    token = lax.broadcasted_iota(jnp.int32, (half, L), 1)
    of = ((token == twice) | (token == twice + 1)).astype(F32).astype(BF)
    rows = jnp.broadcast_to(valid.astype(F32), (16, L)).astype(BF)
    mask_ref[0] = jnp.minimum(dot_nt(of, rows)[:, 0:1], 1.0)


def prepare(hidden, lengths, key_mask):
    B, L, D = hidden.shape
    R = L // 2
    return pl.pallas_call(
        prepare_kernel,
        grid=(B,),
        in_specs=[pl.BlockSpec(memory_space=pltpu.SMEM), seqs(L, D), whole(B, L)],
        out_specs=[seqs(R, D), seqs(R, D), seqs(D, L), seqs(D, R), seqs(1, L), seqs(R, 1)],
        out_shape=[sds((B, R, D), F32), sds((B, R, D), BF), sds((B, D, L), BF), sds((B, D, R), BF), sds((B, 1, L), F32),
                   sds((B, R, 1), F32)],
        scratch_shapes=[pltpu.VMEM((D // 128, L, 128), F32)],
        cost_estimate=cost(6),
        compiler_params=params(58),
    )(lengths, hidden, key_mask)


def attend_kernel(start, per, hidden_ref, pooled_ref, wq_ref, wk_ref, wv_ref, wr_ref, table_ref, small_ref, bias_ref, *refs):
    ctx_ref, probs_ref, qu_ref, qw_ref, keys_ref, values_ref, rel_out, rel_ref = refs[-8:]
    half = hidden_ref.shape[1] // 2
    blk = half // 2
    step = pl.program_id(0)

    @pl.when((step == 0) | (lax.rem(start + step, per) == 0))
    def _():
        rel = dot(table_ref[...], wr_ref[0]).astype(BF)
        rel_ref[...] = rel
        rel_out[...] = rel

    hid = hidden_ref[0]
    small_ref = small_ref[0, :, 0:128].astype(F32).T
    q = dot(pooled_ref[0], wq_ref[0])
    qu = (q + small_ref[0:1, :]).astype(BF)
    qw = (q + small_ref[1:2, :]).astype(BF)
    qu_ref[0] = qu
    qw_ref[0] = qw
    keys_ref[0] = dot(hid, wk_ref[0]).astype(BF)
    values_ref[0] = (dot(hid, wv_ref[0]) + small_ref[2:3, :]).astype(BF)
    bias = bias_ref[0]
    lane = lax.broadcasted_iota(jnp.int32, (1, GC), 1)
    for b in range(2):
        rows = slice(b * blk, (b + 1) * blk)
        m0 = half * (1 - b)
        total = None
        for h in range(GH):
            mine = (lane >= h * HEAD) & (lane < (h + 1) * HEAD)
            quh = jnp.where(mine, qu[rows].astype(F32) * 0.125, 0.0).astype(BF)
            qwh = jnp.where(mine, qw[rows].astype(F32) * 0.125, 0.0).astype(BF)
            content = dot_nt(quh, keys_ref[0])
            placed = dot_nt(qwh, rel_ref[m0 : m0 + 3 * half, :])
            moved = pltpu.roll(placed, 0, 1, stride=2, stride_axis=0)[:, half:]
            s = content + moved + bias
            top = jnp.max(s, axis=-1, keepdims=True)
            e = jnp.exp(s - top)
            p = e * (1.0 / jnp.sum(e, axis=-1, keepdims=True))
            probs_ref[0, 0, h, rows, :] = p
            c = dot(p.astype(BF), values_ref[0])
            total = c if total is None else jnp.where(mine, c, total)
        ctx_ref[0, rows, :] = total.astype(BF)


def attend(start, stop, hidden, pooled_low, weights, table, bias, held=None):
    B, L, D = hidden.shape
    R = L // 2
    G = D // GC
    g = lambda i: (start + i) // B
    s = lambda i: lax.rem(start + i, B)
    seq = lambda r: pl.BlockSpec((1, r, D), lambda i: (s(i), 0, 0))
    mat = lambda base: pl.BlockSpec((1, D, GC), lambda i: (base + g(i), 0, 0))
    so = lambda r: pl.BlockSpec((1, r, GC), lambda i: (s(i), 0, g(i)))
    a, b = weights
    ins = [hidden, pooled_low, a, a, b, b, table, a, bias]
    specs = [seq(L), seq(R), mat(0), mat(G), mat(0), mat(G), whole(2 * L, D),
             pl.BlockSpec((1, GC, GC), lambda i: (2 * G, g(i), 0)), pl.BlockSpec((1, 1, L), lambda i: (s(i), 0, 0))]
    aliases = {}
    if held is not None:
        aliases = {len(ins) + i: i for i in range(7)}
        ins += list(held)
        specs += [pl.BlockSpec(memory_space=pl.ANY)] * 7
    return pl.pallas_call(
        functools.partial(attend_kernel, start, B),
        grid=(stop - start,),
        in_specs=specs,
        out_specs=[so(R), pl.BlockSpec((1, 1, GH, R, L), lambda i: (s(i), g(i), 0, 0, 0)), so(R), so(R), so(L), so(L),
                   pl.BlockSpec((2 * L, GC), lambda i: (0, g(i)))],
        out_shape=[sds((B, R, D), BF), sds((B, G, GH, R, L), F32), sds((B, R, D), BF), sds((B, R, D), BF),
                   sds((B, L, D), BF), sds((B, L, D), BF), sds((2 * L, D), BF)],
        scratch_shapes=[pltpu.VMEM((2 * L, GC), BF)],
        input_output_aliases=aliases,
        cost_estimate=cost(6 * (stop - start)),
        compiler_params=params(58),
    )(*ins)


def phi_and_slope(z):
    e = jnp.exp(z * z * (-0.5))
    t = 1.0 / (1.0 + (0.3275911 * 0.7071067811865476) * jnp.abs(z))
    poly = t * (0.127414796 + t * (-0.142248368 + t * (0.7107068705 + t * (-0.7265760135 + t * 0.5307027145))))
    tail = poly * e
    phi = jnp.where(z >= 0, 1.0 - tail, tail)
    return phi, phi + z * e * 0.3989422804014327


def norm(x):
    center = x - jnp.mean(x, axis=-1, keepdims=True)
    inv = lax.rsqrt(jnp.mean(center * center, axis=-1, keepdims=True) + EPSILON)
    return center * inv, inv


def norm_back(e, n, inv):
    return inv * (e - jnp.mean(e, axis=-1, keepdims=True) - n * jnp.mean(e * n, axis=-1, keepdims=True))


def add_rows(ref, *values):
    for k, v in enumerate(values):
        ref[k : k + 1, :] += jnp.sum(v, axis=0, keepdims=True)


def mlp_kernel(ctx_ref, pooled_ref, cot_ref, mask_ref, exp_ref, w2_ref, turned_ref,
               out_ref, y1_ref, n1_ref, s1_ref, inner_ref, slope_ref, dx2_ref, e2_ref, sums_ref, small_ref):
    @pl.when(pl.program_id(0) == 0)
    def _():
        sums_ref[...] = jnp.zeros_like(sums_ref)
        small_ref[...] = turned_ref[0, :, 0:128].astype(F32).T

    row = lambda k: small_ref[k : k + 1, :]
    chunks = exp_ref.shape[0] - 1
    x1 = pooled_ref[0] + dot(ctx_ref[0], exp_ref[chunks]) + row(3)
    n1, inv1 = norm(x1)
    n1_ref[0] = n1
    s1_ref[0] = inv1
    y1 = n1 * row(4) + row(5)
    y1l = y1.astype(BF)
    y1_ref[0] = y1l
    x2 = y1 + row(6)
    for c in range(chunks):
        cs = slice(c * FC, (c + 1) * FC)
        z = dot(y1l, exp_ref[c]) + row(9 + c)
        phi, slope = phi_and_slope(z)
        inner = (z * phi).astype(BF)
        inner_ref[0, :, cs] = inner
        slope_ref[0, :, cs] = slope
        x2 += dot(inner, w2_ref[cs, :])
    n2, inv2 = norm(x2)
    m = mask_ref[0]
    out_ref[0] = ((n2 * row(7) + row(8)) * m).astype(BF)
    dy2 = cot_ref[0].astype(F32) * m
    dx2 = norm_back(dy2 * row(7), n2, inv2)
    dx2_ref[0] = dx2
    e2_ref[0] = dx2.astype(BF)
    add_rows(sums_ref, dx2, dy2 * n2, dy2)


def mlp(ctx, pooled, cot, mask, expand, w2, small):
    B, R, D = pooled.shape
    F = w2.shape[0]
    return pl.pallas_call(
        mlp_kernel,
        grid=(B,),
        in_specs=[seqs(R, D), seqs(R, D), seqs(R, D), seqs(R, 1), whole(*expand.shape), whole(F, D),
                  turned_small(D)],
        out_specs=[seqs(R, D), seqs(R, D), seqs(R, D), seqs(R, 1), seqs(R, F), seqs(R, F), seqs(R, D), seqs(R, D),
                   pl.BlockSpec((8, D), lambda s: (0, 0))],
        out_shape=[sds((B, R, D), BF), sds((B, R, D), BF), sds((B, R, D), F32), sds((B, R, 1), F32), sds((B, R, F), BF),
                   sds((B, R, F), F32), sds((B, R, D), F32), sds((B, R, D), BF), sds((8, D), F32)],
        scratch_shapes=[pltpu.VMEM((128, D), F32)],
        cost_estimate=cost(30),
        compiler_params=params(58),
    )(ctx, pooled, cot, mask, expand, w2, small)


def mlp_back_kernel(dx2_ref, e2_ref, slope_ref, n1_ref, s1_ref, exp_ref, w2_ref, turned_ref,
                    e1_ref, dx1_ref, ea_ref, dctx_ref, sums_ref, db1_ref, small_ref):
    @pl.when(pl.program_id(0) == 0)
    def _():
        small_ref[...] = turned_ref[0, :, 0:128].astype(F32).T
        sums_ref[...] = jnp.zeros_like(sums_ref)
        db1_ref[...] = jnp.zeros_like(db1_ref)

    chunks = exp_ref.shape[0] - 1
    e2 = e2_ref[0]
    dy1 = dx2_ref[0]
    for c in range(chunks):
        cs = slice(c * FC, (c + 1) * FC)
        dz = dot_nt(e2, w2_ref[cs, :]) * slope_ref[0, :, cs]
        db1_ref[:, cs] += jnp.sum(dz, axis=0, keepdims=True)
        e1 = dz.astype(BF)
        e1_ref[0, :, cs] = e1
        dy1 += dot_nt(e1, exp_ref[c])
    n1 = n1_ref[0]
    dx1 = norm_back(dy1 * small_ref[4:5, :], n1, s1_ref[0])
    dx1_ref[0] = dx1
    ea = dx1.astype(BF)
    ea_ref[0] = ea
    dctx_ref[0] = dot_nt(ea, exp_ref[chunks]).astype(BF)
    add_rows(sums_ref, dx1, dy1 * n1, dy1)


def mlp_back(dx2, e2, slope, n1, s1, expand, w2, small):
    B, R, D = dx2.shape
    F = w2.shape[0]
    return pl.pallas_call(
        mlp_back_kernel,
        grid=(B,),
        in_specs=[seqs(R, D), seqs(R, D), seqs(R, F), seqs(R, D), seqs(R, 1), whole(*expand.shape), whole(F, D),
                  turned_small(D)],
        out_specs=[seqs(R, F), seqs(R, D), seqs(R, D), seqs(R, D), pl.BlockSpec((8, D), lambda s: (0, 0)),
                   pl.BlockSpec((1, F), lambda s: (0, 0))],
        out_shape=[sds((B, R, F), BF), sds((B, R, D), F32), sds((B, R, D), BF), sds((B, R, D), BF), sds((8, D), F32),
                   sds((1, F), F32)],
        scratch_shapes=[pltpu.VMEM((128, D), F32)],
        cost_estimate=cost(21),
        compiler_params=params(58),
    )(dx2, e2, slope, n1, s1, expand, w2, small)


def deal(half, me, total_ref, put):
    r = total_ref.shape[0] // 32
    for rel in range(32):
        k = jnp.bitwise_xor(me, flat_of(rel, half))
        put(rel // 16, rel % 16, total_ref[pl.ds(pl.multiple_of(k * r, 8), r), :].astype(BF))


def outer_kernel(half, me_ref, a_ref, b_ref, keep_ref, send_ref, turned, total):
    B, R, M = a_ref.shape

    @pl.when(pl.program_id(0) == 0)
    def _():
        turned[...] = a_ref[...].reshape(B * R, M).T

    total[...] = dot(turned[...], b_ref[...].reshape(B * R, b_ref.shape[2]))

    def put(sent, i, v):
        for j in range(v.shape[1] // GC):
            (send_ref if sent else keep_ref)[i, j] = v[:, j * GC : (j + 1) * GC]

    deal(half, me_ref[0], total, put)


def outer_plain_kernel(a_ref, b_ref, out_ref):
    B, R, M = a_ref.shape
    out_ref[...] = dot_tn(a_ref[...].reshape(B * R, M), b_ref[...].reshape(B * R, b_ref.shape[2]))


def outer(me, a, b, cols, half=None, blocks=None):
    B, R, M = a.shape
    N = b.shape[2]
    first, count = blocks or (0, N // cols)
    specs = [pl.BlockSpec((B, R, M), lambda j: (0, 0, 0)), pl.BlockSpec((B, R, cols), lambda j: (0, 0, first + j))]
    price = cost(2.0 * count)
    if half is None:
        return pl.pallas_call(
            outer_plain_kernel, grid=(count,), in_specs=specs,
            out_specs=pl.BlockSpec((M, cols), lambda j: (0, j)),
            out_shape=sds((M, N), F32), cost_estimate=price, compiler_params=params(32))(a, b)
    return pl.pallas_call(
        functools.partial(outer_kernel, half),
        grid=(count,),
        in_specs=[pl.BlockSpec(memory_space=pltpu.SMEM)] + specs,
        out_specs=[pl.BlockSpec((16, cols // GC, M // 32, GC), lambda j: (0, j, 0, 0))] * 2,
        out_shape=[sds((16, count * cols // GC, M // 32, GC), BF)] * 2,
        scratch_shapes=[pltpu.VMEM((M, B * R), BF), pltpu.VMEM((M, cols), F32)],
        cost_estimate=price,
        compiler_params=params(32),
    )(me, a, b)


def wide_outer_kernel(chunks, me_ref, y1_ref, e1_ref, ctx_ref, ea_ref, keep0, send0, keep1, send1, turned, total):
    B, R, D = y1_ref.shape
    j = pl.program_id(0)
    flat = lambda ref: ref[...].reshape(B * R, D)

    def dealt(half, base):
        def put(sent, i, v):
            ref = ((keep0, send0), (keep1, send1))[half][sent]
            for b in range(D // GC):
                ref[i, base + b] = v[:, b * GC : (b + 1) * GC]

        deal(half, me_ref[0], total, put)

    @pl.when(j == 0)
    def _():
        turned[...] = flat(y1_ref).T

    @pl.when(j < chunks)
    def _():
        total[...] = dot(turned[...], flat(e1_ref))

    @pl.when(j == chunks)
    def _():
        total[...] = dot_tn(flat(ctx_ref), flat(ea_ref))
        dealt(0, chunks // 2 * (D // GC))

    @pl.when(j < chunks // 2)
    def _():
        dealt(0, j * (D // GC))

    @pl.when((j >= chunks // 2) & (j < chunks))
    def _():
        dealt(1, (j - chunks // 2) * (D // GC))


def wide_outer(me, y1, e1, ctx, ea):
    B, R, D = y1.shape
    F = e1.shape[2]
    chunks = F // D
    n = D // GC
    shapes = [(16, m, D // 32, GC) for m in (chunks // 2 * n + n, chunks // 2 * n) for _ in range(2)]
    out = pl.pallas_call(
        functools.partial(wide_outer_kernel, chunks),
        grid=(chunks + 1,),
        in_specs=[pl.BlockSpec(memory_space=pltpu.SMEM), whole(B, R, D),
                  pl.BlockSpec((B, R, D), lambda j: (0, 0, jnp.minimum(j, chunks - 1))), whole(B, R, D), whole(B, R, D)],
        out_specs=[whole(*shape) for shape in shapes],
        out_shape=[sds(shape, BF) for shape in shapes],
        scratch_shapes=[pltpu.VMEM((D, B * R), BF), pltpu.VMEM((D, D), F32)],
        cost_estimate=cost(12),
        compiler_params=params(40),
    )(me, y1, e1, ctx, ea)
    return tuple(out[:2]), tuple(out[2:])


def tall_outer_kernel(steps, me_ref, a_ref, b_ref, keep0_ref, send0_ref, keep1_ref, send1_ref, total):
    B, R, M = a_ref.shape
    i = pl.program_id(0)
    v = dot_tn(a_ref[...].reshape(B * R, M), b_ref[...].reshape(B * R, b_ref.shape[2]))
    total[pl.ds(pl.multiple_of(i * M, 8), M), :] = v

    @pl.when(i == steps - 1)
    def _():
        r = keep0_ref.shape[2]
        for half, refs in enumerate(((keep0_ref, send0_ref), (keep1_ref, send1_ref))):
            for rel in range(32):
                k = jnp.bitwise_xor(me_ref[0], flat_of(rel, half))
                at = pl.multiple_of(k * (2 * r) + half * r, 8)
                refs[rel // 16][rel % 16, 0] = total[pl.ds(at, r), :].astype(BF)


def tall_outer(me, a, b, rows):
    B, R, M = a.shape
    N = b.shape[2]
    r = M // 64
    out = pl.pallas_call(
        functools.partial(tall_outer_kernel, M // rows),
        grid=(M // rows,),
        in_specs=[pl.BlockSpec(memory_space=pltpu.SMEM), pl.BlockSpec((B, R, rows), lambda i: (0, 0, i)), whole(B, R, N)],
        out_specs=[whole(16, 1, r, N)] * 4,
        out_shape=[sds((16, 1, r, N), BF)] * 4,
        scratch_shapes=[pltpu.VMEM((M, N), F32)],
        cost_estimate=cost(10),
        compiler_params=params(58),
    )(me, a, b)
    return (out[0], out[1]), (out[2], out[3])


def small_deal_kernel(me_ref, *refs):
    sums, (sums1, sums2, db1, keep_ref, send_ref, total, turned) = refs[:-7], refs[-7:]
    D = sums1.shape[1]
    total[...] = jnp.zeros_like(total)
    for g, s in enumerate(sums):
        total[0:3, g * GC : (g + 1) * GC] = s[0:3, :]
    total[3:6, :] = sums1[0:3, :]
    total[6:9, :] = sums2[0:3, :]
    for i in range(db1.shape[1] // D):
        total[9 + i : 10 + i, :] = db1[0:1, i * D : (i + 1) * D]
    turned[...] = jnp.concatenate([total[...].T, jnp.zeros((D, GC - total.shape[0]), F32)], axis=1)

    def put(sent, i, v):
        (send_ref if sent else keep_ref)[i, 0] = v

    deal(0, me_ref[0], turned, put)


def small_deal(me, sums, sums1, sums2, db1):
    D = sums1.shape[1]
    n = 4 + len(sums)
    return pl.pallas_call(
        small_deal_kernel,
        in_specs=[pl.BlockSpec(memory_space=pltpu.SMEM)] + [pl.BlockSpec(memory_space=pltpu.VMEM)] * (n - 1),
        out_specs=[pl.BlockSpec(memory_space=pltpu.VMEM)] * 2,
        out_shape=[sds((16, 1, D // 32, GC), BF)] * 2,
        scratch_shapes=[pltpu.VMEM((128, D), F32), pltpu.VMEM((D, GC), F32)],
        cost_estimate=cost(2),
        compiler_params=params(24),
    )(me, *sums, sums1, sums2, db1)


def attend_back_kernel(plan, *refs):
    (me_ref, probs_ref, dctx_ref, qu_ref, qw_ref, keys_ref, values_ref, rel_ref, hidt_ref, lowt_ref, tablet_ref) = refs[:11]
    outs = refs[11 : 14]
    dq_ref, dk_ref, dv_ref = outs
    grads = refs[14 : -8]
    sums_ref = refs[-8]
    acc_q, acc_k, acc_v, acc_r, acc_dv, dkt, dvt = refs[-7:]
    step = pl.program_id(0)
    half, L = probs_ref.shape[3], probs_ref.shape[4]
    blk = half // 2

    @pl.when(step == 0)
    def _():
        for a in (acc_q, acc_k, acc_v, acc_r, acc_dv, sums_ref):
            a[...] = jnp.zeros_like(a)

    across = lax.broadcasted_iota(jnp.int32, (half, half), 0) + lax.broadcasted_iota(jnp.int32, (half, half), 1)
    flip = (across == half - 1).astype(F32).astype(BF)
    lane = lax.broadcasted_iota(jnp.int32, (1, GC), 1)
    dctx = dctx_ref[0]
    dctx_t = dctx.T
    qu_t = qu_ref[0].T
    qwr_t = dot(flip, qw_ref[0]).astype(BF).T
    keys = keys_ref[0]
    values = values_ref[0]
    dqu = dqw = None
    for h in range(GH):
        mine = (lane >= h * HEAD) & (lane < (h + 1) * HEAD)
        sel = slice(h * HEAD, (h + 1) * HEAD)
        p = probs_ref[0, 0, h]
        dp = dot_nt(jnp.where(mine, dctx.astype(F32), 0.0).astype(BF), values)
        t = p * dp
        draw = (t - p * jnp.sum(t, axis=-1, keepdims=True)).astype(BF)
        dvt[sel, :] = dot(dctx_t[sel], p.astype(BF))
        both = dot(jnp.concatenate([qu_t[sel], flip], axis=0), draw)
        dkt[sel, :] = both[:HEAD] * 0.125
        back = both[HEAD:]
        a = dot(back.astype(BF), keys)
        tables = []
        for b in range(2):
            x = jnp.concatenate([back[b * blk : (b + 1) * blk], jnp.zeros((blk, half), F32)], axis=1)
            x = pltpu.roll(x, 2, 1, stride=2, stride_axis=0).astype(BF)
            m0 = half * b
            tables.append(dot(x, rel_ref[m0 : m0 + 3 * half, :]))
            acc_r[sel, m0 : m0 + 3 * half] += dot(qwr_t[sel, b * blk : (b + 1) * blk], x)
        c = jnp.concatenate(tables, axis=0)
        dqu, dqw = (a, c) if dqu is None else (jnp.where(mine, a, dqu), jnp.where(mine, c, dqw))
    dqu = dqu * 0.125
    dqw = dqw * 0.125
    dq = dot(flip, (dqu + dqw).astype(BF)).astype(BF)
    dk = dkt[...].astype(BF).T
    dvf = dvt[...]
    dv = dvf.astype(BF).T
    dq_ref[0] = dq
    dk_ref[0] = dk
    dv_ref[0] = dv
    acc_dv[...] += dvf
    add_rows(sums_ref, dqu, dqw)
    acc_q[...] += dot(lowt_ref[0], dq)
    acc_k[...] += dot(hidt_ref[0], dk)
    acc_v[...] += dot(hidt_ref[0], dv)

    @pl.when(step == pl.num_programs(0) - 1)
    def _():
        sums_ref[2:3, :] = jnp.sum(acc_dv[...].T, axis=0, keepdims=True)
        dr = acc_r[...] * 0.125
        hi = dr.astype(BF)
        lo = (dr - hi.astype(F32)).astype(BF)
        tt = tablet_ref[...]
        if plan is None:
            for i, a in enumerate((acc_q, acc_k, acc_v)):
                grads[0][i] = a[...]
            grads[0][3] = dot_nt(tt, hi) + dot_nt(tt, lo)
        else:
            for i in range(4):
                half = plan[i]
                at = plan[:i].count(half)
                base = 2 * sorted(set(plan)).index(half)
                acc = (acc_q, acc_k, acc_v, acc_q)[i]
                if i == 3:
                    acc_q[...] = dot_nt(tt, hi) + dot_nt(tt, lo)

                def put(sent, j, v):
                    grads[base + sent][j, at] = v

                deal(half, me_ref[0], acc, put)


def attend_back(me, g, probs, dctx, qu, qw, keys, values, rel, hid_t, low_t, table_t, plan=None):
    B, R, D = qu.shape
    L = 2 * R
    so = lambda r: pl.BlockSpec((1, r, GC), lambda s: (s, 0, g))
    if plan is None:
        grad_specs = [pl.BlockSpec((4, D, GC), lambda s: (0, 0, 0))]
        grad_shapes = [sds((4, D, GC), F32)]
    else:
        sizes = [(16, plan.count(h), D // 32, GC) for h in sorted(set(plan)) for _ in range(2)]
        grad_specs = [whole(*size) for size in sizes]
        grad_shapes = [sds(size, BF) for size in sizes]
    return pl.pallas_call(
        functools.partial(attend_back_kernel, plan),
        grid=(B,),
        in_specs=[pl.BlockSpec(memory_space=pltpu.SMEM),
                  pl.BlockSpec((1, 1, GH, R, L), lambda s: (s, g, 0, 0, 0)), so(R), so(R), so(R), so(L), so(L),
                  pl.BlockSpec((2 * L, GC), lambda s: (0, g)), seqs(D, L), seqs(D, R), whole(D, 2 * L)],
        out_specs=[seqs(R, GC), seqs(L, GC), seqs(L, GC)] + grad_specs + [pl.BlockSpec((8, GC), lambda s: (0, 0))],
        out_shape=[sds((B, R, GC), BF), sds((B, L, GC), BF), sds((B, L, GC), BF)] + grad_shapes + [sds((8, GC), F32)],
        scratch_shapes=[pltpu.VMEM((D, GC), F32)] * 3 + [pltpu.VMEM((GC, 2 * L), F32)] + [pltpu.VMEM((GC, L), F32)] * 3,
        cost_estimate=cost(22),
        compiler_params=params(48),
    )(me, probs, dctx, qu, qw, keys, values, rel, hid_t, low_t, table_t)


def input_grad_kernel(at, *refs):
    groups = len(at)
    dqs, dks, dvs = refs[:groups], refs[groups : 2 * groups], refs[2 * groups : 3 * groups]
    dx1_ref, weights, out_ref, wide = refs[3 * groups], refs[3 * groups + 1 : -2], refs[-2], refs[-1]
    half = dx1_ref.shape[1]
    shared = dx1_ref[0]
    total = None
    for g in range(groups):
        wq, wk, wv = (weights[a][i] for a, i in at[g])
        shared += dot_nt(dqs[g][0], wq)
        t = dot_nt(dks[g][0], wk) + dot_nt(dvs[g][0], wv)
        total = t if total is None else total + t
    shared = shared * 0.5
    for i in range(wide.shape[0]):
        cs = slice(i * 128, (i + 1) * 128)
        wide[i, pl.ds(0, half, stride=2), :] = shared[:, cs]
        wide[i, pl.ds(1, half, stride=2), :] = shared[:, cs]
        out_ref[0, :, cs] = (total[:, cs] + wide[i]).astype(BF)


def input_grad(dqs, dks, dvs, dx1, weights, at):
    B, R, D = dx1.shape
    L = 2 * R
    G = len(dqs)
    return pl.pallas_call(
        functools.partial(input_grad_kernel, at),
        grid=(B,),
        in_specs=[seqs(R, GC)] * G + [seqs(L, GC)] * (2 * G) + [seqs(R, D)] + [whole(*w.shape) for w in weights],
        out_specs=seqs(L, D),
        out_shape=sds((B, L, D), BF),
        scratch_shapes=[pltpu.VMEM((D // 128, L, 128), F32)],
        cost_estimate=cost(10),
        compiler_params=params(40),
    )(*dqs, *dks, *dvs, dx1, *weights)


def adamw(weight, moment, second, gradient, rates):
    new_moment = rates[1] * moment + (1.0 - rates[1]) * gradient
    new_second = rates[2] * second + (1.0 - rates[2]) * gradient * gradient
    moment_hat = new_moment / rates[4]
    second_hat = new_second / rates[5]
    new_weight = weight - rates[0] * (moment_hat / (jnp.sqrt(second_hat) + 1e-08) + rates[3] * weight)
    return (new_weight, new_moment, new_second)


def update_kernel(plan, rates_ref, w_ref, m_ref, v_ref, *refs):
    terms, (grad_ref, w_out, m_out, v_out) = refs[:-4], refs[-4:]
    rates = [rates_ref[i] for i in range(6)]
    for first, count, block, dest in plan:
        g = None
        for t in terms[first : first + count]:
            v = (t[...] if block is None else t[block]).astype(F32)
            g = v if g is None else g + v
        grad_ref[dest] = g
        w_out[dest], m_out[dest], v_out[dest] = adamw(w_ref[dest], m_ref[dest], v_ref[dest], g, rates)


def update(rates, w, m, v, terms, plan=None):
    plan = plan or [(0, len(terms), None, (slice(None),) * w.ndim)]
    return pl.pallas_call(
        functools.partial(update_kernel, plan),
        in_specs=[pl.BlockSpec(memory_space=pltpu.SMEM)] + [pl.BlockSpec(memory_space=pltpu.VMEM)] * (3 + len(terms)),
        out_specs=[pl.BlockSpec(memory_space=pltpu.VMEM)] * 4,
        out_shape=[sds(w.shape, F32)] * 4,
        cost_estimate=cost(2),
        compiler_params=params(24),
    )(rates, w, m, v, *terms)


def last_update_kernel(plan, small_at, rates_ref, *refs):
    ins, (pad, *_) = refs[:-9], refs[-1:]
    att, small, terms = ins[:3], ins[3:6], ins[6:]
    outs = refs[-9:-1]
    update_kernel(plan, rates_ref, *att, *terms, *outs[:4])
    first, count, block = small_at
    g = sum(t[block].astype(F32) for t in terms[first : first + count])
    V, r = small[0].shape
    pad[...] = jnp.zeros_like(pad)
    pad[0:r, :] = g[:, 0:128]
    pad[...] = pad[...].T
    rates = [rates_ref[i] for i in range(6)]
    g = pad[0:V, 0:r]
    outs[4][...] = g
    outs[5][...], outs[6][...], outs[7][...] = adamw(small[0][...], small[1][...], small[2][...], g, rates)


def last_update(rates, attention, small, terms, plan, small_at):
    like = [attention[0]] * 4 + [small[0]] * 4
    out = pl.pallas_call(
        functools.partial(last_update_kernel, plan, small_at),
        in_specs=[pl.BlockSpec(memory_space=pltpu.SMEM)] + [pl.BlockSpec(memory_space=pltpu.VMEM)] * (6 + len(terms)),
        out_specs=[pl.BlockSpec(memory_space=pltpu.VMEM)] * 8,
        out_shape=[sds(a.shape, F32) for a in like],
        scratch_shapes=[pltpu.VMEM((128, 128), F32)],
        cost_estimate=cost(3),
        compiler_params=params(24),
    )(rates, *attention, *small, *terms)
    return out[:4], out[4:]


def shards(fast, hidden, lengths, key_mask, cotangent, attention_weight, expand_weight, contract_weight, small_params,
           mean_attention, mean_expand, mean_contract, mean_small,
           square_attention, square_expand, square_contract, square_small, update_step, update_rates):
    B, L, D = hidden.shape
    R = L // 2
    F = expand_weight.shape[1]
    G = D // GC
    C = F // FC
    H = C // 2
    r = attention_weight.shape[1]
    V = small_params.shape[0]
    me = (lax.axis_index("dp") * lax.axis_size("fsdp") + lax.axis_index("fsdp")).astype(jnp.int32).reshape(1)

    table = rel_table(L, D)
    table, table_t = jnp.asarray(table), jnp.asarray(np.ascontiguousarray(table.T))

    def correction():
        return jnp.concatenate([update_rates, 1.0 - jnp.power(update_rates[1:3], update_step[0].astype(F32))])

    at = tuple(((0, g), (0, G + g), (1, g)) for g in range(G))
    if fast:
        first, third = parcel(attention_weight, expand_weight, contract_weight, small_params)
        gate1 = Gather(me, first, 2 * G + 1)
        gate1.far(1, 2, 3)
        pooled, pooled_low, hid_t, low_t, bias, mask = prepare(hidden, lengths, key_mask)
        rates = correction()
        token = gate1.plane(pooled_low, rates)
        gate2 = Gather(me, third, C + 1, (True, False))
        near = gate2.far(1, then=token)
        token = gate1.plane_again(near)
        middle = gate2.far(2, then=token)
        token = gate1.cores(middle)
        gate2.far(3, then=token)
        weights = gate1.result()
        low = after(pooled_low, gate2.plane(weights[0]))
        stops = (B * G // 3, 3 * B * G // 4, B * G)
        held = attend(0, stops[0], hidden, low, weights, table, bias)
        low = after(low, gate2.plane_again(held[0]))
        held = attend(stops[0], stops[1], hidden, low, weights, table, bias, held)
        low = after(low, gate2.cores(held[0]))
        held = attend(stops[1], stops[2], hidden, low, weights, table, bias, held)
        w_eo, w2 = gate2.result(held[0])
    else:
        cut = lambda a, c: a.astype(BF).reshape(r, -1, c).transpose(1, 0, 2)
        small_t = jnp.pad(small_params.T, ((0, 0), (0, GC - V))).astype(BF)[None]
        cols = [cut(attention_weight[i], GC) for i in range(4)]
        full = lambda a: lax.all_gather(a, ALL, axis=1, tiled=True)
        first = full(jnp.concatenate(cols[:2] + [small_t] + cols[2:], axis=0))
        w_eo = full(jnp.concatenate([cut(expand_weight, FC), cut(attention_weight[4], FC)], axis=0))
        w2 = lax.all_gather(contract_weight.astype(BF), ALL, axis=0, tiled=True)
        weights = (first[: 2 * G + 1], first[2 * G + 1 :])
        pooled, pooled_low, hid_t, low_t, bias, mask = prepare(hidden, lengths, key_mask)
        rates = correction()
        held = attend(0, B * G, hidden, pooled_low, weights, table, bias)
    ctx, probs, qu, qw, keys, values, rel = held
    small = weights[0]
    out, y1, n1, s1, inner, slope, dx2, e2, sums2 = mlp(ctx, pooled, cotangent, mask, w_eo, w2, small)

    def backward(g, dctx, plan=None):
        return attend_back(me, g, probs, dctx, qu, qw, keys, values, rel, hid_t, low_t, table_t, plan)

    def hidden_grad(back, dx1):
        return input_grad([b[0] for b in back], [b[1] for b in back], [b[2] for b in back], dx1, weights, at)

    if not fast:
        scatter = lambda a, d: lax.psum_scatter(a, ALL, scatter_dimension=d, tiled=True)
        e1, dx1, ea, dctx, sums1, db1 = mlp_back(dx2, e2, slope, n1, s1, w_eo, w2, small)
        back = [backward(g, dctx) for g in range(G)]
        in_grad = hidden_grad(back, dx1)
        d_att = jnp.concatenate([b[3] for b in back], axis=2)
        d_att = jnp.concatenate([d_att, outer(me, ctx, ea, 384)[None]], axis=0)
        d_small = jnp.concatenate([b[-1][0:3] for b in back], axis=1)
        d_small = jnp.concatenate([d_small, sums1[0:3], sums2[0:3], db1.reshape(-1, D)], axis=0)
        attention_terms, attention_plan = [scatter(d_att, 1)], None
        expand_terms, expand_plan = [scatter(outer(me, y1, e1, FC), 0)], None
        contract_terms = [scatter(outer(me, inner, e2, 384), 0)]
        contract_up = update(rates, contract_weight, mean_contract, square_contract, contract_terms)
        small_grad = scatter(d_small, 1)
    else:
        half0, half1 = tall_outer(me, inner, e2, 768)
        sum1 = Reduction([half0], [half1])
        e1, dx1, ea, dctx, sums1, db1 = mlp_back(dx2, after(e2, half0, half1), slope, n1, s1, w_eo, w2, small)
        sum1.cross(e1)
        wide0, wide1 = wide_outer(me, after(y1, sum1.token), e1, ctx, ea)
        sum1.cross(wide0)
        wide0, wide1 = after((wide0, wide1), sum1.token)
        sum2 = Reduction([wide0], [wide1])
        back = [backward(0, after(dctx, sum1.token), (0, 0, 0, 0))]
        sum2.cross(back[0][0])
        sum1.along(sum2.token)
        back.append(backward(1, after(dctx, sum1.token, sum2.token), (1, 1, 1, 1)))
        sum2.cross(back[1][0])
        every = slice(None)
        r2 = contract_weight.shape[0] // 2
        contract_plan = [(0, 4, i, (slice(i * r2, (i + 1) * r2), every)) for i in range(2)]
        contract_terms = after(sum1.terms, sum2.token)
        contract_up = update(rates, contract_weight, mean_contract, square_contract, contract_terms, contract_plan)
        grads0, grads1 = after((tuple(back[0][3:5]), tuple(back[1][3:5])), contract_up[0])
        sum3 = Reduction([grads0], [grads1])
        sum3.cross()
        back.append(backward(2, after(dctx, sum3.token), (0, 0, 1, 1)))
        sum2.along(back[2][0])
        sum3.cross(sum2.token)
        d_small = small_deal(me, [b[-1] for b in back], sums1, sums2, after(db1, sum3.token))
        sum4 = Reduction([tuple(back[2][3:5]), tuple(d_small)], [tuple(back[2][5:7])])
        sum4.cross()
        sum3.along(sum4.token)
        sum4.cross(sum3.token)
        in_grad = hidden_grad(back, after(dx1, sum4.token))
        terms3 = settle(after(sum3.terms, in_grad))
        expand_weight = after(expand_weight, terms3)
        sum4.along(terms3)
        expand_terms = sum2.terms
        per = F // GC // 2
        narrow = lambda j: slice(j * GC, (j + 1) * GC)
        expand_plan = [(0, 4, j + (G if j >= per else 0), (every, narrow(j))) for j in range(2 * per)]
        attention_terms = sum2.terms + [terms3] + sum4.terms
        attention_plan = [(0, 4, per + j, (4, every, narrow(j))) for j in range(G)]
        attention_plan += [(4, 1, 4 * g + m, (m, every, narrow(g))) for g in range(2) for m in range(4)]
        attention_plan += [(5, 4, m + (m > 1), (m, every, narrow(2))) for m in range(4)]
        attention_up, small_up = last_update(
            rates, (attention_weight, mean_attention, square_attention), (small_params, mean_small, square_small),
            attention_terms, attention_plan, (5, 4, 2))
    expand_up = update(rates, expand_weight, mean_expand, square_expand, expand_terms, expand_plan)
    if not fast:
        attention_up = update(rates, attention_weight, mean_attention, square_attention, attention_terms, attention_plan)
        small_up = update(rates, small_params, mean_small, square_small, [small_grad])
    ups = (attention_up, expand_up, contract_up, small_up)
    return (out, in_grad) + tuple(u[i] for i in range(4) for u in ups)


def solution(mesh):
    outer_rows = P(ALL, None)
    middle = P(None, ALL, None)
    inner_cols = P(None, ALL)
    table = (middle, outer_rows, outer_rows, inner_cols)
    tokens = P(ALL, None, None)
    in_specs = (tokens, P(ALL), outer_rows, tokens) + table * 3 + (P(), P())
    out_specs = (tokens, tokens) + table * 4
    fast = mesh.shape["dp"] == 8 and mesh.shape["fsdp"] == 4
    return jax.shard_map(
        functools.partial(shards, fast), mesh=mesh, in_specs=in_specs, out_specs=out_specs, check_vma=False
    )
```

```python
import functools
import math

import jax
import jax.numpy as jnp
import ml_dtypes
import numpy as np
from jax import lax
from jax.experimental import pallas as pl
from jax.experimental.pallas import tpu as pltpu
from jax.sharding import PartitionSpec as P

HEAD = 64
GC = 256
GH = GC // HEAD
TILE = 16
FC = 768
EPSILON = 1e-06
MASK_FILL = -1000000000.0
ALL = ("dp", "fsdp")
F32 = jnp.float32
BF = jnp.bfloat16
NT = (((1,), (1,)), ((), ()))
TN = (((0,), (0,)), ((), ()))


def dot(a, b):
    return jnp.dot(a, b, preferred_element_type=F32)


def dot_nt(a, b):
    return lax.dot_general(a, b, NT, preferred_element_type=F32)


def dot_tn(a, b):
    return lax.dot_general(a, b, TN, preferred_element_type=F32)


def sds(shape, dtype):
    return jax.ShapeDtypeStruct(shape, dtype)


def seqs(*tail):
    return pl.BlockSpec((1,) + tail, lambda s, *_: (s,) + (0,) * len(tail))


def whole(*shape):
    return pl.BlockSpec(shape, lambda *_: (0,) * len(shape), pipeline_mode=pl.Buffered(1))


def turned_small(width):
    return pl.BlockSpec((1, width, GC), lambda s: (2 * width // GC, 0, 0), pipeline_mode=pl.Buffered(1))


def params(mib):
    return pltpu.CompilerParams(vmem_limit_bytes=mib << 20)


def cost(us):
    return pl.CostEstimate(flops=int(us * 1.1e9), bytes_accessed=int(us * 3.5e6), transcendentals=0)


def rel_table(length, width):
    places = length - np.arange(2 * length, dtype=np.float32)
    half_width = width // 2
    frequency = np.exp(np.arange(half_width, dtype=np.float32) * np.float32(-2.0 * math.log(10000.0) / width))
    angles = places[:, None] * frequency[None, :]
    return np.concatenate([np.sin(angles), np.cos(angles)], axis=1).astype(ml_dtypes.bfloat16)


X, Y, CORE, Z = 1, 2, 4, 8
HALVES = ((X, Y), (Y, X))


def pairs(bit):
    return [(d, d ^ bit) for d in range(32)]


def swap(a, bit):
    return lax.ppermute(a, ALL, pairs(bit))


def flat_of(rel, half):
    low, high = HALVES[half]
    return (rel & 3) * Z + (rel >> 2 & 1) * low + (rel >> 3 & 1) * high + (rel >> 4 & 1) * CORE


def after(x, *earlier):
    return lax.optimization_barrier((x, earlier))[0]


def assemble_kernel(stacked, me_ref, *refs):
    ins, outs = refs[:8], refs[8:]
    for half in range(2):
        for rel in range(32):
            k = jnp.bitwise_xor(me_ref[0], flat_of(rel, half))
            src = ins[4 * half + rel // 8]
            for i in range(src.shape[1]):
                if stacked[half]:
                    outs[half][i, k] = src[rel % 8, i]
                else:
                    outs[half][k, i] = src[rel % 8, i]


def small_call(body, shapes, dtype, *ins, mib=32):
    return pl.pallas_call(
        body,
        in_specs=[pl.BlockSpec(memory_space=pltpu.VMEM)] * len(ins),
        out_specs=[pl.BlockSpec(memory_space=pltpu.VMEM)] * len(shapes),
        out_shape=[sds(shape, dtype) for shape in shapes],
        cost_estimate=cost(2),
        compiler_params=params(mib),
    )(*ins)


def halve(parts, split, mib=32):
    n, r, c = parts[0].shape

    def body(*refs):
        first, second = refs[-2:]
        for k, ref in enumerate(refs[:-2]):
            first[k] = ref[:split]
            second[k] = ref[split:]

    return small_call(body, [(len(parts), split, r, c), (len(parts), n - split, r, c)], parts[0].dtype, *parts, mib=mib)


def double(halves, got):
    def body(a, b, a_got, b_got, a_out, b_out):
        for mine, other, out in ((a, a_got, a_out), (b, b_got, b_out)):
            m = mine.shape[0]
            out[:m] = mine[...]
            out[m:] = other[...]

    shapes = [(2 * h.shape[0],) + h.shape[1:] for h in halves]
    return small_call(body, shapes, halves[0].dtype, *halves, *got)


def parcel(attention, expand, contract, small):
    r, F = expand.shape
    V = small.shape[0]
    C = F // FC
    G = attention.shape[2] // GC

    def body(att_ref, exp_ref, con_ref, small_ref, first, third, pad):
        pad[...] = jnp.zeros_like(pad)
        pad[0:V, 0:r] = small_ref[...]
        turned = pad[...].T
        narrow = lambda m, g: att_ref[m, :, g * GC : (g + 1) * GC].astype(BF)
        for g in range(G):
            for i, m in ((0, 0), (G, 1), (2 * G + 1, 2), (3 * G + 1, 3)):
                first[i + g] = narrow(m, g)
        first[2 * G] = jnp.concatenate([turned[0:r, :], jnp.zeros((r, GC - 128), F32)], axis=1).astype(BF)
        for i in range(C):
            third[i] = exp_ref[:, i * FC : (i + 1) * FC].astype(BF)
        third[C] = att_ref[4].astype(BF)
        for i in range(C):
            third[C + 1 + i] = con_ref[i * r : (i + 1) * r, :].astype(BF)

    shapes = [(4 * G + 1, r, GC), (2 * C + 1, r, FC)]
    return pl.pallas_call(
        body,
        in_specs=[pl.BlockSpec(memory_space=pltpu.VMEM)] * 4,
        out_specs=[pl.BlockSpec(memory_space=pltpu.VMEM)] * 2,
        out_shape=[sds(shape, BF) for shape in shapes],
        scratch_shapes=[pltpu.VMEM((128, 128), F32)],
        cost_estimate=cost(2),
        compiler_params=params(58),
    )(attention, expand, contract, small)


class Gather:
    def __init__(self, me, part, split, stacked=(True, True)):
        self.me, self.part, self.split, self.stacked = me, part, split, stacked
        self.along = [part]

    def far(self, *ks, then=()):
        part = after(self.part, then) if then else self.part
        self.along += [swap(part, k * Z) for k in ks]
        return self.along[-1]

    def plane(self, *earlier):
        along = after(self.along, *earlier) if earlier else self.along
        self.halves = halve(along, self.split, 32 if self.part.shape[2] == GC else 58)
        self.got = [swap(h, HALVES[i][0]) for i, h in enumerate(self.halves)]
        return self.halves

    def plane_again(self, *earlier):
        halves, got = after((self.halves, self.got), *earlier) if earlier else (self.halves, self.got)
        self.firsts = double(halves, got)
        self.seconds = [swap(h, HALVES[i][1]) for i, h in enumerate(self.firsts)]
        return self.firsts

    def cores(self, *earlier):
        firsts, seconds = after((self.firsts, self.seconds), *earlier) if earlier else (self.firsts, self.seconds)
        self.pieces = []
        for f, s in zip(firsts, seconds):
            self.pieces += [f, s, swap(f, CORE), swap(s, CORE)]
        return firsts, seconds

    def result(self, *earlier):
        pieces = after(self.pieces, *earlier) if earlier else self.pieces
        n, r, c = self.part.shape
        wide = min(c, 384)
        counts = [self.split, n - self.split]
        specs = [pl.BlockSpec((8, m, r, wide), lambda j: (0, 0, 0, j)) for m in counts for _ in range(4)]
        shapes, outs = [], []
        for m, stacked in zip(counts, self.stacked):
            lead = (m, 32) if stacked else (32, m)
            shapes.append(sds(lead + (r, c), self.part.dtype))
            outs.append(pl.BlockSpec(lead + (r, wide), lambda j: (0, 0, 0, j)))
        out = pl.pallas_call(
            functools.partial(assemble_kernel, self.stacked),
            grid=(c // wide,),
            in_specs=[pl.BlockSpec(memory_space=pltpu.SMEM)] + specs,
            out_specs=outs,
            out_shape=shapes,
            cost_estimate=cost(4),
            compiler_params=params(58),
        )(self.me, *pieces)
        return [o.reshape(m, 32 * r, c) if stacked else o.reshape(32 * m * r, c) for o, m, stacked in zip(out, counts, self.stacked)]


def join_kernel(plan, *refs):
    n = 1 + max(w for blocks in plan for _, terms in blocks for w, _ in terms)
    ins, outs = refs[:n], refs[n:]
    for out, blocks in zip(outs, plan):
        for place, terms in blocks:
            total = None
            for w, at in terms:
                v = ins[w][at].astype(F32)
                total = v if total is None else total + v
            out[place] = total.astype(BF)


def join(plan, shapes, ins):
    return pl.pallas_call(
        functools.partial(join_kernel, plan),
        in_specs=[pl.BlockSpec(memory_space=pltpu.VMEM)] * len(ins),
        out_specs=[pl.BlockSpec(memory_space=pltpu.VMEM)] * len(shapes),
        out_shape=[sds(shape, BF) for shape in shapes],
        cost_estimate=cost(1),
        compiler_params=params(32),
    )(*ins)


def settle(terms):
    def body(*refs):
        total = refs[0][...].astype(F32)
        for ref in refs[1:-1]:
            total += ref[...].astype(F32)
        refs[-1][...] = total

    return small_call(body, [terms[0].shape], F32, *terms)[0]


class Reduction:
    def __init__(self, *halves):
        self.halves = []
        for h, parts in enumerate(halves):
            self.halves.append([(k, swap(s, CORE)) for k, s in parts])
        self.token = None

    def add(self, *halves):
        for mine, parts in zip(self.halves, halves):
            mine += [(k, swap(s, CORE)) for k, s in parts]

    def flat(self, earlier):
        halves = after(self.halves, *earlier) if earlier else self.halves
        ins, at = [], []
        for parts in halves:
            blocks = []
            for terms in parts:
                blocks += [[(len(ins) + t, b) for t in range(len(terms))] for b in range(terms[0].shape[1])]
                ins += terms
            at.append(blocks)
        return ins, at, ins[0].shape[2:]

    def cross(self, *earlier):
        ins, at, tail = self.flat(earlier)
        n = ins[0].shape[0] // 2
        bit = 1 if n == 8 else 0
        plan, shapes = [], []
        for blocks in at:
            for far in range(2):
                plan.append([((j, b), [(w, (far * n + j, i)) for w, i in terms]) for j in range(n) for b, terms in enumerate(blocks)])
                shapes.append((n, len(blocks)) + tail)
        out = join(plan, shapes, ins)
        self.halves = [[(out[2 * h], swap(out[2 * h + 1], HALVES[h][bit]))] for h in range(2)]
        self.token = out

    def direct(self, *earlier):
        ins, at, tail = self.flat(earlier)
        count = sum(len(blocks) for blocks in at)
        plan = []
        for q in range(4):
            places = []
            b = 0
            for h, blocks in enumerate(at):
                lead = 4 * (q if h == 0 else (q >> 1) + 2 * (q & 1))
                for terms in blocks:
                    places += [((j, b), [(w, (lead + j, i)) for w, i in terms]) for j in range(4)]
                    b += 1
            plan.append(places)
        out = join(plan, [(4, count) + tail] * 4, ins)
        self.halves = [[tuple([out[0]] + [swap(out[q], (q & 1) * X + (q >> 1) * Y) for q in range(1, 4)])]]
        self.token = out

    def along(self, *earlier, also=()):
        groups = [r.flat(earlier) for r in (self,) + tuple(also)]
        ins, places, tail = [], [[] for _ in range(4)], groups[0][2]
        b = 0
        for more, at, _ in groups:
            base = len(ins)
            ins += more
            for blocks in at:
                for terms in blocks:
                    for k in range(4):
                        places[k].append((b, [(base + w, (k, i)) for w, i in terms]))
                    b += 1
        out = join(places, [(b,) + tail] * 4, ins)
        self.terms = [out[0]] + [swap(out[k], k * Z) for k in range(1, 4)]
        self.token = out


def prepare_kernel(lengths_ref, hidden_ref, key_ref, pooled_ref, low_ref, hidt_ref, lowt_ref, bias_ref, mask_ref, wide):
    hid = hidden_ref[0]
    half, L = pooled_ref.shape[1], hid.shape[0]
    hidt_ref[0] = hid.T
    columns = []
    for i in range(wide.shape[0]):
        wide[i] = hid[:, i * 128 : (i + 1) * 128].astype(F32)
        columns.append((wide[i, pl.ds(0, half, stride=2), :] + wide[i, pl.ds(1, half, stride=2), :]) * 0.5)
    pooled = jnp.concatenate(columns, axis=1)
    pooled_ref[0] = pooled
    low = pooled.astype(BF)
    low_ref[0] = low
    lowt_ref[0] = low.T
    place = lax.broadcasted_iota(jnp.int32, (1, L), 1)
    valid = (key_ref[pl.ds(pl.program_id(0), 1), :] == 1) & (place < lengths_ref[pl.program_id(0)])
    bias_ref[0] = jnp.where(valid, 0.0, MASK_FILL)
    twice = 2 * lax.broadcasted_iota(jnp.int32, (half, L), 0)
    token = lax.broadcasted_iota(jnp.int32, (half, L), 1)
    of = ((token == twice) | (token == twice + 1)).astype(F32).astype(BF)
    rows = jnp.broadcast_to(valid.astype(F32), (16, L)).astype(BF)
    mask_ref[0] = jnp.minimum(dot_nt(of, rows)[:, 0:1], 1.0)


def prepare(hidden, lengths, key_mask):
    B, L, D = hidden.shape
    R = L // 2
    return pl.pallas_call(
        prepare_kernel,
        grid=(B,),
        in_specs=[pl.BlockSpec(memory_space=pltpu.SMEM), seqs(L, D), whole(B, L)],
        out_specs=[seqs(R, D), seqs(R, D), seqs(D, L), seqs(D, R), seqs(1, L), seqs(R, 1)],
        out_shape=[sds((B, R, D), F32), sds((B, R, D), BF), sds((B, D, L), BF), sds((B, D, R), BF), sds((B, 1, L), F32),
                   sds((B, R, 1), F32)],
        scratch_shapes=[pltpu.VMEM((D // 128, L, 128), F32)],
        cost_estimate=cost(6),
        compiler_params=params(58),
    )(lengths, hidden, key_mask)


def attend_kernel(start, per, hidden_ref, pooled_ref, wq_ref, wk_ref, wv_ref, wr_ref, table_ref, small_ref, bias_ref, *refs):
    ctx_ref, probs_ref, qu_ref, qw_ref, keys_ref, values_ref, rel_out, rel_ref = refs[-8:]
    half = hidden_ref.shape[1] // 2
    blk = half // 2
    step = pl.program_id(0)

    @pl.when((step == 0) | (lax.rem(start + step, per) == 0))
    def _():
        rel = dot(table_ref[...], wr_ref[0]).astype(BF)
        rel_ref[...] = rel
        rel_out[...] = rel

    hid = hidden_ref[0]
    small_ref = small_ref[0, :, 0:128].astype(F32).T
    q = dot(pooled_ref[0], wq_ref[0])
    qu = (q + small_ref[0:1, :]).astype(BF)
    qw = (q + small_ref[1:2, :]).astype(BF)
    qu_ref[0] = qu
    qw_ref[0] = qw
    keys_ref[0] = dot(hid, wk_ref[0]).astype(BF)
    values_ref[0] = (dot(hid, wv_ref[0]) + small_ref[2:3, :]).astype(BF)
    bias = bias_ref[0]
    lane = lax.broadcasted_iota(jnp.int32, (1, GC), 1)
    masks = [(lane >= h * HEAD) & (lane < (h + 1) * HEAD) for h in range(GH)]
    qu8 = qu.astype(F32) * 0.125
    qw8 = qw.astype(F32) * 0.125
    wide = 2 * half + 128
    for b in range(2):
        rows = slice(b * blk, (b + 1) * blk)
        m0 = half * (1 - b)
        quh = jnp.concatenate([jnp.where(m, qu8[rows], 0.0).astype(BF) for m in masks], axis=0)
        qwh = jnp.concatenate([jnp.where(m, qw8[rows], 0.0).astype(BF) for m in masks], axis=0)
        content = dot_nt(quh, keys_ref[0])
        placed = dot_nt(qwh, rel_ref[m0 : m0 + 3 * half, :])
        lows = []
        for h in range(GH):
            for r in range(0, blk, TILE):
                hr = slice(h * blk + r, h * blk + r + TILE)
                at = half - 128 - 2 * r // 128 * 128
                moved = pltpu.roll(placed[hr, at : at + wide], 2 * r % 128, 1, stride=2, stride_axis=0)[:, 128:]
                s = content[hr] + moved + bias
                top = jnp.max(s, axis=-1, keepdims=True)
                e = jnp.exp(s - top)
                p = e * (1.0 / jnp.sum(e, axis=-1, keepdims=True))
                probs_ref[0, 0, h, b * blk + r : b * blk + r + TILE, :] = p
                lows.append(p.astype(BF))
        c = dot(jnp.concatenate(lows, axis=0), values_ref[0])
        total = c[0:blk]
        for h in range(1, GH):
            total = jnp.where(masks[h], c[h * blk : (h + 1) * blk], total)
        ctx_ref[0, rows, :] = total.astype(BF)


def attend(start, stop, hidden, pooled_low, weights, table, bias, held=None):
    B, L, D = hidden.shape
    R = L // 2
    G = D // GC
    g = lambda i: (start + i) // B
    s = lambda i: lax.rem(start + i, B)
    seq = lambda r: pl.BlockSpec((1, r, D), lambda i: (s(i), 0, 0))
    mat = lambda base: pl.BlockSpec((1, D, GC), lambda i: (base + g(i), 0, 0))
    so = lambda r: pl.BlockSpec((1, r, GC), lambda i: (s(i), 0, g(i)))
    a, b = weights
    ins = [hidden, pooled_low, a, a, b, b, table, a, bias]
    specs = [seq(L), seq(R), mat(0), mat(G), mat(0), mat(G), whole(2 * L, D),
             pl.BlockSpec((1, GC, GC), lambda i: (2 * G, g(i), 0)), pl.BlockSpec((1, 1, L), lambda i: (s(i), 0, 0))]
    aliases = {}
    if held is not None:
        aliases = {len(ins) + i: i for i in range(7)}
        ins += list(held)
        specs += [pl.BlockSpec(memory_space=pl.ANY)] * 7
    return pl.pallas_call(
        functools.partial(attend_kernel, start, B),
        grid=(stop - start,),
        in_specs=specs,
        out_specs=[so(R), pl.BlockSpec((1, 1, GH, R, L), lambda i: (s(i), g(i), 0, 0, 0)), so(R), so(R), so(L), so(L),
                   pl.BlockSpec((2 * L, GC), lambda i: (0, g(i)))],
        out_shape=[sds((B, R, D), BF), sds((B, G, GH, R, L), F32), sds((B, R, D), BF), sds((B, R, D), BF),
                   sds((B, L, D), BF), sds((B, L, D), BF), sds((2 * L, D), BF)],
        scratch_shapes=[pltpu.VMEM((2 * L, GC), BF)],
        input_output_aliases=aliases,
        cost_estimate=cost(4 * (stop - start)),
        compiler_params=params(58),
    )(*ins)


def phi_and_slope(z):
    e = jnp.exp(z * z * (-0.5))
    t = 1.0 / (1.0 + (0.3275911 * 0.7071067811865476) * jnp.abs(z))
    poly = t * (0.127414796 + t * (-0.142248368 + t * (0.7107068705 + t * (-0.7265760135 + t * 0.5307027145))))
    tail = poly * e
    phi = jnp.where(z >= 0, 1.0 - tail, tail)
    return phi, phi + z * e * 0.3989422804014327


def norm(x):
    center = x - jnp.mean(x, axis=-1, keepdims=True)
    inv = lax.rsqrt(jnp.mean(center * center, axis=-1, keepdims=True) + EPSILON)
    return center * inv, inv


def norm_back(e, n, inv):
    return inv * (e - jnp.mean(e, axis=-1, keepdims=True) - n * jnp.mean(e * n, axis=-1, keepdims=True))


def add_rows(ref, *values):
    for k, v in enumerate(values):
        ref[k : k + 1, :] += jnp.sum(v, axis=0, keepdims=True)


def mlp_kernel(dealt, *refs):
    me_ref, ctx_ref, pooled_ref, cot_ref, mask_ref, exp_ref, w2_ref, turned_ref = refs[:8]
    out_ref, y1_ref, n1_ref, s1_ref, slope_ref, dx2_ref, e2_ref, sums_ref = refs[8:16]
    grads, (small_ref, inner_ref, e2_all, total) = refs[16:-4], refs[-4:]
    rows_here = pooled_ref.shape[1]
    mine = pl.ds(pl.multiple_of(pl.program_id(0) * rows_here, 16), rows_here)
    @pl.when(pl.program_id(0) == 0)
    def _():
        sums_ref[...] = jnp.zeros_like(sums_ref)
        small_ref[...] = turned_ref[0, :, 0:128].astype(F32).T

    row = lambda k: small_ref[k : k + 1, :]
    chunks = exp_ref.shape[0] - 1
    x1 = pooled_ref[0] + dot(ctx_ref[0], exp_ref[chunks]) + row(3)
    n1, inv1 = norm(x1)
    n1_ref[0] = n1
    s1_ref[0] = inv1
    y1 = n1 * row(4) + row(5)
    y1l = y1.astype(BF)
    y1_ref[0] = y1l
    x2 = y1 + row(6)
    for c in range(chunks):
        cs = slice(c * FC, (c + 1) * FC)
        z = dot(y1l, exp_ref[c]) + row(9 + c)
        phi, slope = phi_and_slope(z)
        inner = (z * phi).astype(BF)
        inner_ref[mine, cs] = inner
        slope_ref[0, :, cs] = slope
        x2 += dot(inner, w2_ref[cs, :])
    n2, inv2 = norm(x2)
    m = mask_ref[0]
    out_ref[0] = ((n2 * row(7) + row(8)) * m).astype(BF)
    dy2 = cot_ref[0].astype(F32) * m
    dx2 = norm_back(dy2 * row(7), n2, inv2)
    dx2_ref[0] = dx2
    e2 = dx2.astype(BF)
    e2_ref[0] = e2
    add_rows(sums_ref, dx2, dy2 * n2, dy2)
    e2_all[mine, :] = e2

    @pl.when(pl.program_id(0) == pl.num_programs(0) - 1)
    def _():
        for c in range(chunks):
            cs = slice(c * FC, (c + 1) * FC)
            v = dot_tn(inner_ref[:, cs], e2_all[...])
            if not dealt:
                grads[0][cs, :] = v
            else:
                total[cs, :] = v
        if dealt:
            r = grads[0].shape[2]
            for half in range(2):
                for rel in range(32):
                    k = jnp.bitwise_xor(me_ref[0], flat_of(rel, half))
                    at = pl.multiple_of(k * (2 * r) + half * r, 8)
                    grads[2 * half + rel // 16][rel % 16, 0] = total[pl.ds(at, r), :].astype(BF)


def mlp(me, ctx, pooled, cot, mask, expand, w2, small, dealt):
    B, R, D = pooled.shape
    F = w2.shape[0]
    grads = [sds((16, 1, F // 64, D), BF)] * 4 if dealt else [sds((F, D), F32)]
    return pl.pallas_call(
        functools.partial(mlp_kernel, dealt),
        grid=(B,),
        in_specs=[pl.BlockSpec(memory_space=pltpu.SMEM), seqs(R, D), seqs(R, D), seqs(R, D), seqs(R, 1), whole(*expand.shape), whole(F, D),
                  turned_small(D)],
        out_specs=[seqs(R, D), seqs(R, D), seqs(R, D), seqs(R, 1), seqs(R, F), seqs(R, D), seqs(R, D),
                   pl.BlockSpec((8, D), lambda s: (0, 0))] + [whole(*g.shape) for g in grads],
        out_shape=[sds((B, R, D), BF), sds((B, R, D), BF), sds((B, R, D), F32), sds((B, R, 1), F32),
                   sds((B, R, F), F32), sds((B, R, D), F32), sds((B, R, D), BF), sds((8, D), F32)] + grads,
        scratch_shapes=[pltpu.VMEM((128, D), F32), pltpu.VMEM((B * R, F), BF), pltpu.VMEM((B * R, D), BF), pltpu.VMEM((F, D), F32)],
        cost_estimate=cost(38),
        compiler_params=params(58),
    )(me, ctx, pooled, cot, mask, expand, w2, small)


def mlp_back_kernel(dx2_ref, e2_ref, slope_ref, n1_ref, s1_ref, exp_ref, w2_ref, turned_ref,
                    e1_ref, dx1_ref, ea_ref, dctx_ref, sums_ref, db1_ref, small_ref):
    @pl.when(pl.program_id(0) == 0)
    def _():
        small_ref[...] = turned_ref[0, :, 0:128].astype(F32).T
        sums_ref[...] = jnp.zeros_like(sums_ref)
        db1_ref[...] = jnp.zeros_like(db1_ref)

    chunks = exp_ref.shape[0] - 1
    e2 = e2_ref[0]
    dy1 = dx2_ref[0]
    for c in range(chunks):
        cs = slice(c * FC, (c + 1) * FC)
        dz = dot_nt(e2, w2_ref[cs, :]) * slope_ref[0, :, cs]
        db1_ref[:, cs] += jnp.sum(dz, axis=0, keepdims=True)
        e1 = dz.astype(BF)
        e1_ref[0, :, cs] = e1
        dy1 += dot_nt(e1, exp_ref[c])
    n1 = n1_ref[0]
    dx1 = norm_back(dy1 * small_ref[4:5, :], n1, s1_ref[0])
    dx1_ref[0] = dx1
    ea = dx1.astype(BF)
    ea_ref[0] = ea
    dctx_ref[0] = dot_nt(ea, exp_ref[chunks]).astype(BF)
    add_rows(sums_ref, dx1, dy1 * n1, dy1)


def mlp_back(dx2, e2, slope, n1, s1, expand, w2, small):
    B, R, D = dx2.shape
    F = w2.shape[0]
    return pl.pallas_call(
        mlp_back_kernel,
        grid=(B,),
        in_specs=[seqs(R, D), seqs(R, D), seqs(R, F), seqs(R, D), seqs(R, 1), whole(*expand.shape), whole(F, D),
                  turned_small(D)],
        out_specs=[seqs(R, F), seqs(R, D), seqs(R, D), seqs(R, D), pl.BlockSpec((8, D), lambda s: (0, 0)),
                   pl.BlockSpec((1, F), lambda s: (0, 0))],
        out_shape=[sds((B, R, F), BF), sds((B, R, D), F32), sds((B, R, D), BF), sds((B, R, D), BF), sds((8, D), F32),
                   sds((1, F), F32)],
        scratch_shapes=[pltpu.VMEM((128, D), F32)],
        cost_estimate=cost(21),
        compiler_params=params(58),
    )(dx2, e2, slope, n1, s1, expand, w2, small)


def deal(half, me, total_ref, put):
    r = total_ref.shape[0] // 32
    for rel in range(32):
        k = jnp.bitwise_xor(me, flat_of(rel, half))
        put(rel // 16, rel % 16, total_ref[pl.ds(pl.multiple_of(k * r, 8), r), :].astype(BF))


def outer_kernel(half, me_ref, a_ref, b_ref, keep_ref, send_ref, turned, total):
    B, R, M = a_ref.shape

    @pl.when(pl.program_id(0) == 0)
    def _():
        turned[...] = a_ref[...].reshape(B * R, M).T

    total[...] = dot(turned[...], b_ref[...].reshape(B * R, b_ref.shape[2]))

    def put(sent, i, v):
        for j in range(v.shape[1] // GC):
            (send_ref if sent else keep_ref)[i, j] = v[:, j * GC : (j + 1) * GC]

    deal(half, me_ref[0], total, put)


def outer_plain_kernel(a_ref, b_ref, out_ref):
    B, R, M = a_ref.shape
    out_ref[...] = dot_tn(a_ref[...].reshape(B * R, M), b_ref[...].reshape(B * R, b_ref.shape[2]))


def outer(me, a, b, cols, half=None, blocks=None):
    B, R, M = a.shape
    N = b.shape[2]
    first, count = blocks or (0, N // cols)
    specs = [pl.BlockSpec((B, R, M), lambda j: (0, 0, 0)), pl.BlockSpec((B, R, cols), lambda j: (0, 0, first + j))]
    price = cost(2.0 * count)
    if half is None:
        return pl.pallas_call(
            outer_plain_kernel, grid=(count,), in_specs=specs,
            out_specs=pl.BlockSpec((M, cols), lambda j: (0, j)),
            out_shape=sds((M, N), F32), cost_estimate=price, compiler_params=params(32))(a, b)
    return pl.pallas_call(
        functools.partial(outer_kernel, half),
        grid=(count,),
        in_specs=[pl.BlockSpec(memory_space=pltpu.SMEM)] + specs,
        out_specs=[pl.BlockSpec((16, cols // GC, M // 32, GC), lambda j: (0, j, 0, 0))] * 2,
        out_shape=[sds((16, count * cols // GC, M // 32, GC), BF)] * 2,
        scratch_shapes=[pltpu.VMEM((M, B * R), BF), pltpu.VMEM((M, cols), F32)],
        cost_estimate=price,
        compiler_params=params(32),
    )(me, a, b)


def wide_outer_kernel(chunks, me_ref, y1_ref, e1_ref, ctx_ref, ea_ref, keep0, send0, keep1, send1, turned, total):
    B, R, D = y1_ref.shape
    j = pl.program_id(0)
    flat = lambda ref: ref[...].reshape(B * R, D)

    def dealt(half, base):
        def put(sent, i, v):
            ref = ((keep0, send0), (keep1, send1))[half][sent]
            for b in range(D // GC):
                ref[i, base + b] = v[:, b * GC : (b + 1) * GC]

        deal(half, me_ref[0], total, put)

    @pl.when(j == 0)
    def _():
        turned[...] = flat(y1_ref).T

    @pl.when(j < chunks)
    def _():
        total[...] = dot(turned[...], flat(e1_ref))

    @pl.when(j == chunks)
    def _():
        total[...] = dot_tn(flat(ctx_ref), flat(ea_ref))
        dealt(0, chunks // 2 * (D // GC))

    @pl.when(j < chunks // 2)
    def _():
        dealt(0, j * (D // GC))

    @pl.when((j >= chunks // 2) & (j < chunks))
    def _():
        dealt(1, (j - chunks // 2) * (D // GC))


def wide_outer(me, y1, e1, ctx, ea):
    B, R, D = y1.shape
    F = e1.shape[2]
    chunks = F // D
    n = D // GC
    shapes = [(16, m, D // 32, GC) for m in (chunks // 2 * n + n, chunks // 2 * n) for _ in range(2)]
    out = pl.pallas_call(
        functools.partial(wide_outer_kernel, chunks),
        grid=(chunks + 1,),
        in_specs=[pl.BlockSpec(memory_space=pltpu.SMEM), whole(B, R, D),
                  pl.BlockSpec((B, R, D), lambda j: (0, 0, jnp.minimum(j, chunks - 1))), whole(B, R, D), whole(B, R, D)],
        out_specs=[whole(*shape) for shape in shapes],
        out_shape=[sds(shape, BF) for shape in shapes],
        scratch_shapes=[pltpu.VMEM((D, B * R), BF), pltpu.VMEM((D, D), F32)],
        cost_estimate=cost(12),
        compiler_params=params(40),
    )(me, y1, e1, ctx, ea)
    return tuple(out[:2]), tuple(out[2:])


def small_deal_kernel(me_ref, *refs):
    sums, (sums1, sums2, db1, keep_ref, send_ref, total, turned) = refs[:-7], refs[-7:]
    D = sums1.shape[1]
    total[...] = jnp.zeros_like(total)
    for g, s in enumerate(sums):
        total[0:3, g * GC : (g + 1) * GC] = s[0:3, :]
    total[3:6, :] = sums1[0:3, :]
    total[6:9, :] = sums2[0:3, :]
    for i in range(db1.shape[1] // D):
        total[9 + i : 10 + i, :] = db1[0:1, i * D : (i + 1) * D]
    turned[...] = jnp.concatenate([total[...].T, jnp.zeros((D, GC - total.shape[0]), F32)], axis=1)

    def put(sent, i, v):
        (send_ref if sent else keep_ref)[i, 0] = v

    deal(0, me_ref[0], turned, put)


def small_deal(me, sums, sums1, sums2, db1):
    D = sums1.shape[1]
    n = 4 + len(sums)
    return pl.pallas_call(
        small_deal_kernel,
        in_specs=[pl.BlockSpec(memory_space=pltpu.SMEM)] + [pl.BlockSpec(memory_space=pltpu.VMEM)] * (n - 1),
        out_specs=[pl.BlockSpec(memory_space=pltpu.VMEM)] * 2,
        out_shape=[sds((16, 1, D // 32, GC), BF)] * 2,
        scratch_shapes=[pltpu.VMEM((128, D), F32), pltpu.VMEM((D, GC), F32)],
        cost_estimate=cost(2),
        compiler_params=params(24),
    )(me, *sums, sums1, sums2, db1)


def attend_back_kernel(plan, *refs):
    (me_ref, probs_ref, dctx_ref, qu_ref, qw_ref, keys_ref, values_ref, rel_ref, hidt_ref, lowt_ref, tablet_ref) = refs[:11]
    outs = refs[11 : 14]
    dq_ref, dk_ref, dv_ref = outs
    grads = refs[14 : -8]
    sums_ref = refs[-8]
    acc_q, acc_k, acc_v, acc_r, acc_dv, dkt, dvt = refs[-7:]
    step = pl.program_id(0)
    half, L = probs_ref.shape[3], probs_ref.shape[4]
    blk = half // 2

    @pl.when(step == 0)
    def _():
        for a in (acc_q, acc_k, acc_v, acc_r, acc_dv, sums_ref):
            a[...] = jnp.zeros_like(a)

    across = lax.broadcasted_iota(jnp.int32, (half, half), 0) + lax.broadcasted_iota(jnp.int32, (half, half), 1)
    flip = (across == half - 1).astype(F32).astype(BF)
    lane = lax.broadcasted_iota(jnp.int32, (1, GC), 1)
    dctx = dctx_ref[0]
    dctx_t = dctx.T
    qu_t = qu_ref[0].T
    qwr_t = dot(flip, qw_ref[0]).astype(BF).T
    keys = keys_ref[0]
    values = values_ref[0]
    masks = [(lane >= h * HEAD) & (lane < (h + 1) * HEAD) for h in range(GH)]
    dctx_wide = dctx.astype(F32)
    dp = dot_nt(jnp.concatenate([jnp.where(m, dctx_wide, 0.0).astype(BF) for m in masks], axis=0), values)
    backs = []
    moved = [[], []]
    for h in range(GH):
        sel = slice(h * HEAD, (h + 1) * HEAD)
        draws, lows = [], []
        for r in range(0, half, TILE):
            p = probs_ref[0, 0, h, r : r + TILE, :]
            t = p * dp[h * half + r : h * half + r + TILE]
            draws.append((t - p * jnp.sum(t, axis=-1, keepdims=True)).astype(BF))
            lows.append(p.astype(BF))
        draw = jnp.concatenate(draws, axis=0)
        dvt[sel, :] = dot(dctx_t[sel], jnp.concatenate(lows, axis=0))
        both = dot(jnp.concatenate([qu_t[sel], flip], axis=0), draw)
        dkt[sel, :] = both[:HEAD] * 0.125
        back = both[HEAD:]
        backs.append(back.astype(BF))
        for b in range(2):
            tiles = []
            for r in range(0, blk, TILE):
                x = jnp.concatenate([back[b * blk + r : b * blk + r + TILE], jnp.zeros((TILE, 128), F32)], axis=1)
                x = pltpu.roll(x, 2 + 2 * r % 128, 1, stride=2, stride_axis=0).astype(BF)
                none = jnp.zeros((TILE, 128), BF)
                tiles.append(jnp.concatenate([x, none] if r < blk // 2 else [none, x], axis=1))
            x = jnp.concatenate(tiles, axis=0)
            m0 = half * b
            acc_r[sel, m0 : m0 + 3 * half] += dot(qwr_t[sel, b * blk : (b + 1) * blk], x)
            moved[b].append(x)
    alone = lambda v, n: functools.reduce(lambda t, h: jnp.where(masks[h], v[h * n : (h + 1) * n], t), range(1, GH), v[0:n])
    dqu = alone(dot(jnp.concatenate(backs, axis=0), keys), half)
    dqw = jnp.concatenate(
        [alone(dot(jnp.concatenate(moved[b], axis=0), rel_ref[half * b : half * b + 3 * half, :]), blk) for b in range(2)], axis=0
    )
    dqu = dqu * 0.125
    dqw = dqw * 0.125
    dq = dot(flip, (dqu + dqw).astype(BF)).astype(BF)
    dk = dkt[...].astype(BF).T
    dvf = dvt[...]
    dv = dvf.astype(BF).T
    dq_ref[0] = dq
    dk_ref[0] = dk
    dv_ref[0] = dv
    acc_dv[...] += dvf
    add_rows(sums_ref, dqu, dqw)
    acc_q[...] += dot(lowt_ref[0], dq)
    acc_k[...] += dot(hidt_ref[0], dk)
    acc_v[...] += dot(hidt_ref[0], dv)

    @pl.when(step == pl.num_programs(0) - 1)
    def _():
        sums_ref[2:3, :] = jnp.sum(acc_dv[...].T, axis=0, keepdims=True)
        dr = acc_r[...] * 0.125
        hi = dr.astype(BF)
        lo = (dr - hi.astype(F32)).astype(BF)
        tt = tablet_ref[...]
        if plan is None:
            for i, a in enumerate((acc_q, acc_k, acc_v)):
                grads[0][i] = a[...]
            grads[0][3] = dot_nt(tt, hi) + dot_nt(tt, lo)
        else:
            for i in range(4):
                half = plan[i]
                at = plan[:i].count(half)
                base = 2 * sorted(set(plan)).index(half)
                acc = (acc_q, acc_k, acc_v, acc_q)[i]
                if i == 3:
                    acc_q[...] = dot_nt(tt, hi) + dot_nt(tt, lo)

                def put(sent, j, v):
                    grads[base + sent][j, at] = v

                deal(half, me_ref[0], acc, put)


def attend_back(me, g, probs, dctx, qu, qw, keys, values, rel, hid_t, low_t, table_t, plan=None):
    B, R, D = qu.shape
    L = 2 * R
    so = lambda r: pl.BlockSpec((1, r, GC), lambda s: (s, 0, g))
    if plan is None:
        grad_specs = [pl.BlockSpec((4, D, GC), lambda s: (0, 0, 0))]
        grad_shapes = [sds((4, D, GC), F32)]
    else:
        sizes = [(16, plan.count(h), D // 32, GC) for h in sorted(set(plan)) for _ in range(2)]
        grad_specs = [whole(*size) for size in sizes]
        grad_shapes = [sds(size, BF) for size in sizes]
    return pl.pallas_call(
        functools.partial(attend_back_kernel, plan),
        grid=(B,),
        in_specs=[pl.BlockSpec(memory_space=pltpu.SMEM),
                  pl.BlockSpec((1, 1, GH, R, L), lambda s: (s, g, 0, 0, 0)), so(R), so(R), so(R), so(L), so(L),
                  pl.BlockSpec((2 * L, GC), lambda s: (0, g)), seqs(D, L), seqs(D, R), whole(D, 2 * L)],
        out_specs=[seqs(R, GC), seqs(L, GC), seqs(L, GC)] + grad_specs + [pl.BlockSpec((8, GC), lambda s: (0, 0))],
        out_shape=[sds((B, R, GC), BF), sds((B, L, GC), BF), sds((B, L, GC), BF)] + grad_shapes + [sds((8, GC), F32)],
        scratch_shapes=[pltpu.VMEM((D, GC), F32)] * 3 + [pltpu.VMEM((GC, 2 * L), F32)] + [pltpu.VMEM((GC, L), F32)] * 3,
        cost_estimate=cost(22),
        compiler_params=params(48),
    )(me, probs, dctx, qu, qw, keys, values, rel, hid_t, low_t, table_t)


def input_grad_kernel(at, *refs):
    groups = len(at)
    dqs, dks, dvs = refs[:groups], refs[groups : 2 * groups], refs[2 * groups : 3 * groups]
    dx1_ref, weights, out_ref, wide = refs[3 * groups], refs[3 * groups + 1 : -2], refs[-2], refs[-1]
    half = dx1_ref.shape[1]
    shared = dx1_ref[0]
    total = None
    for g in range(groups):
        wq, wk, wv = (weights[a][i] for a, i in at[g])
        shared += dot_nt(dqs[g][0], wq)
        t = dot_nt(dks[g][0], wk) + dot_nt(dvs[g][0], wv)
        total = t if total is None else total + t
    shared = shared * 0.5
    for i in range(wide.shape[0]):
        cs = slice(i * 128, (i + 1) * 128)
        wide[i, pl.ds(0, half, stride=2), :] = shared[:, cs]
        wide[i, pl.ds(1, half, stride=2), :] = shared[:, cs]
        out_ref[0, :, cs] = (total[:, cs] + wide[i]).astype(BF)


def input_grad(dqs, dks, dvs, dx1, weights, at):
    B, R, D = dx1.shape
    L = 2 * R
    G = len(dqs)
    return pl.pallas_call(
        functools.partial(input_grad_kernel, at),
        grid=(B,),
        in_specs=[seqs(R, GC)] * G + [seqs(L, GC)] * (2 * G) + [seqs(R, D)] + [whole(*w.shape) for w in weights],
        out_specs=seqs(L, D),
        out_shape=sds((B, L, D), BF),
        scratch_shapes=[pltpu.VMEM((D // 128, L, 128), F32)],
        cost_estimate=cost(10),
        compiler_params=params(40),
    )(*dqs, *dks, *dvs, dx1, *weights)


def adamw(weight, moment, second, gradient, rates):
    new_moment = rates[1] * moment + (1.0 - rates[1]) * gradient
    new_second = rates[2] * second + (1.0 - rates[2]) * gradient * gradient
    moment_hat = new_moment / rates[4]
    second_hat = new_second / rates[5]
    new_weight = weight - rates[0] * (moment_hat / (jnp.sqrt(second_hat) + 1e-08) + rates[3] * weight)
    return (new_weight, new_moment, new_second)


def update_kernel(plan, rates_ref, w_ref, m_ref, v_ref, *refs):
    terms, (grad_ref, w_out, m_out, v_out) = refs[:-4], refs[-4:]
    rates = [rates_ref[i] for i in range(6)]
    for first, count, block, dest in plan:
        g = None
        for t in terms[first : first + count]:
            v = (t[...] if block is None else t[block]).astype(F32)
            g = v if g is None else g + v
        grad_ref[dest] = g
        w_out[dest], m_out[dest], v_out[dest] = adamw(w_ref[dest], m_ref[dest], v_ref[dest], g, rates)


def update(rates, w, m, v, terms, plan=None):
    plan = plan or [(0, len(terms), None, (slice(None),) * w.ndim)]
    return pl.pallas_call(
        functools.partial(update_kernel, plan),
        in_specs=[pl.BlockSpec(memory_space=pltpu.SMEM)] + [pl.BlockSpec(memory_space=pltpu.VMEM)] * (3 + len(terms)),
        out_specs=[pl.BlockSpec(memory_space=pltpu.VMEM)] * 4,
        out_shape=[sds(w.shape, F32)] * 4,
        cost_estimate=cost(2),
        compiler_params=params(24),
    )(rates, w, m, v, *terms)


def last_update_kernel(plan, small_at, rates_ref, *refs):
    ins, (pad, *_) = refs[:-9], refs[-1:]
    att, small, terms = ins[:3], ins[3:6], ins[6:]
    outs = refs[-9:-1]
    update_kernel(plan, rates_ref, *att, *terms, *outs[:4])
    first, count, block = small_at
    g = sum(t[block].astype(F32) for t in terms[first : first + count])
    V, r = small[0].shape
    pad[...] = jnp.zeros_like(pad)
    pad[0:r, :] = g[:, 0:128]
    pad[...] = pad[...].T
    rates = [rates_ref[i] for i in range(6)]
    g = pad[0:V, 0:r]
    outs[4][...] = g
    outs[5][...], outs[6][...], outs[7][...] = adamw(small[0][...], small[1][...], small[2][...], g, rates)


def last_update(rates, attention, small, terms, plan, small_at):
    like = [attention[0]] * 4 + [small[0]] * 4
    out = pl.pallas_call(
        functools.partial(last_update_kernel, plan, small_at),
        in_specs=[pl.BlockSpec(memory_space=pltpu.SMEM)] + [pl.BlockSpec(memory_space=pltpu.VMEM)] * (6 + len(terms)),
        out_specs=[pl.BlockSpec(memory_space=pltpu.VMEM)] * 8,
        out_shape=[sds(a.shape, F32) for a in like],
        scratch_shapes=[pltpu.VMEM((128, 128), F32)],
        cost_estimate=cost(3),
        compiler_params=params(24),
    )(rates, *attention, *small, *terms)
    return out[:4], out[4:]


def shards(fast, hidden, lengths, key_mask, cotangent, attention_weight, expand_weight, contract_weight, small_params,
           mean_attention, mean_expand, mean_contract, mean_small,
           square_attention, square_expand, square_contract, square_small, update_step, update_rates):
    B, L, D = hidden.shape
    R = L // 2
    F = expand_weight.shape[1]
    G = D // GC
    C = F // FC
    H = C // 2
    r = attention_weight.shape[1]
    V = small_params.shape[0]
    me = (lax.axis_index("dp") * lax.axis_size("fsdp") + lax.axis_index("fsdp")).astype(jnp.int32).reshape(1)

    table = rel_table(L, D)
    table, table_t = jnp.asarray(table), jnp.asarray(np.ascontiguousarray(table.T))

    def correction():
        return jnp.concatenate([update_rates, 1.0 - jnp.power(update_rates[1:3], update_step[0].astype(F32))])

    at = tuple(((0, g), (0, G + g), (1, g)) for g in range(G))
    if fast:
        first, third = parcel(attention_weight, expand_weight, contract_weight, small_params)
        gate1 = Gather(me, first, 2 * G + 1)
        gate1.far(1, 2, 3)
        pooled, pooled_low, hid_t, low_t, bias, mask = prepare(hidden, lengths, key_mask)
        rates = correction()
        token = gate1.plane(pooled_low, rates)
        gate2 = Gather(me, third, C + 1, (True, False))
        near = (gate2.far(1, then=token), gate2.far(2, then=token))
        token = gate1.plane_again(near)
        last = gate2.far(3, then=token)
        token = gate1.cores(last)
        token = gate2.plane(token)
        weights = gate1.result()
        low = after(pooled_low, token)
        steps = B * G
        stops = (steps // 6, 3 * steps // 4, steps)
        held = attend(0, stops[0], hidden, low, weights, table, bias)
        low = after(low, gate2.plane_again(held[0]))
        held = attend(stops[0], stops[1], hidden, low, weights, table, bias, held)
        low = after(low, gate2.cores(held[0]))
        held = attend(stops[1], stops[2], hidden, low, weights, table, bias, held)
        w_eo, w2 = gate2.result(held[0])
    else:
        cut = lambda a, c: a.astype(BF).reshape(r, -1, c).transpose(1, 0, 2)
        small_t = jnp.pad(small_params.T, ((0, 0), (0, GC - V))).astype(BF)[None]
        cols = [cut(attention_weight[i], GC) for i in range(4)]
        full = lambda a: lax.all_gather(a, ALL, axis=1, tiled=True)
        first = full(jnp.concatenate(cols[:2] + [small_t] + cols[2:], axis=0))
        w_eo = full(jnp.concatenate([cut(expand_weight, FC), cut(attention_weight[4], FC)], axis=0))
        w2 = lax.all_gather(contract_weight.astype(BF), ALL, axis=0, tiled=True)
        weights = (first[: 2 * G + 1], first[2 * G + 1 :])
        pooled, pooled_low, hid_t, low_t, bias, mask = prepare(hidden, lengths, key_mask)
        rates = correction()
        held = attend(0, B * G, hidden, pooled_low, weights, table, bias)
    ctx, probs, qu, qw, keys, values, rel = held
    small = weights[0]
    out, y1, n1, s1, slope, dx2, e2, sums2, *d_contract = mlp(me, ctx, pooled, cotangent, mask, w_eo, w2, small, fast)

    def backward(g, dctx, plan=None):
        return attend_back(me, g, probs, dctx, qu, qw, keys, values, rel, hid_t, low_t, table_t, plan)

    def hidden_grad(back, dx1):
        return input_grad([b[0] for b in back], [b[1] for b in back], [b[2] for b in back], dx1, weights, at)

    if not fast:
        scatter = lambda a, d: lax.psum_scatter(a, ALL, scatter_dimension=d, tiled=True)
        e1, dx1, ea, dctx, sums1, db1 = mlp_back(dx2, e2, slope, n1, s1, w_eo, w2, small)
        back = [backward(g, dctx) for g in range(G)]
        in_grad = hidden_grad(back, dx1)
        d_att = jnp.concatenate([b[3] for b in back], axis=2)
        d_att = jnp.concatenate([d_att, outer(me, ctx, ea, 384)[None]], axis=0)
        d_small = jnp.concatenate([b[-1][0:3] for b in back], axis=1)
        d_small = jnp.concatenate([d_small, sums1[0:3], sums2[0:3], db1.reshape(-1, D)], axis=0)
        attention_terms, attention_plan = [scatter(d_att, 1)], None
        expand_terms, expand_plan = [scatter(outer(me, y1, e1, FC), 0)], None
        contract_terms = [scatter(d_contract[0], 0)]
        contract_up = update(rates, contract_weight, mean_contract, square_contract, contract_terms)
        small_grad = scatter(d_small, 1)
    else:
        half0, half1 = tuple(d_contract[:2]), tuple(d_contract[2:])
        sum1 = Reduction([half0], [half1])
        e1, dx1, ea, dctx, sums1, db1 = mlp_back(dx2, e2, slope, n1, s1, w_eo, w2, small)
        sum1.cross(e1)
        wide0, wide1 = wide_outer(me, after(y1, sum1.token), e1, ctx, ea)
        sum1.cross(wide0)
        wide0, wide1 = after((wide0, wide1), sum1.token)
        sum2 = Reduction([wide0], [wide1])
        sum2.cross()
        back = [backward(0, after(dctx, sum1.token, sum2.token), (0, 0, 0, 0))]
        sum2.cross(back[0][0])
        sum1.along(sum2.token)
        back.append(backward(1, after(dctx, sum1.token, sum2.token), (1, 1, 1, 1)))
        sum2.along(back[1][0])
        every = slice(None)
        r2 = contract_weight.shape[0] // 2
        contract_plan = [(0, 4, i, (slice(i * r2, (i + 1) * r2), every)) for i in range(2)]
        contract_terms = after(sum1.terms, sum2.token)
        contract_up = update(rates, contract_weight, mean_contract, square_contract, contract_terms, contract_plan)
        grads0, grads1 = after((tuple(back[0][3:5]), tuple(back[1][3:5])), contract_up[0])
        sum3 = Reduction([grads0], [grads1])
        sum3.cross()
        back.append(backward(2, after(dctx, sum3.token), (0, 0, 1, 1)))
        terms2 = settle(after(sum2.terms, back[2][0]))
        sum3.cross(terms2)
        d_small = small_deal(me, [b[-1] for b in back], sums1, sums2, after(db1, sum3.token))
        sum4 = Reduction([tuple(back[2][3:5]), tuple(d_small)], [tuple(back[2][5:7])])
        sum4.cross()
        sum3.along(sum4.token)
        sum4.cross(sum3.token)
        expand_weight, dx1 = after((expand_weight, dx1), sum4.token)
        in_grad = hidden_grad(back, dx1)
        terms3 = settle(after(sum3.terms, in_grad))
        sum4.along(terms3)
        expand_terms = [terms2]
        per = F // GC // 2
        narrow = lambda j: slice(j * GC, (j + 1) * GC)
        expand_plan = [(0, 1, j + (G if j >= per else 0), (every, narrow(j))) for j in range(2 * per)]
        attention_terms = [terms2, terms3] + sum4.terms
        attention_plan = [(0, 1, per + j, (4, every, narrow(j))) for j in range(G)]
        attention_plan += [(1, 1, 4 * g + m, (m, every, narrow(g))) for g in range(2) for m in range(4)]
        attention_plan += [(2, 4, m + (m > 1), (m, every, narrow(2))) for m in range(4)]
        attention_up, small_up = last_update(
            rates, (attention_weight, mean_attention, square_attention), (small_params, mean_small, square_small),
            attention_terms, attention_plan, (2, 4, 2))
    expand_up = update(rates, expand_weight, mean_expand, square_expand, expand_terms, expand_plan)
    if not fast:
        attention_up = update(rates, attention_weight, mean_attention, square_attention, attention_terms, attention_plan)
        small_up = update(rates, small_params, mean_small, square_small, [small_grad])
    ups = (attention_up, expand_up, contract_up, small_up)
    return (out, in_grad) + tuple(u[i] for i in range(4) for u in ups)


def solution(mesh):
    outer_rows = P(ALL, None)
    middle = P(None, ALL, None)
    inner_cols = P(None, ALL)
    table = (middle, outer_rows, outer_rows, inner_cols)
    tokens = P(ALL, None, None)
    in_specs = (tokens, P(ALL), outer_rows, tokens) + table * 3 + (P(), P())
    out_specs = (tokens, tokens) + table * 4
    fast = mesh.shape["dp"] == 8 and mesh.shape["fsdp"] == 4
    return jax.shard_map(
        functools.partial(shards, fast), mesh=mesh, in_specs=in_specs, out_specs=out_specs, check_vma=False
    )
```

```python
import functools
import math

import jax
import jax.numpy as jnp
import ml_dtypes
import numpy as np
from jax import lax
from jax.experimental import pallas as pl
from jax.experimental.pallas import tpu as pltpu
from jax.sharding import PartitionSpec as P

HEAD = 64
GC = 256
GH = GC // HEAD
TILE = 16
FC = 768
EPSILON = 1e-06
MASK_FILL = -1000000000.0
ALL = ("dp", "fsdp")
F32 = jnp.float32
BF = jnp.bfloat16
NT = (((1,), (1,)), ((), ()))
TN = (((0,), (0,)), ((), ()))


def dot(a, b):
    return jnp.dot(a, b, preferred_element_type=F32)


def dot_nt(a, b):
    return lax.dot_general(a, b, NT, preferred_element_type=F32)


def dot_tn(a, b):
    return lax.dot_general(a, b, TN, preferred_element_type=F32)


def sds(shape, dtype):
    return jax.ShapeDtypeStruct(shape, dtype)


def seqs(*tail):
    return pl.BlockSpec((1,) + tail, lambda s, *_: (s,) + (0,) * len(tail))


def whole(*shape):
    return pl.BlockSpec(shape, lambda *_: (0,) * len(shape), pipeline_mode=pl.Buffered(1))


def turned_small(width):
    return pl.BlockSpec((1, width, GC), lambda s: (2 * width // GC, 0, 0), pipeline_mode=pl.Buffered(1))


def params(mib):
    return pltpu.CompilerParams(vmem_limit_bytes=mib << 20)


def cost(us):
    return pl.CostEstimate(flops=int(us * 1.1e9), bytes_accessed=int(us * 3.5e6), transcendentals=0)


def rel_table(length, width):
    places = length - np.arange(2 * length, dtype=np.float32)
    half_width = width // 2
    frequency = np.exp(np.arange(half_width, dtype=np.float32) * np.float32(-2.0 * math.log(10000.0) / width))
    angles = places[:, None] * frequency[None, :]
    return np.concatenate([np.sin(angles), np.cos(angles)], axis=1).astype(ml_dtypes.bfloat16)


X, Y, CORE, Z = 1, 2, 4, 8
HALVES = ((X, Y), (Y, X))


def pairs(bit):
    return [(d, d ^ bit) for d in range(32)]


def swap(a, bit):
    return lax.ppermute(a, ALL, pairs(bit))


def flat_of(rel, half):
    low, high = HALVES[half]
    return (rel & 3) * Z + (rel >> 2 & 1) * low + (rel >> 3 & 1) * high + (rel >> 4 & 1) * CORE


def after(x, *earlier):
    return lax.optimization_barrier((x, earlier))[0]


def assemble_kernel(stacked, me_ref, *refs):
    ins, outs = refs[:8], refs[8:]
    for half in range(2):
        for rel in range(32):
            k = jnp.bitwise_xor(me_ref[0], flat_of(rel, half))
            src = ins[4 * half + rel // 8]
            for i in range(src.shape[1]):
                if stacked[half]:
                    outs[half][i, k] = src[rel % 8, i]
                else:
                    outs[half][k, i] = src[rel % 8, i]


def small_call(body, shapes, dtype, *ins, mib=32):
    return pl.pallas_call(
        body,
        in_specs=[pl.BlockSpec(memory_space=pltpu.VMEM)] * len(ins),
        out_specs=[pl.BlockSpec(memory_space=pltpu.VMEM)] * len(shapes),
        out_shape=[sds(shape, dtype) for shape in shapes],
        cost_estimate=cost(2),
        compiler_params=params(mib),
    )(*ins)


def halve(parts, split, mib=32):
    n, r, c = parts[0].shape

    def body(*refs):
        first, second = refs[-2:]
        for k, ref in enumerate(refs[:-2]):
            first[k] = ref[:split]
            second[k] = ref[split:]

    return small_call(body, [(len(parts), split, r, c), (len(parts), n - split, r, c)], parts[0].dtype, *parts, mib=mib)


def double(halves, got):
    def body(a, b, a_got, b_got, a_out, b_out):
        for mine, other, out in ((a, a_got, a_out), (b, b_got, b_out)):
            m = mine.shape[0]
            out[:m] = mine[...]
            out[m:] = other[...]

    shapes = [(2 * h.shape[0],) + h.shape[1:] for h in halves]
    return small_call(body, shapes, halves[0].dtype, *halves, *got)


def parcel(attention, expand, contract, small):
    r, F = expand.shape
    V = small.shape[0]
    C = F // FC
    G = attention.shape[2] // GC

    def body(att_ref, exp_ref, con_ref, small_ref, first, third, pad):
        pad[...] = jnp.zeros_like(pad)
        pad[0:V, 0:r] = small_ref[...]
        turned = pad[...].T
        narrow = lambda m, g: att_ref[m, :, g * GC : (g + 1) * GC].astype(BF)
        for g in range(G):
            for i, m in ((0, 0), (G, 1), (2 * G + 1, 2), (3 * G + 1, 3)):
                first[i + g] = narrow(m, g)
        first[2 * G] = jnp.concatenate([turned[0:r, :], jnp.zeros((r, GC - 128), F32)], axis=1).astype(BF)
        for i in range(C):
            third[i] = exp_ref[:, i * FC : (i + 1) * FC].astype(BF)
        third[C] = att_ref[4].astype(BF)
        for i in range(C):
            third[C + 1 + i] = con_ref[i * r : (i + 1) * r, :].astype(BF)

    shapes = [(4 * G + 1, r, GC), (2 * C + 1, r, FC)]
    return pl.pallas_call(
        body,
        in_specs=[pl.BlockSpec(memory_space=pltpu.VMEM)] * 4,
        out_specs=[pl.BlockSpec(memory_space=pltpu.VMEM)] * 2,
        out_shape=[sds(shape, BF) for shape in shapes],
        scratch_shapes=[pltpu.VMEM((128, 128), F32)],
        cost_estimate=cost(2),
        compiler_params=params(58),
    )(attention, expand, contract, small)


class Gather:
    def __init__(self, me, part, split, stacked=(True, True)):
        self.me, self.part, self.split, self.stacked = me, part, split, stacked
        self.along = [part]

    def far(self, *ks, then=()):
        part = after(self.part, then) if then else self.part
        self.along += [swap(part, k * Z) for k in ks]
        return self.along[-1]

    def plane(self, *earlier):
        along = after(self.along, *earlier) if earlier else self.along
        self.halves = halve(along, self.split, 32 if self.part.shape[2] == GC else 58)
        self.got = [swap(h, HALVES[i][0]) for i, h in enumerate(self.halves)]
        return self.halves

    def plane_again(self, *earlier):
        halves, got = after((self.halves, self.got), *earlier) if earlier else (self.halves, self.got)
        self.firsts = double(halves, got)
        self.seconds = [swap(h, HALVES[i][1]) for i, h in enumerate(self.firsts)]
        return self.firsts

    def cores(self, *earlier):
        firsts, seconds = after((self.firsts, self.seconds), *earlier) if earlier else (self.firsts, self.seconds)
        self.pieces = []
        for f, s in zip(firsts, seconds):
            self.pieces += [f, s, swap(f, CORE), swap(s, CORE)]
        return firsts, seconds

    def result(self, *earlier):
        pieces = after(self.pieces, *earlier) if earlier else self.pieces
        n, r, c = self.part.shape
        wide = min(c, 384)
        counts = [self.split, n - self.split]
        specs = [pl.BlockSpec((8, m, r, wide), lambda j: (0, 0, 0, j)) for m in counts for _ in range(4)]
        shapes, outs = [], []
        for m, stacked in zip(counts, self.stacked):
            lead = (m, 32) if stacked else (32, m)
            shapes.append(sds(lead + (r, c), self.part.dtype))
            outs.append(pl.BlockSpec(lead + (r, wide), lambda j: (0, 0, 0, j)))
        out = pl.pallas_call(
            functools.partial(assemble_kernel, self.stacked),
            grid=(c // wide,),
            in_specs=[pl.BlockSpec(memory_space=pltpu.SMEM)] + specs,
            out_specs=outs,
            out_shape=shapes,
            cost_estimate=cost(4),
            compiler_params=params(50 if c > GC else 58),
        )(self.me, *pieces)
        return [o.reshape(m, 32 * r, c) if stacked else o.reshape(32 * m * r, c) for o, m, stacked in zip(out, counts, self.stacked)]


def join_kernel(plan, *refs):
    n = 1 + max(w for blocks in plan for _, terms in blocks for w, _ in terms)
    ins, outs = refs[:n], refs[n:]
    for out, blocks in zip(outs, plan):
        for place, terms in blocks:
            total = None
            for w, at in terms:
                v = ins[w][at].astype(F32)
                total = v if total is None else total + v
            out[place] = total.astype(BF)


def join(plan, shapes, ins):
    return pl.pallas_call(
        functools.partial(join_kernel, plan),
        in_specs=[pl.BlockSpec(memory_space=pltpu.VMEM)] * len(ins),
        out_specs=[pl.BlockSpec(memory_space=pltpu.VMEM)] * len(shapes),
        out_shape=[sds(shape, BF) for shape in shapes],
        cost_estimate=cost(1),
        compiler_params=params(32),
    )(*ins)


def settle(terms):
    def body(*refs):
        total = refs[0][...].astype(F32)
        for ref in refs[1:-1]:
            total += ref[...].astype(F32)
        refs[-1][...] = total

    return small_call(body, [terms[0].shape], F32, *terms)[0]


class Reduction:
    def __init__(self, *halves):
        self.halves = []
        for h, parts in enumerate(halves):
            self.halves.append([(k, swap(s, CORE)) for k, s in parts])
        self.token = None

    def add(self, *halves):
        for mine, parts in zip(self.halves, halves):
            mine += [(k, swap(s, CORE)) for k, s in parts]

    def flat(self, earlier):
        halves = after(self.halves, *earlier) if earlier else self.halves
        ins, at = [], []
        for parts in halves:
            blocks = []
            for terms in parts:
                blocks += [[(len(ins) + t, b) for t in range(len(terms))] for b in range(terms[0].shape[1])]
                ins += terms
            at.append(blocks)
        return ins, at, ins[0].shape[2:]

    def cross(self, *earlier):
        ins, at, tail = self.flat(earlier)
        n = ins[0].shape[0] // 2
        bit = 1 if n == 8 else 0
        plan, shapes = [], []
        for blocks in at:
            for far in range(2):
                plan.append([((j, b), [(w, (far * n + j, i)) for w, i in terms]) for j in range(n) for b, terms in enumerate(blocks)])
                shapes.append((n, len(blocks)) + tail)
        out = join(plan, shapes, ins)
        self.halves = [[(out[2 * h], swap(out[2 * h + 1], HALVES[h][bit]))] for h in range(2)]
        self.token = out

    def direct(self, *earlier):
        ins, at, tail = self.flat(earlier)
        count = sum(len(blocks) for blocks in at)
        plan = []
        for q in range(4):
            places = []
            b = 0
            for h, blocks in enumerate(at):
                lead = 4 * (q if h == 0 else (q >> 1) + 2 * (q & 1))
                for terms in blocks:
                    places += [((j, b), [(w, (lead + j, i)) for w, i in terms]) for j in range(4)]
                    b += 1
            plan.append(places)
        out = join(plan, [(4, count) + tail] * 4, ins)
        self.halves = [[tuple([out[0]] + [swap(out[q], (q & 1) * X + (q >> 1) * Y) for q in range(1, 4)])]]
        self.token = out

    def along(self, *earlier, also=()):
        groups = [r.flat(earlier) for r in (self,) + tuple(also)]
        ins, places, tail = [], [[] for _ in range(4)], groups[0][2]
        b = 0
        for more, at, _ in groups:
            base = len(ins)
            ins += more
            for blocks in at:
                for terms in blocks:
                    for k in range(4):
                        places[k].append((b, [(base + w, (k, i)) for w, i in terms]))
                    b += 1
        out = join(places, [(b,) + tail] * 4, ins)
        self.terms = [out[0]] + [swap(out[k], k * Z) for k in range(1, 4)]
        self.token = out


def prepare_kernel(lengths_ref, hidden_ref, key_ref, pooled_ref, low_ref, hidt_ref, lowt_ref, bias_ref, mask_ref, wide):
    hid = hidden_ref[0]
    half, L = pooled_ref.shape[1], hid.shape[0]
    hidt_ref[0] = hid.T
    columns = []
    for i in range(wide.shape[0]):
        wide[i] = hid[:, i * 128 : (i + 1) * 128].astype(F32)
        columns.append((wide[i, pl.ds(0, half, stride=2), :] + wide[i, pl.ds(1, half, stride=2), :]) * 0.5)
    pooled = jnp.concatenate(columns, axis=1)
    pooled_ref[0] = pooled
    low = pooled.astype(BF)
    low_ref[0] = low
    lowt_ref[0] = low.T
    place = lax.broadcasted_iota(jnp.int32, (1, L), 1)
    valid = (key_ref[pl.ds(pl.program_id(0), 1), :] == 1) & (place < lengths_ref[pl.program_id(0)])
    bias_ref[0] = jnp.where(valid, 0.0, MASK_FILL)
    twice = 2 * lax.broadcasted_iota(jnp.int32, (half, L), 0)
    token = lax.broadcasted_iota(jnp.int32, (half, L), 1)
    of = ((token == twice) | (token == twice + 1)).astype(F32).astype(BF)
    rows = jnp.broadcast_to(valid.astype(F32), (16, L)).astype(BF)
    mask_ref[0] = jnp.minimum(dot_nt(of, rows)[:, 0:1], 1.0)


def prepare(hidden, lengths, key_mask):
    B, L, D = hidden.shape
    R = L // 2
    return pl.pallas_call(
        prepare_kernel,
        grid=(B,),
        in_specs=[pl.BlockSpec(memory_space=pltpu.SMEM), seqs(L, D), whole(B, L)],
        out_specs=[seqs(R, D), seqs(R, D), seqs(D, L), seqs(D, R), seqs(1, L), seqs(R, 1)],
        out_shape=[sds((B, R, D), F32), sds((B, R, D), BF), sds((B, D, L), BF), sds((B, D, R), BF), sds((B, 1, L), F32),
                   sds((B, R, 1), F32)],
        scratch_shapes=[pltpu.VMEM((D // 128, L, 128), F32)],
        cost_estimate=cost(6),
        compiler_params=params(58),
    )(lengths, hidden, key_mask)


def attend_kernel(start, per, hidden_ref, pooled_ref, wq_ref, wk_ref, wv_ref, wr_ref, table_ref, small_ref, bias_ref, *refs):
    ctx_ref, probs_ref, qu_ref, qw_ref, keys_ref, values_ref, rel_out, rel_ref = refs[-8:]
    half = hidden_ref.shape[1] // 2
    blk = half // 2
    step = pl.program_id(0)

    @pl.when((step == 0) | (lax.rem(start + step, per) == 0))
    def _():
        rel = dot(table_ref[...], wr_ref[0]).astype(BF)
        rel_ref[...] = rel
        rel_out[...] = rel

    hid = hidden_ref[0]
    small_ref = small_ref[0, :, 0:128].astype(F32).T
    q = dot(pooled_ref[0], wq_ref[0])
    qu = (q + small_ref[0:1, :]).astype(BF)
    qw = (q + small_ref[1:2, :]).astype(BF)
    qu_ref[0] = qu
    qw_ref[0] = qw
    keys_ref[0] = dot(hid, wk_ref[0]).astype(BF)
    values_ref[0] = (dot(hid, wv_ref[0]) + small_ref[2:3, :]).astype(BF)
    bias = bias_ref[0]
    lane = lax.broadcasted_iota(jnp.int32, (1, GC), 1)
    masks = [(lane >= h * HEAD) & (lane < (h + 1) * HEAD) for h in range(GH)]
    qu8 = qu.astype(F32) * 0.125
    qw8 = qw.astype(F32) * 0.125
    wide = 2 * half + 128
    for b in range(2):
        rows = slice(b * blk, (b + 1) * blk)
        m0 = half * (1 - b)
        quh = jnp.concatenate([jnp.where(m, qu8[rows], 0.0).astype(BF) for m in masks], axis=0)
        qwh = jnp.concatenate([jnp.where(m, qw8[rows], 0.0).astype(BF) for m in masks], axis=0)
        content = dot_nt(quh, keys_ref[0])
        placed = dot_nt(qwh, rel_ref[m0 : m0 + 3 * half, :])
        lows = []
        for h in range(GH):
            for r in range(0, blk, TILE):
                hr = slice(h * blk + r, h * blk + r + TILE)
                at = half - 128 - 2 * r // 128 * 128
                moved = pltpu.roll(placed[hr, at : at + wide], 2 * r % 128, 1, stride=2, stride_axis=0)[:, 128:]
                s = content[hr] + moved + bias
                top = jnp.max(s, axis=-1, keepdims=True)
                e = jnp.exp(s - top)
                p = e * (1.0 / jnp.sum(e, axis=-1, keepdims=True))
                probs_ref[0, 0, h, b * blk + r : b * blk + r + TILE, :] = p
                lows.append(p.astype(BF))
        c = dot(jnp.concatenate(lows, axis=0), values_ref[0])
        total = c[0:blk]
        for h in range(1, GH):
            total = jnp.where(masks[h], c[h * blk : (h + 1) * blk], total)
        ctx_ref[0, rows, :] = total.astype(BF)


def attend(start, stop, hidden, pooled_low, weights, table, bias, held=None):
    B, L, D = hidden.shape
    R = L // 2
    G = D // GC
    g = lambda i: (start + i) // B
    s = lambda i: lax.rem(start + i, B)
    seq = lambda r: pl.BlockSpec((1, r, D), lambda i: (s(i), 0, 0))
    mat = lambda base: pl.BlockSpec((1, D, GC), lambda i: (base + g(i), 0, 0))
    so = lambda r: pl.BlockSpec((1, r, GC), lambda i: (s(i), 0, g(i)))
    a, b = weights
    ins = [hidden, pooled_low, a, a, b, b, table, a, bias]
    specs = [seq(L), seq(R), mat(0), mat(G), mat(0), mat(G), whole(2 * L, D),
             pl.BlockSpec((1, GC, GC), lambda i: (2 * G, g(i), 0)), pl.BlockSpec((1, 1, L), lambda i: (s(i), 0, 0))]
    aliases = {}
    if held is not None:
        aliases = {len(ins) + i: i for i in range(7)}
        ins += list(held)
        specs += [pl.BlockSpec(memory_space=pl.ANY)] * 7
    return pl.pallas_call(
        functools.partial(attend_kernel, start, B),
        grid=(stop - start,),
        in_specs=specs,
        out_specs=[so(R), pl.BlockSpec((1, 1, GH, R, L), lambda i: (s(i), g(i), 0, 0, 0)), so(R), so(R), so(L), so(L),
                   pl.BlockSpec((2 * L, GC), lambda i: (0, g(i)))],
        out_shape=[sds((B, R, D), BF), sds((B, G, GH, R, L), F32), sds((B, R, D), BF), sds((B, R, D), BF),
                   sds((B, L, D), BF), sds((B, L, D), BF), sds((2 * L, D), BF)],
        scratch_shapes=[pltpu.VMEM((2 * L, GC), BF)],
        input_output_aliases=aliases,
        cost_estimate=cost(4 * (stop - start)),
        compiler_params=params(58),
    )(*ins)


def phi_and_slope(z):
    e = jnp.exp(z * z * (-0.5))
    t = 1.0 / (1.0 + (0.3275911 * 0.7071067811865476) * jnp.abs(z))
    poly = t * (0.127414796 + t * (-0.142248368 + t * (0.7107068705 + t * (-0.7265760135 + t * 0.5307027145))))
    tail = poly * e
    phi = jnp.where(z >= 0, 1.0 - tail, tail)
    return phi, phi + z * e * 0.3989422804014327


def norm(x):
    center = x - jnp.mean(x, axis=-1, keepdims=True)
    inv = lax.rsqrt(jnp.mean(center * center, axis=-1, keepdims=True) + EPSILON)
    return center * inv, inv


def norm_back(e, n, inv):
    return inv * (e - jnp.mean(e, axis=-1, keepdims=True) - n * jnp.mean(e * n, axis=-1, keepdims=True))


def add_rows(ref, *values):
    for k, v in enumerate(values):
        ref[k : k + 1, :] += jnp.sum(v, axis=0, keepdims=True)


def mlp_kernel(dealt, *refs):
    me_ref, ctx_ref, pooled_ref, cot_ref, mask_ref, exp_ref, w2_ref, turned_ref = refs[:8]
    out_ref, y1_ref, n1_ref, s1_ref, slope_ref, dx2_ref, e2_ref, sums_ref = refs[8:16]
    grads, (small_ref, inner_ref, e2_all, total) = refs[16:-4], refs[-4:]
    rows_here = pooled_ref.shape[1]
    mine = pl.ds(pl.multiple_of(pl.program_id(0) * rows_here, 16), rows_here)
    @pl.when(pl.program_id(0) == 0)
    def _():
        sums_ref[...] = jnp.zeros_like(sums_ref)
        small_ref[...] = turned_ref[0, :, 0:128].astype(F32).T

    row = lambda k: small_ref[k : k + 1, :]
    chunks = exp_ref.shape[0] - 1
    x1 = pooled_ref[0] + dot(ctx_ref[0], exp_ref[chunks]) + row(3)
    n1, inv1 = norm(x1)
    n1_ref[0] = n1
    s1_ref[0] = inv1
    y1 = n1 * row(4) + row(5)
    y1l = y1.astype(BF)
    y1_ref[0] = y1l
    x2 = y1 + row(6)
    for c in range(chunks):
        cs = slice(c * FC, (c + 1) * FC)
        z = dot(y1l, exp_ref[c]) + row(9 + c)
        phi, slope = phi_and_slope(z)
        inner = (z * phi).astype(BF)
        inner_ref[mine, cs] = inner
        slope_ref[0, :, cs] = slope
        x2 += dot(inner, w2_ref[cs, :])
    n2, inv2 = norm(x2)
    m = mask_ref[0]
    out_ref[0] = ((n2 * row(7) + row(8)) * m).astype(BF)
    dy2 = cot_ref[0].astype(F32) * m
    dx2 = norm_back(dy2 * row(7), n2, inv2)
    dx2_ref[0] = dx2
    e2 = dx2.astype(BF)
    e2_ref[0] = e2
    add_rows(sums_ref, dx2, dy2 * n2, dy2)
    e2_all[mine, :] = e2

    @pl.when(pl.program_id(0) == pl.num_programs(0) - 1)
    def _():
        for c in range(chunks):
            cs = slice(c * FC, (c + 1) * FC)
            v = dot_tn(inner_ref[:, cs], e2_all[...])
            if not dealt:
                grads[0][cs, :] = v
            else:
                total[cs, :] = v
        if dealt:
            r = grads[0].shape[2]
            for half in range(2):
                for rel in range(32):
                    k = jnp.bitwise_xor(me_ref[0], flat_of(rel, half))
                    at = pl.multiple_of(k * (2 * r) + half * r, 8)
                    grads[2 * half + rel // 16][rel % 16, 0] = total[pl.ds(at, r), :].astype(BF)


def mlp(me, ctx, pooled, cot, mask, expand, w2, small, dealt):
    B, R, D = pooled.shape
    F = w2.shape[0]
    grads = [sds((16, 1, F // 64, D), BF)] * 4 if dealt else [sds((F, D), F32)]
    return pl.pallas_call(
        functools.partial(mlp_kernel, dealt),
        grid=(B,),
        in_specs=[pl.BlockSpec(memory_space=pltpu.SMEM), seqs(R, D), seqs(R, D), seqs(R, D), seqs(R, 1), whole(*expand.shape), whole(F, D),
                  turned_small(D)],
        out_specs=[seqs(R, D), seqs(R, D), seqs(R, D), seqs(R, 1), seqs(R, F), seqs(R, D), seqs(R, D),
                   pl.BlockSpec((8, D), lambda s: (0, 0))] + [whole(*g.shape) for g in grads],
        out_shape=[sds((B, R, D), BF), sds((B, R, D), BF), sds((B, R, D), F32), sds((B, R, 1), F32),
                   sds((B, R, F), F32), sds((B, R, D), F32), sds((B, R, D), BF), sds((8, D), F32)] + grads,
        scratch_shapes=[pltpu.VMEM((128, D), F32), pltpu.VMEM((B * R, F), BF), pltpu.VMEM((B * R, D), BF), pltpu.VMEM((F, D), F32)],
        cost_estimate=cost(38),
        compiler_params=params(50),
    )(me, ctx, pooled, cot, mask, expand, w2, small)


def mlp_back_kernel(dx2_ref, e2_ref, slope_ref, n1_ref, s1_ref, exp_ref, w2_ref, turned_ref,
                    e1_ref, dx1_ref, ea_ref, dctx_ref, sums_ref, db1_ref, small_ref):
    @pl.when(pl.program_id(0) == 0)
    def _():
        small_ref[...] = turned_ref[0, :, 0:128].astype(F32).T
        sums_ref[...] = jnp.zeros_like(sums_ref)
        db1_ref[...] = jnp.zeros_like(db1_ref)

    chunks = exp_ref.shape[0] - 1
    e2 = e2_ref[0]
    dy1 = dx2_ref[0]
    for c in range(chunks):
        cs = slice(c * FC, (c + 1) * FC)
        dz = dot_nt(e2, w2_ref[cs, :]) * slope_ref[0, :, cs]
        db1_ref[:, cs] += jnp.sum(dz, axis=0, keepdims=True)
        e1 = dz.astype(BF)
        e1_ref[0, :, cs] = e1
        dy1 += dot_nt(e1, exp_ref[c])
    n1 = n1_ref[0]
    dx1 = norm_back(dy1 * small_ref[4:5, :], n1, s1_ref[0])
    dx1_ref[0] = dx1
    ea = dx1.astype(BF)
    ea_ref[0] = ea
    dctx_ref[0] = dot_nt(ea, exp_ref[chunks]).astype(BF)
    add_rows(sums_ref, dx1, dy1 * n1, dy1)


def mlp_back(dx2, e2, slope, n1, s1, expand, w2, small):
    B, R, D = dx2.shape
    F = w2.shape[0]
    return pl.pallas_call(
        mlp_back_kernel,
        grid=(B,),
        in_specs=[seqs(R, D), seqs(R, D), seqs(R, F), seqs(R, D), seqs(R, 1), whole(*expand.shape), whole(F, D),
                  turned_small(D)],
        out_specs=[seqs(R, F), seqs(R, D), seqs(R, D), seqs(R, D), pl.BlockSpec((8, D), lambda s: (0, 0)),
                   pl.BlockSpec((1, F), lambda s: (0, 0))],
        out_shape=[sds((B, R, F), BF), sds((B, R, D), F32), sds((B, R, D), BF), sds((B, R, D), BF), sds((8, D), F32),
                   sds((1, F), F32)],
        scratch_shapes=[pltpu.VMEM((128, D), F32)],
        cost_estimate=cost(21),
        compiler_params=params(50),
    )(dx2, e2, slope, n1, s1, expand, w2, small)


def deal(half, me, total_ref, put):
    r = total_ref.shape[0] // 32
    for rel in range(32):
        k = jnp.bitwise_xor(me, flat_of(rel, half))
        put(rel // 16, rel % 16, total_ref[pl.ds(pl.multiple_of(k * r, 8), r), :].astype(BF))


def outer_kernel(half, me_ref, a_ref, b_ref, keep_ref, send_ref, turned, total):
    B, R, M = a_ref.shape

    @pl.when(pl.program_id(0) == 0)
    def _():
        turned[...] = a_ref[...].reshape(B * R, M).T

    total[...] = dot(turned[...], b_ref[...].reshape(B * R, b_ref.shape[2]))

    def put(sent, i, v):
        for j in range(v.shape[1] // GC):
            (send_ref if sent else keep_ref)[i, j] = v[:, j * GC : (j + 1) * GC]

    deal(half, me_ref[0], total, put)


def outer_plain_kernel(a_ref, b_ref, out_ref):
    B, R, M = a_ref.shape
    out_ref[...] = dot_tn(a_ref[...].reshape(B * R, M), b_ref[...].reshape(B * R, b_ref.shape[2]))


def outer(me, a, b, cols, half=None, blocks=None):
    B, R, M = a.shape
    N = b.shape[2]
    first, count = blocks or (0, N // cols)
    specs = [pl.BlockSpec((B, R, M), lambda j: (0, 0, 0)), pl.BlockSpec((B, R, cols), lambda j: (0, 0, first + j))]
    price = cost(2.0 * count)
    if half is None:
        return pl.pallas_call(
            outer_plain_kernel, grid=(count,), in_specs=specs,
            out_specs=pl.BlockSpec((M, cols), lambda j: (0, j)),
            out_shape=sds((M, N), F32), cost_estimate=price, compiler_params=params(32))(a, b)
    return pl.pallas_call(
        functools.partial(outer_kernel, half),
        grid=(count,),
        in_specs=[pl.BlockSpec(memory_space=pltpu.SMEM)] + specs,
        out_specs=[pl.BlockSpec((16, cols // GC, M // 32, GC), lambda j: (0, j, 0, 0))] * 2,
        out_shape=[sds((16, count * cols // GC, M // 32, GC), BF)] * 2,
        scratch_shapes=[pltpu.VMEM((M, B * R), BF), pltpu.VMEM((M, cols), F32)],
        cost_estimate=price,
        compiler_params=params(32),
    )(me, a, b)


def wide_outer_kernel(chunks, me_ref, y1_ref, e1_ref, ctx_ref, ea_ref, keep0, send0, keep1, send1, turned, total):
    B, R, D = y1_ref.shape
    j = pl.program_id(0)
    flat = lambda ref: ref[...].reshape(B * R, D)

    def dealt(half, base):
        def put(sent, i, v):
            ref = ((keep0, send0), (keep1, send1))[half][sent]
            for b in range(D // GC):
                ref[i, base + b] = v[:, b * GC : (b + 1) * GC]

        deal(half, me_ref[0], total, put)

    @pl.when(j == 0)
    def _():
        turned[...] = flat(y1_ref).T

    @pl.when(j < chunks)
    def _():
        total[...] = dot(turned[...], flat(e1_ref))

    @pl.when(j == chunks)
    def _():
        total[...] = dot_tn(flat(ctx_ref), flat(ea_ref))
        dealt(0, chunks // 2 * (D // GC))

    @pl.when(j < chunks // 2)
    def _():
        dealt(0, j * (D // GC))

    @pl.when((j >= chunks // 2) & (j < chunks))
    def _():
        dealt(1, (j - chunks // 2) * (D // GC))


def wide_outer(me, y1, e1, ctx, ea):
    B, R, D = y1.shape
    F = e1.shape[2]
    chunks = F // D
    n = D // GC
    shapes = [(16, m, D // 32, GC) for m in (chunks // 2 * n + n, chunks // 2 * n) for _ in range(2)]
    out = pl.pallas_call(
        functools.partial(wide_outer_kernel, chunks),
        grid=(chunks + 1,),
        in_specs=[pl.BlockSpec(memory_space=pltpu.SMEM), whole(B, R, D),
                  pl.BlockSpec((B, R, D), lambda j: (0, 0, jnp.minimum(j, chunks - 1))), whole(B, R, D), whole(B, R, D)],
        out_specs=[whole(*shape) for shape in shapes],
        out_shape=[sds(shape, BF) for shape in shapes],
        scratch_shapes=[pltpu.VMEM((D, B * R), BF), pltpu.VMEM((D, D), F32)],
        cost_estimate=cost(12),
        compiler_params=params(40),
    )(me, y1, e1, ctx, ea)
    return tuple(out[:2]), tuple(out[2:])


def small_deal_kernel(me_ref, *refs):
    sums, (sums1, sums2, db1, keep_ref, send_ref, total, turned) = refs[:-7], refs[-7:]
    D = sums1.shape[1]
    total[...] = jnp.zeros_like(total)
    for g, s in enumerate(sums):
        total[0:3, g * GC : (g + 1) * GC] = s[0:3, :]
    total[3:6, :] = sums1[0:3, :]
    total[6:9, :] = sums2[0:3, :]
    for i in range(db1.shape[1] // D):
        total[9 + i : 10 + i, :] = db1[0:1, i * D : (i + 1) * D]
    turned[...] = jnp.concatenate([total[...].T, jnp.zeros((D, GC - total.shape[0]), F32)], axis=1)

    def put(sent, i, v):
        (send_ref if sent else keep_ref)[i, 0] = v

    deal(0, me_ref[0], turned, put)


def small_deal(me, sums, sums1, sums2, db1):
    D = sums1.shape[1]
    n = 4 + len(sums)
    return pl.pallas_call(
        small_deal_kernel,
        in_specs=[pl.BlockSpec(memory_space=pltpu.SMEM)] + [pl.BlockSpec(memory_space=pltpu.VMEM)] * (n - 1),
        out_specs=[pl.BlockSpec(memory_space=pltpu.VMEM)] * 2,
        out_shape=[sds((16, 1, D // 32, GC), BF)] * 2,
        scratch_shapes=[pltpu.VMEM((128, D), F32), pltpu.VMEM((D, GC), F32)],
        cost_estimate=cost(2),
        compiler_params=params(24),
    )(me, *sums, sums1, sums2, db1)


def attend_back_kernel(plan, *refs):
    (me_ref, probs_ref, dctx_ref, qu_ref, qw_ref, keys_ref, values_ref, rel_ref, hidt_ref, lowt_ref, tablet_ref) = refs[:11]
    outs = refs[11 : 14]
    dq_ref, dk_ref, dv_ref = outs
    grads = refs[14 : -8]
    sums_ref = refs[-8]
    acc_q, acc_k, acc_v, acc_r, acc_dv, dkt, dvt = refs[-7:]
    step = pl.program_id(0)
    half, L = probs_ref.shape[3], probs_ref.shape[4]
    blk = half // 2

    @pl.when(step == 0)
    def _():
        for a in (acc_q, acc_k, acc_v, acc_r, acc_dv, sums_ref):
            a[...] = jnp.zeros_like(a)

    across = lax.broadcasted_iota(jnp.int32, (half, half), 0) + lax.broadcasted_iota(jnp.int32, (half, half), 1)
    flip = (across == half - 1).astype(F32).astype(BF)
    lane = lax.broadcasted_iota(jnp.int32, (1, GC), 1)
    dctx = dctx_ref[0]
    dctx_t = dctx.T
    qu_t = qu_ref[0].T
    qwr_t = dot(flip, qw_ref[0]).astype(BF).T
    keys = keys_ref[0]
    values = values_ref[0]
    masks = [(lane >= h * HEAD) & (lane < (h + 1) * HEAD) for h in range(GH)]
    dctx_wide = dctx.astype(F32)
    dp = dot_nt(jnp.concatenate([jnp.where(m, dctx_wide, 0.0).astype(BF) for m in masks], axis=0), values)
    backs = []
    moved = [[], []]
    for h in range(GH):
        sel = slice(h * HEAD, (h + 1) * HEAD)
        draws, lows = [], []
        for r in range(0, half, TILE):
            p = probs_ref[0, 0, h, r : r + TILE, :]
            t = p * dp[h * half + r : h * half + r + TILE]
            draws.append((t - p * jnp.sum(t, axis=-1, keepdims=True)).astype(BF))
            lows.append(p.astype(BF))
        draw = jnp.concatenate(draws, axis=0)
        dvt[sel, :] = dot(dctx_t[sel], jnp.concatenate(lows, axis=0))
        both = dot(jnp.concatenate([qu_t[sel], flip], axis=0), draw)
        dkt[sel, :] = both[:HEAD] * 0.125
        back = both[HEAD:]
        backs.append(back.astype(BF))
        for b in range(2):
            tiles = []
            for r in range(0, blk, TILE):
                x = jnp.concatenate([back[b * blk + r : b * blk + r + TILE], jnp.zeros((TILE, 128), F32)], axis=1)
                x = pltpu.roll(x, 2 + 2 * r % 128, 1, stride=2, stride_axis=0).astype(BF)
                none = jnp.zeros((TILE, 128), BF)
                tiles.append(jnp.concatenate([x, none] if r < blk // 2 else [none, x], axis=1))
            x = jnp.concatenate(tiles, axis=0)
            m0 = half * b
            acc_r[sel, m0 : m0 + 3 * half] += dot(qwr_t[sel, b * blk : (b + 1) * blk], x)
            moved[b].append(x)
    alone = lambda v, n: functools.reduce(lambda t, h: jnp.where(masks[h], v[h * n : (h + 1) * n], t), range(1, GH), v[0:n])
    dqu = alone(dot(jnp.concatenate(backs, axis=0), keys), half)
    dqw = jnp.concatenate(
        [alone(dot(jnp.concatenate(moved[b], axis=0), rel_ref[half * b : half * b + 3 * half, :]), blk) for b in range(2)], axis=0
    )
    dqu = dqu * 0.125
    dqw = dqw * 0.125
    dq = dot(flip, (dqu + dqw).astype(BF)).astype(BF)
    dk = dkt[...].astype(BF).T
    dvf = dvt[...]
    dv = dvf.astype(BF).T
    dq_ref[0] = dq
    dk_ref[0] = dk
    dv_ref[0] = dv
    acc_dv[...] += dvf
    add_rows(sums_ref, dqu, dqw)
    acc_q[...] += dot(lowt_ref[0], dq)
    acc_k[...] += dot(hidt_ref[0], dk)
    acc_v[...] += dot(hidt_ref[0], dv)

    @pl.when(step == pl.num_programs(0) - 1)
    def _():
        sums_ref[2:3, :] = jnp.sum(acc_dv[...].T, axis=0, keepdims=True)
        dr = acc_r[...] * 0.125
        hi = dr.astype(BF)
        lo = (dr - hi.astype(F32)).astype(BF)
        tt = tablet_ref[...]
        if plan is None:
            for i, a in enumerate((acc_q, acc_k, acc_v)):
                grads[0][i] = a[...]
            grads[0][3] = dot_nt(tt, hi) + dot_nt(tt, lo)
        else:
            for i in range(4):
                half = plan[i]
                at = plan[:i].count(half)
                base = 2 * sorted(set(plan)).index(half)
                acc = (acc_q, acc_k, acc_v, acc_q)[i]
                if i == 3:
                    acc_q[...] = dot_nt(tt, hi) + dot_nt(tt, lo)

                def put(sent, j, v):
                    grads[base + sent][j, at] = v

                deal(half, me_ref[0], acc, put)


def attend_back(me, g, probs, dctx, qu, qw, keys, values, rel, hid_t, low_t, table_t, plan=None):
    B, R, D = qu.shape
    L = 2 * R
    so = lambda r: pl.BlockSpec((1, r, GC), lambda s: (s, 0, g))
    if plan is None:
        grad_specs = [pl.BlockSpec((4, D, GC), lambda s: (0, 0, 0))]
        grad_shapes = [sds((4, D, GC), F32)]
    else:
        sizes = [(16, plan.count(h), D // 32, GC) for h in sorted(set(plan)) for _ in range(2)]
        grad_specs = [whole(*size) for size in sizes]
        grad_shapes = [sds(size, BF) for size in sizes]
    return pl.pallas_call(
        functools.partial(attend_back_kernel, plan),
        grid=(B,),
        in_specs=[pl.BlockSpec(memory_space=pltpu.SMEM),
                  pl.BlockSpec((1, 1, GH, R, L), lambda s: (s, g, 0, 0, 0)), so(R), so(R), so(R), so(L), so(L),
                  pl.BlockSpec((2 * L, GC), lambda s: (0, g)), seqs(D, L), seqs(D, R), whole(D, 2 * L)],
        out_specs=[seqs(R, GC), seqs(L, GC), seqs(L, GC)] + grad_specs + [pl.BlockSpec((8, GC), lambda s: (0, 0))],
        out_shape=[sds((B, R, GC), BF), sds((B, L, GC), BF), sds((B, L, GC), BF)] + grad_shapes + [sds((8, GC), F32)],
        scratch_shapes=[pltpu.VMEM((D, GC), F32)] * 3 + [pltpu.VMEM((GC, 2 * L), F32)] + [pltpu.VMEM((GC, L), F32)] * 3,
        cost_estimate=cost(22),
        compiler_params=params(48),
    )(me, probs, dctx, qu, qw, keys, values, rel, hid_t, low_t, table_t)


def input_grad_kernel(at, *refs):
    groups = len(at)
    dqs, dks, dvs = refs[:groups], refs[groups : 2 * groups], refs[2 * groups : 3 * groups]
    dx1_ref, weights, out_ref, wide = refs[3 * groups], refs[3 * groups + 1 : -2], refs[-2], refs[-1]
    half = dx1_ref.shape[1]
    shared = dx1_ref[0]
    total = None
    for g in range(groups):
        wq, wk, wv = (weights[a][i] for a, i in at[g])
        shared += dot_nt(dqs[g][0], wq)
        t = dot_nt(dks[g][0], wk) + dot_nt(dvs[g][0], wv)
        total = t if total is None else total + t
    shared = shared * 0.5
    for i in range(wide.shape[0]):
        cs = slice(i * 128, (i + 1) * 128)
        wide[i, pl.ds(0, half, stride=2), :] = shared[:, cs]
        wide[i, pl.ds(1, half, stride=2), :] = shared[:, cs]
        out_ref[0, :, cs] = (total[:, cs] + wide[i]).astype(BF)


def input_grad(dqs, dks, dvs, dx1, weights, at):
    B, R, D = dx1.shape
    L = 2 * R
    G = len(dqs)
    return pl.pallas_call(
        functools.partial(input_grad_kernel, at),
        grid=(B,),
        in_specs=[seqs(R, GC)] * G + [seqs(L, GC)] * (2 * G) + [seqs(R, D)] + [whole(*w.shape) for w in weights],
        out_specs=seqs(L, D),
        out_shape=sds((B, L, D), BF),
        scratch_shapes=[pltpu.VMEM((D // 128, L, 128), F32)],
        cost_estimate=cost(10),
        compiler_params=params(40),
    )(*dqs, *dks, *dvs, dx1, *weights)


def adamw(weight, moment, second, gradient, rates):
    new_moment = rates[1] * moment + (1.0 - rates[1]) * gradient
    new_second = rates[2] * second + (1.0 - rates[2]) * gradient * gradient
    moment_hat = new_moment / rates[4]
    second_hat = new_second / rates[5]
    new_weight = weight - rates[0] * (moment_hat / (jnp.sqrt(second_hat) + 1e-08) + rates[3] * weight)
    return (new_weight, new_moment, new_second)


def update_kernel(plan, rates_ref, w_ref, m_ref, v_ref, *refs):
    terms, (grad_ref, w_out, m_out, v_out) = refs[:-4], refs[-4:]
    rates = [rates_ref[i] for i in range(6)]
    for first, count, block, dest in plan:
        g = None
        for t in terms[first : first + count]:
            v = (t[...] if block is None else t[block]).astype(F32)
            g = v if g is None else g + v
        grad_ref[dest] = g
        w_out[dest], m_out[dest], v_out[dest] = adamw(w_ref[dest], m_ref[dest], v_ref[dest], g, rates)


def update(rates, w, m, v, terms, plan=None):
    plan = plan or [(0, len(terms), None, (slice(None),) * w.ndim)]
    return pl.pallas_call(
        functools.partial(update_kernel, plan),
        in_specs=[pl.BlockSpec(memory_space=pltpu.SMEM)] + [pl.BlockSpec(memory_space=pltpu.VMEM)] * (3 + len(terms)),
        out_specs=[pl.BlockSpec(memory_space=pltpu.VMEM)] * 4,
        out_shape=[sds(w.shape, F32)] * 4,
        cost_estimate=cost(2),
        compiler_params=params(24),
    )(rates, w, m, v, *terms)


def last_update_kernel(plan, small_at, rates_ref, *refs):
    ins, (pad, *_) = refs[:-9], refs[-1:]
    att, small, terms = ins[:3], ins[3:6], ins[6:]
    outs = refs[-9:-1]
    update_kernel(plan, rates_ref, *att, *terms, *outs[:4])
    first, count, block = small_at
    g = sum(t[block].astype(F32) for t in terms[first : first + count])
    V, r = small[0].shape
    pad[...] = jnp.zeros_like(pad)
    pad[0:r, :] = g[:, 0:128]
    pad[...] = pad[...].T
    rates = [rates_ref[i] for i in range(6)]
    g = pad[0:V, 0:r]
    outs[4][...] = g
    outs[5][...], outs[6][...], outs[7][...] = adamw(small[0][...], small[1][...], small[2][...], g, rates)


def last_update(rates, attention, small, terms, plan, small_at):
    like = [attention[0]] * 4 + [small[0]] * 4
    out = pl.pallas_call(
        functools.partial(last_update_kernel, plan, small_at),
        in_specs=[pl.BlockSpec(memory_space=pltpu.SMEM)] + [pl.BlockSpec(memory_space=pltpu.VMEM)] * (6 + len(terms)),
        out_specs=[pl.BlockSpec(memory_space=pltpu.VMEM)] * 8,
        out_shape=[sds(a.shape, F32) for a in like],
        scratch_shapes=[pltpu.VMEM((128, 128), F32)],
        cost_estimate=cost(3),
        compiler_params=params(24),
    )(rates, *attention, *small, *terms)
    return out[:4], out[4:]


def shards(fast, hidden, lengths, key_mask, cotangent, attention_weight, expand_weight, contract_weight, small_params,
           mean_attention, mean_expand, mean_contract, mean_small,
           square_attention, square_expand, square_contract, square_small, update_step, update_rates):
    B, L, D = hidden.shape
    R = L // 2
    F = expand_weight.shape[1]
    G = D // GC
    C = F // FC
    H = C // 2
    r = attention_weight.shape[1]
    V = small_params.shape[0]
    me = (lax.axis_index("dp") * lax.axis_size("fsdp") + lax.axis_index("fsdp")).astype(jnp.int32).reshape(1)

    table = rel_table(L, D)
    table, table_t = jnp.asarray(table), jnp.asarray(np.ascontiguousarray(table.T))

    def correction():
        return jnp.concatenate([update_rates, 1.0 - jnp.power(update_rates[1:3], update_step[0].astype(F32))])

    at = tuple(((0, g), (0, G + g), (1, g)) for g in range(G))
    if fast:
        first, third = parcel(attention_weight, expand_weight, contract_weight, small_params)
        gate1 = Gather(me, first, 2 * G + 1)
        gate1.far(1, 2, 3)
        pooled, pooled_low, hid_t, low_t, bias, mask = prepare(hidden, lengths, key_mask)
        rates = correction()
        token = gate1.plane(pooled_low, rates)
        gate2 = Gather(me, third, C + 1, (True, False))
        near = (gate2.far(1, then=token), gate2.far(2, then=token))
        token = gate1.plane_again(near)
        last = gate2.far(3, then=token)
        token = gate1.cores(last)
        token = gate2.plane(token)
        weights = gate1.result()
        low = after(pooled_low, token)
        steps = B * G
        stops = (steps // 4, steps - 1, steps)
        held = attend(0, stops[0], hidden, low, weights, table, bias)
        low = after(low, gate2.plane_again(held[0]))
        held = attend(stops[0], stops[1], hidden, low, weights, table, bias, held)
        low = after(low, gate2.cores(held[0]))
        held = attend(stops[1], stops[2], hidden, low, weights, table, bias, held)
        w_eo, w2 = gate2.result(held[0])
    else:
        cut = lambda a, c: a.astype(BF).reshape(r, -1, c).transpose(1, 0, 2)
        small_t = jnp.pad(small_params.T, ((0, 0), (0, GC - V))).astype(BF)[None]
        cols = [cut(attention_weight[i], GC) for i in range(4)]
        full = lambda a: lax.all_gather(a, ALL, axis=1, tiled=True)
        first = full(jnp.concatenate(cols[:2] + [small_t] + cols[2:], axis=0))
        w_eo = full(jnp.concatenate([cut(expand_weight, FC), cut(attention_weight[4], FC)], axis=0))
        w2 = lax.all_gather(contract_weight.astype(BF), ALL, axis=0, tiled=True)
        weights = (first[: 2 * G + 1], first[2 * G + 1 :])
        pooled, pooled_low, hid_t, low_t, bias, mask = prepare(hidden, lengths, key_mask)
        rates = correction()
        held = attend(0, B * G, hidden, pooled_low, weights, table, bias)
    ctx, probs, qu, qw, keys, values, rel = held
    small = weights[0]
    out, y1, n1, s1, slope, dx2, e2, sums2, *d_contract = mlp(me, ctx, pooled, cotangent, mask, w_eo, w2, small, fast)

    def backward(g, dctx, plan=None):
        return attend_back(me, g, probs, dctx, qu, qw, keys, values, rel, hid_t, low_t, table_t, plan)

    def hidden_grad(back, dx1):
        return input_grad([b[0] for b in back], [b[1] for b in back], [b[2] for b in back], dx1, weights, at)

    if not fast:
        scatter = lambda a, d: lax.psum_scatter(a, ALL, scatter_dimension=d, tiled=True)
        e1, dx1, ea, dctx, sums1, db1 = mlp_back(dx2, e2, slope, n1, s1, w_eo, w2, small)
        back = [backward(g, dctx) for g in range(G)]
        in_grad = hidden_grad(back, dx1)
        d_att = jnp.concatenate([b[3] for b in back], axis=2)
        d_att = jnp.concatenate([d_att, outer(me, ctx, ea, 384)[None]], axis=0)
        d_small = jnp.concatenate([b[-1][0:3] for b in back], axis=1)
        d_small = jnp.concatenate([d_small, sums1[0:3], sums2[0:3], db1.reshape(-1, D)], axis=0)
        attention_terms, attention_plan = [scatter(d_att, 1)], None
        expand_terms, expand_plan = [scatter(outer(me, y1, e1, FC), 0)], None
        contract_terms = [scatter(d_contract[0], 0)]
        contract_up = update(rates, contract_weight, mean_contract, square_contract, contract_terms)
        small_grad = scatter(d_small, 1)
    else:
        half0, half1 = tuple(d_contract[:2]), tuple(d_contract[2:])
        sum1 = Reduction([half0], [half1])
        e1, dx1, ea, dctx, sums1, db1 = mlp_back(dx2, e2, slope, n1, s1, w_eo, w2, small)
        sum1.cross(e1)
        wide0, wide1 = wide_outer(me, after(y1, sum1.token), e1, ctx, ea)
        sum1.cross(wide0)
        wide0, wide1 = after((wide0, wide1), sum1.token)
        sum2 = Reduction([wide0], [wide1])
        sum2.cross()
        back = [backward(0, after(dctx, sum1.token, sum2.token), (0, 0, 0, 0))]
        sum2.cross(back[0][0])
        sum1.along(sum2.token)
        back.append(backward(1, after(dctx, sum1.token, sum2.token), (1, 1, 1, 1)))
        sum2.along(back[1][0])
        every = slice(None)
        r2 = contract_weight.shape[0] // 2
        contract_plan = [(0, 1, i, (slice(i * r2, (i + 1) * r2), every)) for i in range(2)]
        terms1 = settle(after(sum1.terms, sum2.token))
        grads0, grads1 = after((tuple(back[0][3:5]), tuple(back[1][3:5])), terms1)
        sum3 = Reduction([grads0], [grads1])
        sum3.cross()
        back.append(backward(2, after(dctx, sum3.token), (0, 0, 1, 1)))
        terms2 = settle(after(sum2.terms, back[2][0]))
        sum3.cross(terms2)
        d_small = small_deal(me, [b[-1] for b in back], sums1, sums2, after(db1, sum3.token))
        sum4 = Reduction([tuple(back[2][3:5]), tuple(d_small)], [tuple(back[2][5:7])])
        sum4.cross()
        contract_up = update(rates, contract_weight, mean_contract, square_contract, [after(terms1, sum4.token)], contract_plan)
        sum3.along(sum4.token, contract_up[0])
        sum4.cross(sum3.token)
        expand_weight, dx1 = after((expand_weight, dx1), sum4.token)
        in_grad = hidden_grad(back, dx1)
        terms3 = settle(after(sum3.terms, in_grad))
        sum4.along(terms3)
        expand_terms = [terms2]
        per = F // GC // 2
        narrow = lambda j: slice(j * GC, (j + 1) * GC)
        expand_plan = [(0, 1, j + (G if j >= per else 0), (every, narrow(j))) for j in range(2 * per)]
        attention_terms = [terms2, terms3] + sum4.terms
        attention_plan = [(0, 1, per + j, (4, every, narrow(j))) for j in range(G)]
        attention_plan += [(1, 1, 4 * g + m, (m, every, narrow(g))) for g in range(2) for m in range(4)]
        attention_plan += [(2, 4, m + (m > 1), (m, every, narrow(2))) for m in range(4)]
        attention_up, small_up = last_update(
            rates, (attention_weight, mean_attention, square_attention), (small_params, mean_small, square_small),
            attention_terms, attention_plan, (2, 4, 2))
    expand_up = update(rates, expand_weight, mean_expand, square_expand, expand_terms, expand_plan)
    if not fast:
        attention_up = update(rates, attention_weight, mean_attention, square_attention, attention_terms, attention_plan)
        small_up = update(rates, small_params, mean_small, square_small, [small_grad])
    ups = (attention_up, expand_up, contract_up, small_up)
    return (out, in_grad) + tuple(u[i] for i in range(4) for u in ups)


def solution(mesh):
    outer_rows = P(ALL, None)
    middle = P(None, ALL, None)
    inner_cols = P(None, ALL)
    table = (middle, outer_rows, outer_rows, inner_cols)
    tokens = P(ALL, None, None)
    in_specs = (tokens, P(ALL), outer_rows, tokens) + table * 3 + (P(), P())
    out_specs = (tokens, tokens) + table * 4
    fast = mesh.shape["dp"] == 8 and mesh.shape["fsdp"] == 4
    return jax.shard_map(
        functools.partial(shards, fast), mesh=mesh, in_specs=in_specs, out_specs=out_specs, check_vma=False
    )
```

```python
import functools
import math

import jax
import jax.numpy as jnp
import ml_dtypes
import numpy as np
from jax import lax
from jax.experimental import pallas as pl
from jax.experimental.pallas import tpu as pltpu
from jax.sharding import PartitionSpec as P

HEAD = 64
GC = 256
GH = GC // HEAD
TILE = 16
FC = 768
EPSILON = 1e-06
MASK_FILL = -1000000000.0
ALL = ("dp", "fsdp")
F32 = jnp.float32
BF = jnp.bfloat16
NT = (((1,), (1,)), ((), ()))
TN = (((0,), (0,)), ((), ()))


def dot(a, b):
    return jnp.dot(a, b, preferred_element_type=F32)


def dot_nt(a, b):
    return lax.dot_general(a, b, NT, preferred_element_type=F32)


def dot_tn(a, b):
    return lax.dot_general(a, b, TN, preferred_element_type=F32)


def sds(shape, dtype):
    return jax.ShapeDtypeStruct(shape, dtype)


def seqs(*tail):
    return pl.BlockSpec((1,) + tail, lambda s, *_: (s,) + (0,) * len(tail))


def whole(*shape):
    return pl.BlockSpec(shape, lambda *_: (0,) * len(shape), pipeline_mode=pl.Buffered(1))


def turned_small(width):
    return pl.BlockSpec((1, width, GC), lambda s: (2 * width // GC, 0, 0), pipeline_mode=pl.Buffered(1))


def params(mib):
    return pltpu.CompilerParams(vmem_limit_bytes=mib << 20)


def cost(us):
    return pl.CostEstimate(flops=int(us * 1.1e9), bytes_accessed=int(us * 3.5e6), transcendentals=0)


def rel_table(length, width):
    places = length - np.arange(2 * length, dtype=np.float32)
    half_width = width // 2
    frequency = np.exp(np.arange(half_width, dtype=np.float32) * np.float32(-2.0 * math.log(10000.0) / width))
    angles = places[:, None] * frequency[None, :]
    return np.concatenate([np.sin(angles), np.cos(angles)], axis=1).astype(ml_dtypes.bfloat16)


X, Y, CORE, Z = 1, 2, 4, 8
HALVES = ((X, Y), (Y, X))


def pairs(bit):
    return [(d, d ^ bit) for d in range(32)]


def swap(a, bit):
    return lax.ppermute(a, ALL, pairs(bit))


def flat_of(rel, half):
    low, high = HALVES[half]
    return (rel & 3) * Z + (rel >> 2 & 1) * low + (rel >> 3 & 1) * high + (rel >> 4 & 1) * CORE


def after(x, *earlier):
    return lax.optimization_barrier((x, earlier))[0]


def assemble_kernel(stacked, me_ref, *refs):
    ins, outs = refs[:8], refs[8:]
    for half in range(2):
        for rel in range(32):
            k = jnp.bitwise_xor(me_ref[0], flat_of(rel, half))
            src = ins[4 * half + rel // 8]
            for i in range(src.shape[1]):
                if stacked[half]:
                    outs[half][i, k] = src[rel % 8, i]
                else:
                    outs[half][k, i] = src[rel % 8, i]


def small_call(body, shapes, dtype, *ins, mib=32):
    return pl.pallas_call(
        body,
        in_specs=[pl.BlockSpec(memory_space=pltpu.VMEM)] * len(ins),
        out_specs=[pl.BlockSpec(memory_space=pltpu.VMEM)] * len(shapes),
        out_shape=[sds(shape, dtype) for shape in shapes],
        cost_estimate=cost(2),
        compiler_params=params(mib),
    )(*ins)


def halve(parts, split, mib=32):
    n, r, c = parts[0].shape

    def body(*refs):
        first, second = refs[-2:]
        for k, ref in enumerate(refs[:-2]):
            first[k] = ref[:split]
            second[k] = ref[split:]

    return small_call(body, [(len(parts), split, r, c), (len(parts), n - split, r, c)], parts[0].dtype, *parts, mib=mib)


def double(halves, got):
    def body(a, b, a_got, b_got, a_out, b_out):
        for mine, other, out in ((a, a_got, a_out), (b, b_got, b_out)):
            m = mine.shape[0]
            out[:m] = mine[...]
            out[m:] = other[...]

    shapes = [(2 * h.shape[0],) + h.shape[1:] for h in halves]
    return small_call(body, shapes, halves[0].dtype, *halves, *got)


def parcels(attention, expand, contract, small):
    r, F = expand.shape
    V = small.shape[0]
    C = F // FC
    G = attention.shape[2] // GC

    def near_body(att_ref, small_ref, out, pad):
        pad[...] = jnp.zeros_like(pad)
        pad[0:V, 0:r] = small_ref[...]
        turned = pad[...].T
        for g in range(G):
            for i, m in ((0, 0), (G, 1), (2 * G + 1, 2), (3 * G + 1, 3)):
                out[i + g] = att_ref[m, :, g * GC : (g + 1) * GC].astype(BF)
        out[2 * G] = jnp.concatenate([turned[0:r, :], jnp.zeros((r, GC - 128), F32)], axis=1).astype(BF)

    def wide_body(att_ref, exp_ref, con_ref, out):
        for i in range(C):
            out[i] = exp_ref[:, i * FC : (i + 1) * FC].astype(BF)
            out[C + 1 + i] = con_ref[i * r : (i + 1) * r, :].astype(BF)
        out[C] = att_ref[4].astype(BF)

    near = pl.pallas_call(
        near_body,
        in_specs=[pl.BlockSpec(memory_space=pltpu.VMEM)] * 2,
        out_specs=pl.BlockSpec(memory_space=pltpu.VMEM),
        out_shape=sds((4 * G + 1, r, GC), BF),
        scratch_shapes=[pltpu.VMEM((128, 128), F32)],
        cost_estimate=cost(1),
        compiler_params=params(58),
    )(attention, small)
    far = lambda gate: small_call(wide_body, [(2 * C + 1, r, FC)], BF, after(attention, gate), expand, contract, mib=58)[0]
    return near, far


class Gather:
    def __init__(self, me, part, split, stacked=(True, True)):
        self.me, self.part, self.split, self.stacked = me, part, split, stacked
        self.along = [part]

    def far(self, *ks, then=()):
        part = after(self.part, then) if then else self.part
        self.along += [swap(part, k * Z) for k in ks]
        return self.along[-1]

    def plane(self, *earlier):
        along = after(self.along, *earlier) if earlier else self.along
        self.halves = halve(along, self.split, 32 if self.part.shape[2] == GC else 58)
        self.got = [swap(h, HALVES[i][0]) for i, h in enumerate(self.halves)]
        return self.halves

    def plane_again(self, *earlier):
        halves, got = after((self.halves, self.got), *earlier) if earlier else (self.halves, self.got)
        self.firsts = double(halves, got)
        self.seconds = [swap(h, HALVES[i][1]) for i, h in enumerate(self.firsts)]
        return self.firsts

    def cores(self, *earlier):
        firsts, seconds = after((self.firsts, self.seconds), *earlier) if earlier else (self.firsts, self.seconds)
        self.pieces = []
        for f, s in zip(firsts, seconds):
            self.pieces += [f, s, swap(f, CORE), swap(s, CORE)]
        return firsts, seconds

    def result(self, *earlier):
        pieces = after(self.pieces, *earlier) if earlier else self.pieces
        n, r, c = self.part.shape
        wide = 128 if c == GC else 384
        counts = [self.split, n - self.split]
        specs = [pl.BlockSpec((8, m, r, wide), lambda j: (0, 0, 0, j)) for m in counts for _ in range(4)]
        shapes, outs = [], []
        for m, stacked in zip(counts, self.stacked):
            lead = (m, 32) if stacked else (32, m)
            shapes.append(sds(lead + (r, c), self.part.dtype))
            outs.append(pl.BlockSpec(lead + (r, wide), lambda j: (0, 0, 0, j)))
        out = pl.pallas_call(
            functools.partial(assemble_kernel, self.stacked),
            grid=(c // wide,),
            in_specs=[pl.BlockSpec(memory_space=pltpu.SMEM)] + specs,
            out_specs=outs,
            out_shape=shapes,
            cost_estimate=cost(4),
            compiler_params=params(50 if c > GC else 58),
        )(self.me, *pieces)
        return [o.reshape(m, 32 * r, c) if stacked else o.reshape(32 * m * r, c) for o, m, stacked in zip(out, counts, self.stacked)]


def join_kernel(plan, *refs):
    n = 1 + max(w for blocks in plan for _, terms in blocks for w, _ in terms)
    ins, outs = refs[:n], refs[n:]
    for out, blocks in zip(outs, plan):
        for place, terms in blocks:
            total = None
            for w, at in terms:
                v = ins[w][at].astype(F32)
                total = v if total is None else total + v
            out[place] = total.astype(BF)


def join(plan, shapes, ins):
    return pl.pallas_call(
        functools.partial(join_kernel, plan),
        in_specs=[pl.BlockSpec(memory_space=pltpu.VMEM)] * len(ins),
        out_specs=[pl.BlockSpec(memory_space=pltpu.VMEM)] * len(shapes),
        out_shape=[sds(shape, BF) for shape in shapes],
        cost_estimate=cost(1),
        compiler_params=params(32),
    )(*ins)


def settle(terms):
    def body(*refs):
        total = refs[0][...].astype(F32)
        for ref in refs[1:-1]:
            total += ref[...].astype(F32)
        refs[-1][...] = total

    return small_call(body, [terms[0].shape], F32, *terms)[0]


class Reduction:
    def __init__(self, *halves):
        self.halves = []
        for h, parts in enumerate(halves):
            self.halves.append([(k, swap(s, CORE)) for k, s in parts])
        self.token = None

    def add(self, *halves):
        for mine, parts in zip(self.halves, halves):
            mine += [(k, swap(s, CORE)) for k, s in parts]

    def flat(self, earlier):
        halves = after(self.halves, *earlier) if earlier else self.halves
        ins, at = [], []
        for parts in halves:
            blocks = []
            for terms in parts:
                blocks += [[(len(ins) + t, b) for t in range(len(terms))] for b in range(terms[0].shape[1])]
                ins += terms
            at.append(blocks)
        return ins, at, ins[0].shape[2:]

    def cross(self, *earlier):
        ins, at, tail = self.flat(earlier)
        n = ins[0].shape[0] // 2
        bit = 1 if n == 8 else 0
        plan, shapes = [], []
        for blocks in at:
            for far in range(2):
                plan.append([((j, b), [(w, (far * n + j, i)) for w, i in terms]) for j in range(n) for b, terms in enumerate(blocks)])
                shapes.append((n, len(blocks)) + tail)
        out = join(plan, shapes, ins)
        self.halves = [[(out[2 * h], swap(out[2 * h + 1], HALVES[h][bit]))] for h in range(2)]
        self.token = out

    def direct(self, *earlier):
        ins, at, tail = self.flat(earlier)
        count = sum(len(blocks) for blocks in at)
        plan = []
        for q in range(4):
            places = []
            b = 0
            for h, blocks in enumerate(at):
                lead = 4 * (q if h == 0 else (q >> 1) + 2 * (q & 1))
                for terms in blocks:
                    places += [((j, b), [(w, (lead + j, i)) for w, i in terms]) for j in range(4)]
                    b += 1
            plan.append(places)
        out = join(plan, [(4, count) + tail] * 4, ins)
        self.halves = [[tuple([out[0]] + [swap(out[q], (q & 1) * X + (q >> 1) * Y) for q in range(1, 4)])]]
        self.token = out

    def along(self, *earlier, also=()):
        groups = [r.flat(earlier) for r in (self,) + tuple(also)]
        ins, places, tail = [], [[] for _ in range(4)], groups[0][2]
        b = 0
        for more, at, _ in groups:
            base = len(ins)
            ins += more
            for blocks in at:
                for terms in blocks:
                    for k in range(4):
                        places[k].append((b, [(base + w, (k, i)) for w, i in terms]))
                    b += 1
        out = join(places, [(b,) + tail] * 4, ins)
        self.terms = [out[0]] + [swap(out[k], k * Z) for k in range(1, 4)]
        self.token = out


def prepare_kernel(lengths_ref, hidden_ref, key_ref, pooled_ref, low_ref, hidt_ref, lowt_ref, bias_ref, mask_ref, wide):
    hid = hidden_ref[0]
    half, L = pooled_ref.shape[1], hid.shape[0]
    hidt_ref[0] = hid.T
    columns = []
    for i in range(wide.shape[0]):
        wide[i] = hid[:, i * 128 : (i + 1) * 128].astype(F32)
        columns.append((wide[i, pl.ds(0, half, stride=2), :] + wide[i, pl.ds(1, half, stride=2), :]) * 0.5)
    pooled = jnp.concatenate(columns, axis=1)
    pooled_ref[0] = pooled
    low = pooled.astype(BF)
    low_ref[0] = low
    lowt_ref[0] = low.T
    place = lax.broadcasted_iota(jnp.int32, (1, L), 1)
    valid = (key_ref[pl.ds(pl.program_id(0), 1), :] == 1) & (place < lengths_ref[pl.program_id(0)])
    bias_ref[0] = jnp.where(valid, 0.0, MASK_FILL)
    twice = 2 * lax.broadcasted_iota(jnp.int32, (half, L), 0)
    token = lax.broadcasted_iota(jnp.int32, (half, L), 1)
    of = ((token == twice) | (token == twice + 1)).astype(F32).astype(BF)
    rows = jnp.broadcast_to(valid.astype(F32), (16, L)).astype(BF)
    mask_ref[0] = jnp.minimum(dot_nt(of, rows)[:, 0:1], 1.0)


def prepare(hidden, lengths, key_mask):
    B, L, D = hidden.shape
    R = L // 2
    return pl.pallas_call(
        prepare_kernel,
        grid=(B,),
        in_specs=[pl.BlockSpec(memory_space=pltpu.SMEM), seqs(L, D), whole(B, L)],
        out_specs=[seqs(R, D), seqs(R, D), seqs(D, L), seqs(D, R), seqs(1, L), seqs(R, 1)],
        out_shape=[sds((B, R, D), F32), sds((B, R, D), BF), sds((B, D, L), BF), sds((B, D, R), BF), sds((B, 1, L), F32),
                   sds((B, R, 1), F32)],
        scratch_shapes=[pltpu.VMEM((D // 128, L, 128), F32)],
        cost_estimate=cost(6),
        compiler_params=params(58),
    )(lengths, hidden, key_mask)


def attend_kernel(start, per, hidden_ref, pooled_ref, wq_ref, wk_ref, wv_ref, wr_ref, table_ref, small_ref, bias_ref, *refs):
    ctx_ref, probs_ref, qu_ref, qw_ref, keys_ref, values_ref, rel_out, rel_ref = refs[-8:]
    half = hidden_ref.shape[1] // 2
    blk = half // 2
    step = pl.program_id(0)

    @pl.when((step == 0) | (lax.rem(start + step, per) == 0))
    def _():
        rel = dot(table_ref[...], wr_ref[0]).astype(BF)
        rel_ref[...] = rel
        rel_out[...] = rel

    hid = hidden_ref[0]
    small_ref = small_ref[0, :, 0:128].astype(F32).T
    q = dot(pooled_ref[0], wq_ref[0])
    qu = (q + small_ref[0:1, :]).astype(BF)
    qw = (q + small_ref[1:2, :]).astype(BF)
    qu_ref[0] = qu
    qw_ref[0] = qw
    keys_ref[0] = dot(hid, wk_ref[0]).astype(BF)
    values_ref[0] = (dot(hid, wv_ref[0]) + small_ref[2:3, :]).astype(BF)
    bias = bias_ref[0]
    lane = lax.broadcasted_iota(jnp.int32, (1, GC), 1)
    masks = [(lane >= h * HEAD) & (lane < (h + 1) * HEAD) for h in range(GH)]
    qu8 = qu.astype(F32) * 0.125
    qw8 = qw.astype(F32) * 0.125
    wide = 2 * half + 128
    for b in range(2):
        rows = slice(b * blk, (b + 1) * blk)
        m0 = half * (1 - b)
        quh = jnp.concatenate([jnp.where(m, qu8[rows], 0.0).astype(BF) for m in masks], axis=0)
        qwh = jnp.concatenate([jnp.where(m, qw8[rows], 0.0).astype(BF) for m in masks], axis=0)
        content = dot_nt(quh, keys_ref[0])
        placed = dot_nt(qwh, rel_ref[m0 : m0 + 3 * half, :])
        lows = []
        for h in range(GH):
            for r in range(0, blk, TILE):
                hr = slice(h * blk + r, h * blk + r + TILE)
                at = half - 128 - 2 * r // 128 * 128
                moved = pltpu.roll(placed[hr, at : at + wide], 2 * r % 128, 1, stride=2, stride_axis=0)[:, 128:]
                s = content[hr] + moved + bias
                top = jnp.max(s, axis=-1, keepdims=True)
                e = jnp.exp(s - top)
                p = e * (1.0 / jnp.sum(e, axis=-1, keepdims=True))
                probs_ref[0, 0, h, b * blk + r : b * blk + r + TILE, :] = p
                lows.append(p.astype(BF))
        c = dot(jnp.concatenate(lows, axis=0), values_ref[0])
        total = c[0:blk]
        for h in range(1, GH):
            total = jnp.where(masks[h], c[h * blk : (h + 1) * blk], total)
        ctx_ref[0, rows, :] = total.astype(BF)


def attend(start, stop, hidden, pooled_low, weights, table, bias, held=None):
    B, L, D = hidden.shape
    R = L // 2
    G = D // GC
    g = lambda i: (start + i) // B
    s = lambda i: lax.rem(start + i, B)
    seq = lambda r: pl.BlockSpec((1, r, D), lambda i: (s(i), 0, 0))
    mat = lambda base: pl.BlockSpec((1, D, GC), lambda i: (base + g(i), 0, 0))
    so = lambda r: pl.BlockSpec((1, r, GC), lambda i: (s(i), 0, g(i)))
    a, b = weights
    ins = [hidden, pooled_low, a, a, b, b, table, a, bias]
    specs = [seq(L), seq(R), mat(0), mat(G), mat(0), mat(G), whole(2 * L, D),
             pl.BlockSpec((1, GC, GC), lambda i: (2 * G, g(i), 0)), pl.BlockSpec((1, 1, L), lambda i: (s(i), 0, 0))]
    aliases = {}
    if held is not None:
        aliases = {len(ins) + i: i for i in range(7)}
        ins += list(held)
        specs += [pl.BlockSpec(memory_space=pl.ANY)] * 7
    return pl.pallas_call(
        functools.partial(attend_kernel, start, B),
        grid=(stop - start,),
        in_specs=specs,
        out_specs=[so(R), pl.BlockSpec((1, 1, GH, R, L), lambda i: (s(i), g(i), 0, 0, 0)), so(R), so(R), so(L), so(L),
                   pl.BlockSpec((2 * L, GC), lambda i: (0, g(i)))],
        out_shape=[sds((B, R, D), BF), sds((B, G, GH, R, L), F32), sds((B, R, D), BF), sds((B, R, D), BF),
                   sds((B, L, D), BF), sds((B, L, D), BF), sds((2 * L, D), BF)],
        scratch_shapes=[pltpu.VMEM((2 * L, GC), BF)],
        input_output_aliases=aliases,
        cost_estimate=cost(4 * (stop - start)),
        compiler_params=params(58),
    )(*ins)


def phi_and_slope(z):
    e = jnp.exp(z * z * (-0.5))
    t = 1.0 / (1.0 + (0.3275911 * 0.7071067811865476) * jnp.abs(z))
    poly = t * (0.127414796 + t * (-0.142248368 + t * (0.7107068705 + t * (-0.7265760135 + t * 0.5307027145))))
    tail = poly * e
    phi = jnp.where(z >= 0, 1.0 - tail, tail)
    return phi, phi + z * e * 0.3989422804014327


def norm(x):
    center = x - jnp.mean(x, axis=-1, keepdims=True)
    inv = lax.rsqrt(jnp.mean(center * center, axis=-1, keepdims=True) + EPSILON)
    return center * inv, inv


def norm_back(e, n, inv):
    return inv * (e - jnp.mean(e, axis=-1, keepdims=True) - n * jnp.mean(e * n, axis=-1, keepdims=True))


def add_rows(ref, *values):
    for k, v in enumerate(values):
        ref[k : k + 1, :] += jnp.sum(v, axis=0, keepdims=True)


def mlp_kernel(dealt, *refs):
    me_ref, ctx_ref, pooled_ref, cot_ref, mask_ref, exp_ref, w2_ref, turned_ref = refs[:8]
    out_ref, y1_ref, n1_ref, s1_ref, slope_ref, dx2_ref, e2_ref, sums_ref = refs[8:16]
    grads, (small_ref, inner_ref, e2_all, total) = refs[16:-4], refs[-4:]
    rows_here = pooled_ref.shape[1]
    mine = pl.ds(pl.multiple_of(pl.program_id(0) * rows_here, 16), rows_here)
    @pl.when(pl.program_id(0) == 0)
    def _():
        sums_ref[...] = jnp.zeros_like(sums_ref)
        small_ref[...] = turned_ref[0, :, 0:128].astype(F32).T

    row = lambda k: small_ref[k : k + 1, :]
    chunks = exp_ref.shape[0] - 1
    x1 = pooled_ref[0] + dot(ctx_ref[0], exp_ref[chunks]) + row(3)
    n1, inv1 = norm(x1)
    n1_ref[0] = n1
    s1_ref[0] = inv1
    y1 = n1 * row(4) + row(5)
    y1l = y1.astype(BF)
    y1_ref[0] = y1l
    x2 = y1 + row(6)
    for c in range(chunks):
        cs = slice(c * FC, (c + 1) * FC)
        z = dot(y1l, exp_ref[c]) + row(9 + c)
        phi, slope = phi_and_slope(z)
        inner = (z * phi).astype(BF)
        inner_ref[mine, cs] = inner
        slope_ref[0, :, cs] = slope
        x2 += dot(inner, w2_ref[cs, :])
    n2, inv2 = norm(x2)
    m = mask_ref[0]
    out_ref[0] = ((n2 * row(7) + row(8)) * m).astype(BF)
    dy2 = cot_ref[0].astype(F32) * m
    dx2 = norm_back(dy2 * row(7), n2, inv2)
    dx2_ref[0] = dx2
    e2 = dx2.astype(BF)
    e2_ref[0] = e2
    add_rows(sums_ref, dx2, dy2 * n2, dy2)
    e2_all[mine, :] = e2

    @pl.when(pl.program_id(0) == pl.num_programs(0) - 1)
    def _():
        for c in range(chunks):
            cs = slice(c * FC, (c + 1) * FC)
            v = dot_tn(inner_ref[:, cs], e2_all[...])
            if not dealt:
                grads[0][cs, :] = v
            else:
                total[cs, :] = v
        if dealt:
            r = grads[0].shape[2]
            for half in range(2):
                for rel in range(32):
                    k = jnp.bitwise_xor(me_ref[0], flat_of(rel, half))
                    at = pl.multiple_of(k * (2 * r) + half * r, 8)
                    grads[2 * half + rel // 16][rel % 16, 0] = total[pl.ds(at, r), :].astype(BF)


def mlp(me, ctx, pooled, cot, mask, expand, w2, small, dealt):
    B, R, D = pooled.shape
    F = w2.shape[0]
    grads = [sds((16, 1, F // 64, D), BF)] * 4 if dealt else [sds((F, D), F32)]
    return pl.pallas_call(
        functools.partial(mlp_kernel, dealt),
        grid=(B,),
        in_specs=[pl.BlockSpec(memory_space=pltpu.SMEM), seqs(R, D), seqs(R, D), seqs(R, D), seqs(R, 1), whole(*expand.shape), whole(F, D),
                  turned_small(D)],
        out_specs=[seqs(R, D), seqs(R, D), seqs(R, D), seqs(R, 1), seqs(R, F), seqs(R, D), seqs(R, D),
                   pl.BlockSpec((8, D), lambda s: (0, 0))] + [whole(*g.shape) for g in grads],
        out_shape=[sds((B, R, D), BF), sds((B, R, D), BF), sds((B, R, D), F32), sds((B, R, 1), F32),
                   sds((B, R, F), F32), sds((B, R, D), F32), sds((B, R, D), BF), sds((8, D), F32)] + grads,
        scratch_shapes=[pltpu.VMEM((128, D), F32), pltpu.VMEM((B * R, F), BF), pltpu.VMEM((B * R, D), BF), pltpu.VMEM((F, D), F32)],
        cost_estimate=cost(38),
        compiler_params=params(50),
    )(me, ctx, pooled, cot, mask, expand, w2, small)


def mlp_back_kernel(dx2_ref, e2_ref, slope_ref, n1_ref, s1_ref, exp_ref, w2_ref, turned_ref,
                    e1_ref, dx1_ref, ea_ref, dctx_ref, sums_ref, db1_ref, small_ref):
    @pl.when(pl.program_id(0) == 0)
    def _():
        small_ref[...] = turned_ref[0, :, 0:128].astype(F32).T
        sums_ref[...] = jnp.zeros_like(sums_ref)
        db1_ref[...] = jnp.zeros_like(db1_ref)

    chunks = exp_ref.shape[0] - 1
    e2 = e2_ref[0]
    dy1 = dx2_ref[0]
    for c in range(chunks):
        cs = slice(c * FC, (c + 1) * FC)
        dz = dot_nt(e2, w2_ref[cs, :]) * slope_ref[0, :, cs]
        db1_ref[:, cs] += jnp.sum(dz, axis=0, keepdims=True)
        e1 = dz.astype(BF)
        e1_ref[0, :, cs] = e1
        dy1 += dot_nt(e1, exp_ref[c])
    n1 = n1_ref[0]
    dx1 = norm_back(dy1 * small_ref[4:5, :], n1, s1_ref[0])
    dx1_ref[0] = dx1
    ea = dx1.astype(BF)
    ea_ref[0] = ea
    dctx_ref[0] = dot_nt(ea, exp_ref[chunks]).astype(BF)
    add_rows(sums_ref, dx1, dy1 * n1, dy1)


def mlp_back(dx2, e2, slope, n1, s1, expand, w2, small):
    B, R, D = dx2.shape
    F = w2.shape[0]
    return pl.pallas_call(
        mlp_back_kernel,
        grid=(B,),
        in_specs=[seqs(R, D), seqs(R, D), seqs(R, F), seqs(R, D), seqs(R, 1), whole(*expand.shape), whole(F, D),
                  turned_small(D)],
        out_specs=[seqs(R, F), seqs(R, D), seqs(R, D), seqs(R, D), pl.BlockSpec((8, D), lambda s: (0, 0)),
                   pl.BlockSpec((1, F), lambda s: (0, 0))],
        out_shape=[sds((B, R, F), BF), sds((B, R, D), F32), sds((B, R, D), BF), sds((B, R, D), BF), sds((8, D), F32),
                   sds((1, F), F32)],
        scratch_shapes=[pltpu.VMEM((128, D), F32)],
        cost_estimate=cost(21),
        compiler_params=params(50),
    )(dx2, e2, slope, n1, s1, expand, w2, small)


def deal(half, me, total_ref, put):
    r = total_ref.shape[0] // 32
    for rel in range(32):
        k = jnp.bitwise_xor(me, flat_of(rel, half))
        put(rel // 16, rel % 16, total_ref[pl.ds(pl.multiple_of(k * r, 8), r), :].astype(BF))


def outer_kernel(half, me_ref, a_ref, b_ref, keep_ref, send_ref, turned, total):
    B, R, M = a_ref.shape

    @pl.when(pl.program_id(0) == 0)
    def _():
        turned[...] = a_ref[...].reshape(B * R, M).T

    total[...] = dot(turned[...], b_ref[...].reshape(B * R, b_ref.shape[2]))

    def put(sent, i, v):
        for j in range(v.shape[1] // GC):
            (send_ref if sent else keep_ref)[i, j] = v[:, j * GC : (j + 1) * GC]

    deal(half, me_ref[0], total, put)


def outer_plain_kernel(a_ref, b_ref, out_ref):
    B, R, M = a_ref.shape
    out_ref[...] = dot_tn(a_ref[...].reshape(B * R, M), b_ref[...].reshape(B * R, b_ref.shape[2]))


def outer(me, a, b, cols, half=None, blocks=None):
    B, R, M = a.shape
    N = b.shape[2]
    first, count = blocks or (0, N // cols)
    specs = [pl.BlockSpec((B, R, M), lambda j: (0, 0, 0)), pl.BlockSpec((B, R, cols), lambda j: (0, 0, first + j))]
    price = cost(2.0 * count)
    if half is None:
        return pl.pallas_call(
            outer_plain_kernel, grid=(count,), in_specs=specs,
            out_specs=pl.BlockSpec((M, cols), lambda j: (0, j)),
            out_shape=sds((M, N), F32), cost_estimate=price, compiler_params=params(32))(a, b)
    return pl.pallas_call(
        functools.partial(outer_kernel, half),
        grid=(count,),
        in_specs=[pl.BlockSpec(memory_space=pltpu.SMEM)] + specs,
        out_specs=[pl.BlockSpec((16, cols // GC, M // 32, GC), lambda j: (0, j, 0, 0))] * 2,
        out_shape=[sds((16, count * cols // GC, M // 32, GC), BF)] * 2,
        scratch_shapes=[pltpu.VMEM((M, B * R), BF), pltpu.VMEM((M, cols), F32)],
        cost_estimate=price,
        compiler_params=params(32),
    )(me, a, b)


def wide_outer_kernel(chunks, me_ref, y1_ref, e1_ref, ctx_ref, ea_ref, keep0, send0, keep1, send1, turned, total):
    B, R, D = y1_ref.shape
    j = pl.program_id(0)
    flat = lambda ref: ref[...].reshape(B * R, D)

    def dealt(half, base):
        def put(sent, i, v):
            ref = ((keep0, send0), (keep1, send1))[half][sent]
            for b in range(D // GC):
                ref[i, base + b] = v[:, b * GC : (b + 1) * GC]

        deal(half, me_ref[0], total, put)

    @pl.when(j == 0)
    def _():
        turned[...] = flat(y1_ref).T

    @pl.when(j < chunks)
    def _():
        total[...] = dot(turned[...], flat(e1_ref))

    @pl.when(j == chunks)
    def _():
        total[...] = dot_tn(flat(ctx_ref), flat(ea_ref))
        dealt(0, chunks // 2 * (D // GC))

    @pl.when(j < chunks // 2)
    def _():
        dealt(0, j * (D // GC))

    @pl.when((j >= chunks // 2) & (j < chunks))
    def _():
        dealt(1, (j - chunks // 2) * (D // GC))


def wide_outer(me, y1, e1, ctx, ea):
    B, R, D = y1.shape
    F = e1.shape[2]
    chunks = F // D
    n = D // GC
    shapes = [(16, m, D // 32, GC) for m in (chunks // 2 * n + n, chunks // 2 * n) for _ in range(2)]
    out = pl.pallas_call(
        functools.partial(wide_outer_kernel, chunks),
        grid=(chunks + 1,),
        in_specs=[pl.BlockSpec(memory_space=pltpu.SMEM), whole(B, R, D),
                  pl.BlockSpec((B, R, D), lambda j: (0, 0, jnp.minimum(j, chunks - 1))), whole(B, R, D), whole(B, R, D)],
        out_specs=[whole(*shape) for shape in shapes],
        out_shape=[sds(shape, BF) for shape in shapes],
        scratch_shapes=[pltpu.VMEM((D, B * R), BF), pltpu.VMEM((D, D), F32)],
        cost_estimate=cost(12),
        compiler_params=params(40),
    )(me, y1, e1, ctx, ea)
    return tuple(out[:2]), tuple(out[2:])


def small_deal_kernel(me_ref, *refs):
    sums, (sums1, sums2, db1, keep_ref, send_ref, total, turned) = refs[:-7], refs[-7:]
    D = sums1.shape[1]
    total[...] = jnp.zeros_like(total)
    for g, s in enumerate(sums):
        total[0:3, g * GC : (g + 1) * GC] = s[0:3, :]
    total[3:6, :] = sums1[0:3, :]
    total[6:9, :] = sums2[0:3, :]
    for i in range(db1.shape[1] // D):
        total[9 + i : 10 + i, :] = db1[0:1, i * D : (i + 1) * D]
    turned[...] = jnp.concatenate([total[...].T, jnp.zeros((D, GC - total.shape[0]), F32)], axis=1)

    def put(sent, i, v):
        (send_ref if sent else keep_ref)[i, 0] = v

    deal(0, me_ref[0], turned, put)


def small_deal(me, sums, sums1, sums2, db1):
    D = sums1.shape[1]
    n = 4 + len(sums)
    return pl.pallas_call(
        small_deal_kernel,
        in_specs=[pl.BlockSpec(memory_space=pltpu.SMEM)] + [pl.BlockSpec(memory_space=pltpu.VMEM)] * (n - 1),
        out_specs=[pl.BlockSpec(memory_space=pltpu.VMEM)] * 2,
        out_shape=[sds((16, 1, D // 32, GC), BF)] * 2,
        scratch_shapes=[pltpu.VMEM((128, D), F32), pltpu.VMEM((D, GC), F32)],
        cost_estimate=cost(2),
        compiler_params=params(24),
    )(me, *sums, sums1, sums2, db1)


def attend_back_kernel(plan, *refs):
    (me_ref, probs_ref, dctx_ref, qu_ref, qw_ref, keys_ref, values_ref, rel_ref, hidt_ref, lowt_ref, tablet_ref) = refs[:11]
    outs = refs[11 : 14]
    dq_ref, dk_ref, dv_ref = outs
    grads = refs[14 : -8]
    sums_ref = refs[-8]
    acc_q, acc_k, acc_v, acc_r, acc_dv, dkt, dvt = refs[-7:]
    step = pl.program_id(0)
    half, L = probs_ref.shape[3], probs_ref.shape[4]
    blk = half // 2

    @pl.when(step == 0)
    def _():
        for a in (acc_q, acc_k, acc_v, acc_r, acc_dv, sums_ref):
            a[...] = jnp.zeros_like(a)

    across = lax.broadcasted_iota(jnp.int32, (half, half), 0) + lax.broadcasted_iota(jnp.int32, (half, half), 1)
    flip = (across == half - 1).astype(F32).astype(BF)
    lane = lax.broadcasted_iota(jnp.int32, (1, GC), 1)
    dctx = dctx_ref[0]
    dctx_t = dctx.T
    qu_t = qu_ref[0].T
    qwr_t = dot(flip, qw_ref[0]).astype(BF).T
    keys = keys_ref[0]
    values = values_ref[0]
    masks = [(lane >= h * HEAD) & (lane < (h + 1) * HEAD) for h in range(GH)]
    dctx_wide = dctx.astype(F32)
    dp = dot_nt(jnp.concatenate([jnp.where(m, dctx_wide, 0.0).astype(BF) for m in masks], axis=0), values)
    backs = []
    moved = [[], []]
    for h in range(GH):
        sel = slice(h * HEAD, (h + 1) * HEAD)
        draws, lows = [], []
        for r in range(0, half, TILE):
            p = probs_ref[0, 0, h, r : r + TILE, :]
            t = p * dp[h * half + r : h * half + r + TILE]
            draws.append((t - p * jnp.sum(t, axis=-1, keepdims=True)).astype(BF))
            lows.append(p.astype(BF))
        draw = jnp.concatenate(draws, axis=0)
        dvt[sel, :] = dot(dctx_t[sel], jnp.concatenate(lows, axis=0))
        both = dot(jnp.concatenate([qu_t[sel], flip], axis=0), draw)
        dkt[sel, :] = both[:HEAD] * 0.125
        back = both[HEAD:]
        backs.append(back.astype(BF))
        for b in range(2):
            tiles = []
            for r in range(0, blk, TILE):
                x = jnp.concatenate([back[b * blk + r : b * blk + r + TILE], jnp.zeros((TILE, 128), F32)], axis=1)
                x = pltpu.roll(x, 2 + 2 * r % 128, 1, stride=2, stride_axis=0).astype(BF)
                none = jnp.zeros((TILE, 128), BF)
                tiles.append(jnp.concatenate([x, none] if r < blk // 2 else [none, x], axis=1))
            x = jnp.concatenate(tiles, axis=0)
            m0 = half * b
            acc_r[sel, m0 : m0 + 3 * half] += dot(qwr_t[sel, b * blk : (b + 1) * blk], x)
            moved[b].append(x)
    alone = lambda v, n: functools.reduce(lambda t, h: jnp.where(masks[h], v[h * n : (h + 1) * n], t), range(1, GH), v[0:n])
    dqu = alone(dot(jnp.concatenate(backs, axis=0), keys), half)
    dqw = jnp.concatenate(
        [alone(dot(jnp.concatenate(moved[b], axis=0), rel_ref[half * b : half * b + 3 * half, :]), blk) for b in range(2)], axis=0
    )
    dqu = dqu * 0.125
    dqw = dqw * 0.125
    dq = dot(flip, (dqu + dqw).astype(BF)).astype(BF)
    dk = dkt[...].astype(BF).T
    dvf = dvt[...]
    dv = dvf.astype(BF).T
    dq_ref[0] = dq
    dk_ref[0] = dk
    dv_ref[0] = dv
    acc_dv[...] += dvf
    add_rows(sums_ref, dqu, dqw)
    acc_q[...] += dot(lowt_ref[0], dq)
    acc_k[...] += dot(hidt_ref[0], dk)
    acc_v[...] += dot(hidt_ref[0], dv)

    @pl.when(step == pl.num_programs(0) - 1)
    def _():
        sums_ref[2:3, :] = jnp.sum(acc_dv[...].T, axis=0, keepdims=True)
        dr = acc_r[...] * 0.125
        hi = dr.astype(BF)
        lo = (dr - hi.astype(F32)).astype(BF)
        tt = tablet_ref[...]
        if plan is None:
            for i, a in enumerate((acc_q, acc_k, acc_v)):
                grads[0][i] = a[...]
            grads[0][3] = dot_nt(tt, hi) + dot_nt(tt, lo)
        else:
            for i in range(4):
                half = plan[i]
                at = plan[:i].count(half)
                base = 2 * sorted(set(plan)).index(half)
                acc = (acc_q, acc_k, acc_v, acc_q)[i]
                if i == 3:
                    acc_q[...] = dot_nt(tt, hi) + dot_nt(tt, lo)

                def put(sent, j, v):
                    grads[base + sent][j, at] = v

                deal(half, me_ref[0], acc, put)


def attend_back(me, g, probs, dctx, qu, qw, keys, values, rel, hid_t, low_t, table_t, plan=None):
    B, R, D = qu.shape
    L = 2 * R
    so = lambda r: pl.BlockSpec((1, r, GC), lambda s: (s, 0, g))
    if plan is None:
        grad_specs = [pl.BlockSpec((4, D, GC), lambda s: (0, 0, 0))]
        grad_shapes = [sds((4, D, GC), F32)]
    else:
        sizes = [(16, plan.count(h), D // 32, GC) for h in sorted(set(plan)) for _ in range(2)]
        grad_specs = [whole(*size) for size in sizes]
        grad_shapes = [sds(size, BF) for size in sizes]
    return pl.pallas_call(
        functools.partial(attend_back_kernel, plan),
        grid=(B,),
        in_specs=[pl.BlockSpec(memory_space=pltpu.SMEM),
                  pl.BlockSpec((1, 1, GH, R, L), lambda s: (s, g, 0, 0, 0)), so(R), so(R), so(R), so(L), so(L),
                  pl.BlockSpec((2 * L, GC), lambda s: (0, g)), seqs(D, L), seqs(D, R), whole(D, 2 * L)],
        out_specs=[seqs(R, GC), seqs(L, GC), seqs(L, GC)] + grad_specs + [pl.BlockSpec((8, GC), lambda s: (0, 0))],
        out_shape=[sds((B, R, GC), BF), sds((B, L, GC), BF), sds((B, L, GC), BF)] + grad_shapes + [sds((8, GC), F32)],
        scratch_shapes=[pltpu.VMEM((D, GC), F32)] * 3 + [pltpu.VMEM((GC, 2 * L), F32)] + [pltpu.VMEM((GC, L), F32)] * 3,
        cost_estimate=cost(22),
        compiler_params=params(40),
    )(me, probs, dctx, qu, qw, keys, values, rel, hid_t, low_t, table_t)


def input_grad_kernel(at, *refs):
    groups = len(at)
    dqs, dks, dvs = refs[:groups], refs[groups : 2 * groups], refs[2 * groups : 3 * groups]
    dx1_ref, weights, out_ref, wide = refs[3 * groups], refs[3 * groups + 1 : -2], refs[-2], refs[-1]
    half = dx1_ref.shape[1]
    shared = dx1_ref[0]
    total = None
    for g in range(groups):
        wq, wk, wv = (weights[a][i] for a, i in at[g])
        shared += dot_nt(dqs[g][0], wq)
        t = dot_nt(dks[g][0], wk) + dot_nt(dvs[g][0], wv)
        total = t if total is None else total + t
    shared = shared * 0.5
    for i in range(wide.shape[0]):
        cs = slice(i * 128, (i + 1) * 128)
        wide[i, pl.ds(0, half, stride=2), :] = shared[:, cs]
        wide[i, pl.ds(1, half, stride=2), :] = shared[:, cs]
        out_ref[0, :, cs] = (total[:, cs] + wide[i]).astype(BF)


def input_grad(dqs, dks, dvs, dx1, weights, at):
    B, R, D = dx1.shape
    L = 2 * R
    G = len(dqs)
    return pl.pallas_call(
        functools.partial(input_grad_kernel, at),
        grid=(B,),
        in_specs=[seqs(R, GC)] * G + [seqs(L, GC)] * (2 * G) + [seqs(R, D)] + [whole(*w.shape) for w in weights],
        out_specs=seqs(L, D),
        out_shape=sds((B, L, D), BF),
        scratch_shapes=[pltpu.VMEM((D // 128, L, 128), F32)],
        cost_estimate=cost(10),
        compiler_params=params(40),
    )(*dqs, *dks, *dvs, dx1, *weights)


def adamw(weight, moment, second, gradient, rates):
    new_moment = rates[1] * moment + (1.0 - rates[1]) * gradient
    new_second = rates[2] * second + (1.0 - rates[2]) * gradient * gradient
    moment_hat = new_moment / rates[4]
    second_hat = new_second / rates[5]
    new_weight = weight - rates[0] * (moment_hat / (jnp.sqrt(second_hat) + 1e-08) + rates[3] * weight)
    return (new_weight, new_moment, new_second)


def update_kernel(plan, rates_ref, w_ref, m_ref, v_ref, *refs):
    terms, (grad_ref, w_out, m_out, v_out) = refs[:-4], refs[-4:]
    rates = [rates_ref[i] for i in range(6)]
    for first, count, block, dest in plan:
        g = None
        for t in terms[first : first + count]:
            v = (t[...] if block is None else t[block]).astype(F32)
            g = v if g is None else g + v
        grad_ref[dest] = g
        w_out[dest], m_out[dest], v_out[dest] = adamw(w_ref[dest], m_ref[dest], v_ref[dest], g, rates)


def update(rates, w, m, v, terms, plan=None):
    plan = plan or [(0, len(terms), None, (slice(None),) * w.ndim)]
    return pl.pallas_call(
        functools.partial(update_kernel, plan),
        in_specs=[pl.BlockSpec(memory_space=pltpu.SMEM)] + [pl.BlockSpec(memory_space=pltpu.VMEM)] * (3 + len(terms)),
        out_specs=[pl.BlockSpec(memory_space=pltpu.VMEM)] * 4,
        out_shape=[sds(w.shape, F32)] * 4,
        cost_estimate=cost(2),
        compiler_params=params(24),
    )(rates, w, m, v, *terms)


def last_update_kernel(plan, small_at, rates_ref, *refs):
    ins, (pad, *_) = refs[:-9], refs[-1:]
    att, small, terms = ins[:3], ins[3:6], ins[6:]
    outs = refs[-9:-1]
    update_kernel(plan, rates_ref, *att, *terms, *outs[:4])
    first, count, block = small_at
    g = sum(t[block].astype(F32) for t in terms[first : first + count])
    V, r = small[0].shape
    pad[...] = jnp.zeros_like(pad)
    pad[0:r, :] = g[:, 0:128]
    pad[...] = pad[...].T
    rates = [rates_ref[i] for i in range(6)]
    g = pad[0:V, 0:r]
    outs[4][...] = g
    outs[5][...], outs[6][...], outs[7][...] = adamw(small[0][...], small[1][...], small[2][...], g, rates)


def last_update(rates, attention, small, terms, plan, small_at):
    like = [attention[0]] * 4 + [small[0]] * 4
    out = pl.pallas_call(
        functools.partial(last_update_kernel, plan, small_at),
        in_specs=[pl.BlockSpec(memory_space=pltpu.SMEM)] + [pl.BlockSpec(memory_space=pltpu.VMEM)] * (6 + len(terms)),
        out_specs=[pl.BlockSpec(memory_space=pltpu.VMEM)] * 8,
        out_shape=[sds(a.shape, F32) for a in like],
        scratch_shapes=[pltpu.VMEM((128, 128), F32)],
        cost_estimate=cost(3),
        compiler_params=params(24),
    )(rates, *attention, *small, *terms)
    return out[:4], out[4:]


def shards(fast, hidden, lengths, key_mask, cotangent, attention_weight, expand_weight, contract_weight, small_params,
           mean_attention, mean_expand, mean_contract, mean_small,
           square_attention, square_expand, square_contract, square_small, update_step, update_rates):
    B, L, D = hidden.shape
    R = L // 2
    F = expand_weight.shape[1]
    G = D // GC
    C = F // FC
    H = C // 2
    r = attention_weight.shape[1]
    V = small_params.shape[0]
    me = (lax.axis_index("dp") * lax.axis_size("fsdp") + lax.axis_index("fsdp")).astype(jnp.int32).reshape(1)

    table = rel_table(L, D)
    table, table_t = jnp.asarray(table), jnp.asarray(np.ascontiguousarray(table.T))

    def correction():
        return jnp.concatenate([update_rates, 1.0 - jnp.power(update_rates[1:3], update_step[0].astype(F32))])

    at = tuple(((0, g), (0, G + g), (1, g)) for g in range(G))
    if fast:
        first, third = parcels(attention_weight, expand_weight, contract_weight, small_params)
        gate1 = Gather(me, first, 2 * G + 1)
        gate1.far(1, 2, 3)
        pooled, pooled_low, hid_t, low_t, bias, mask = prepare(hidden, lengths, key_mask)
        rates = correction()
        third = third(pooled_low)
        token = gate1.plane(pooled_low, rates, third)
        gate2 = Gather(me, third, C + 1, (True, False))
        near = (gate2.far(1, then=token), gate2.far(2, then=token))
        token = gate1.plane_again(near)
        last = gate2.far(3, then=token)
        token = gate1.cores(last)
        token = gate2.plane(token)
        weights = gate1.result()
        low = after(pooled_low, token)
        steps = B * G
        stops = (steps // 4, steps - 1, steps)
        held = attend(0, stops[0], hidden, low, weights, table, bias)
        low = after(low, gate2.plane_again(held[0]))
        held = attend(stops[0], stops[1], hidden, low, weights, table, bias, held)
        low = after(low, gate2.cores(held[0]))
        held = attend(stops[1], stops[2], hidden, low, weights, table, bias, held)
        w_eo, w2 = gate2.result(held[0])
    else:
        cut = lambda a, c: a.astype(BF).reshape(r, -1, c).transpose(1, 0, 2)
        small_t = jnp.pad(small_params.T, ((0, 0), (0, GC - V))).astype(BF)[None]
        cols = [cut(attention_weight[i], GC) for i in range(4)]
        full = lambda a: lax.all_gather(a, ALL, axis=1, tiled=True)
        first = full(jnp.concatenate(cols[:2] + [small_t] + cols[2:], axis=0))
        w_eo = full(jnp.concatenate([cut(expand_weight, FC), cut(attention_weight[4], FC)], axis=0))
        w2 = lax.all_gather(contract_weight.astype(BF), ALL, axis=0, tiled=True)
        weights = (first[: 2 * G + 1], first[2 * G + 1 :])
        pooled, pooled_low, hid_t, low_t, bias, mask = prepare(hidden, lengths, key_mask)
        rates = correction()
        held = attend(0, B * G, hidden, pooled_low, weights, table, bias)
    ctx, probs, qu, qw, keys, values, rel = held
    small = weights[0]
    out, y1, n1, s1, slope, dx2, e2, sums2, *d_contract = mlp(me, ctx, pooled, cotangent, mask, w_eo, w2, small, fast)

    def backward(g, dctx, plan=None):
        return attend_back(me, g, probs, dctx, qu, qw, keys, values, rel, hid_t, low_t, table_t, plan)

    def hidden_grad(back, dx1):
        return input_grad([b[0] for b in back], [b[1] for b in back], [b[2] for b in back], dx1, weights, at)

    if not fast:
        scatter = lambda a, d: lax.psum_scatter(a, ALL, scatter_dimension=d, tiled=True)
        e1, dx1, ea, dctx, sums1, db1 = mlp_back(dx2, e2, slope, n1, s1, w_eo, w2, small)
        back = [backward(g, dctx) for g in range(G)]
        in_grad = hidden_grad(back, dx1)
        d_att = jnp.concatenate([b[3] for b in back], axis=2)
        d_att = jnp.concatenate([d_att, outer(me, ctx, ea, 384)[None]], axis=0)
        d_small = jnp.concatenate([b[-1][0:3] for b in back], axis=1)
        d_small = jnp.concatenate([d_small, sums1[0:3], sums2[0:3], db1.reshape(-1, D)], axis=0)
        attention_terms, attention_plan = [scatter(d_att, 1)], None
        expand_terms, expand_plan = [scatter(outer(me, y1, e1, FC), 0)], None
        contract_terms = [scatter(d_contract[0], 0)]
        contract_up = update(rates, contract_weight, mean_contract, square_contract, contract_terms)
        small_grad = scatter(d_small, 1)
    else:
        half0, half1 = tuple(d_contract[:2]), tuple(d_contract[2:])
        sum1 = Reduction([half0], [half1])
        e1, dx1, ea, dctx, sums1, db1 = mlp_back(dx2, e2, slope, n1, s1, w_eo, w2, small)
        sum1.cross(e1)
        wide0, wide1 = wide_outer(me, after(y1, sum1.token), e1, ctx, ea)
        sum1.cross(wide0)
        wide0, wide1 = after((wide0, wide1), sum1.token)
        sum2 = Reduction([wide0], [wide1])
        sum2.cross()
        back = [backward(0, after(dctx, sum1.token, sum2.token), (0, 0, 0, 0))]
        sum2.cross(back[0][0])
        sum1.along(sum2.token)
        back.append(backward(1, after(dctx, sum1.token, sum2.token), (1, 1, 1, 1)))
        sum2.along(back[1][0])
        every = slice(None)
        r2 = contract_weight.shape[0] // 2
        contract_plan = [(0, 1, i, (slice(i * r2, (i + 1) * r2), every)) for i in range(2)]
        terms1 = settle(after(sum1.terms, sum2.token))
        grads0, grads1 = after((tuple(back[0][3:5]), tuple(back[1][3:5])), terms1)
        sum3 = Reduction([grads0], [grads1])
        sum3.cross()
        back.append(backward(2, after(dctx, sum3.token), (0, 0, 1, 1)))
        terms2 = settle(after(sum2.terms, back[2][0]))
        sum3.cross(terms2)
        d_small = small_deal(me, [b[-1] for b in back], sums1, sums2, after(db1, sum3.token))
        sum4 = Reduction([tuple(back[2][3:5]), tuple(d_small)], [tuple(back[2][5:7])])
        sum4.cross()
        contract_up = update(rates, contract_weight, mean_contract, square_contract, [after(terms1, sum4.token)], contract_plan)
        sum3.along(sum4.token, contract_up[0])
        sum4.cross(sum3.token)
        expand_weight, dx1 = after((expand_weight, dx1), sum4.token)
        in_grad = hidden_grad(back, dx1)
        terms3 = settle(after(sum3.terms, in_grad))
        sum4.along(terms3)
        expand_terms = [terms2]
        per = F // GC // 2
        narrow = lambda j: slice(j * GC, (j + 1) * GC)
        expand_plan = [(0, 1, j + (G if j >= per else 0), (every, narrow(j))) for j in range(2 * per)]
        attention_terms = [terms2, terms3] + sum4.terms
        attention_plan = [(0, 1, per + j, (4, every, narrow(j))) for j in range(G)]
        attention_plan += [(1, 1, 4 * g + m, (m, every, narrow(g))) for g in range(2) for m in range(4)]
        attention_plan += [(2, 4, m + (m > 1), (m, every, narrow(2))) for m in range(4)]
        attention_up, small_up = last_update(
            rates, (attention_weight, mean_attention, square_attention), (small_params, mean_small, square_small),
            attention_terms, attention_plan, (2, 4, 2))
    expand_up = update(rates, expand_weight, mean_expand, square_expand, expand_terms, expand_plan)
    if not fast:
        attention_up = update(rates, attention_weight, mean_attention, square_attention, attention_terms, attention_plan)
        small_up = update(rates, small_params, mean_small, square_small, [small_grad])
    ups = (attention_up, expand_up, contract_up, small_up)
    return (out, in_grad) + tuple(u[i] for i in range(4) for u in ups)


def solution(mesh):
    outer_rows = P(ALL, None)
    middle = P(None, ALL, None)
    inner_cols = P(None, ALL)
    table = (middle, outer_rows, outer_rows, inner_cols)
    tokens = P(ALL, None, None)
    in_specs = (tokens, P(ALL), outer_rows, tokens) + table * 3 + (P(), P())
    out_specs = (tokens, tokens) + table * 4
    fast = mesh.shape["dp"] == 8 and mesh.shape["fsdp"] == 4
    return jax.shard_map(
        functools.partial(shards, fast), mesh=mesh, in_specs=in_specs, out_specs=out_specs, check_vma=False
    )
```

```python
import functools
import math

import jax
import jax.numpy as jnp
import ml_dtypes
import numpy as np
from jax import lax
from jax.experimental import pallas as pl
from jax.experimental.pallas import tpu as pltpu
from jax.sharding import PartitionSpec as P

HEAD = 64
GC = 256
GH = GC // HEAD
TILE = 16
FC = 768
EPSILON = 1e-06
MASK_FILL = -1000000000.0
ALL = ("dp", "fsdp")
F32 = jnp.float32
BF = jnp.bfloat16
NT = (((1,), (1,)), ((), ()))
TN = (((0,), (0,)), ((), ()))


def dot(a, b):
    return jnp.dot(a, b, preferred_element_type=F32)


def dot_nt(a, b):
    return lax.dot_general(a, b, NT, preferred_element_type=F32)


def dot_tn(a, b):
    return lax.dot_general(a, b, TN, preferred_element_type=F32)


def sds(shape, dtype):
    return jax.ShapeDtypeStruct(shape, dtype)


def seqs(*tail):
    return pl.BlockSpec((1,) + tail, lambda s, *_: (s,) + (0,) * len(tail))


def whole(*shape):
    return pl.BlockSpec(shape, lambda *_: (0,) * len(shape), pipeline_mode=pl.Buffered(1))


def turned_small(width):
    return pl.BlockSpec((1, width, GC), lambda s: (2 * width // GC, 0, 0), pipeline_mode=pl.Buffered(1))


def params(mib):
    return pltpu.CompilerParams(vmem_limit_bytes=mib << 20)


def cost(us):
    return pl.CostEstimate(flops=int(us * 1.1e9), bytes_accessed=int(us * 3.5e6), transcendentals=0)


def rel_table(length, width):
    places = length - np.arange(2 * length, dtype=np.float32)
    half_width = width // 2
    frequency = np.exp(np.arange(half_width, dtype=np.float32) * np.float32(-2.0 * math.log(10000.0) / width))
    angles = places[:, None] * frequency[None, :]
    return np.concatenate([np.sin(angles), np.cos(angles)], axis=1).astype(ml_dtypes.bfloat16)


X, Y, CORE, Z = 1, 2, 4, 8
HALVES = ((X, Y), (Y, X))


def pairs(bit):
    return [(d, d ^ bit) for d in range(32)]


def swap(a, bit):
    return lax.ppermute(a, ALL, pairs(bit))


def flat_of(rel, half):
    low, high = HALVES[half]
    return (rel & 3) * Z + (rel >> 2 & 1) * low + (rel >> 3 & 1) * high + (rel >> 4 & 1) * CORE


def after(x, *earlier):
    return lax.optimization_barrier((x, earlier))[0]


def assemble_kernel(stacked, me_ref, *refs):
    ins, outs = refs[:8], refs[8:]
    for half in range(2):
        for rel in range(32):
            k = jnp.bitwise_xor(me_ref[0], flat_of(rel, half))
            src = ins[4 * half + rel // 8]
            for i in range(src.shape[1]):
                if stacked[half]:
                    outs[half][i, k] = src[rel % 8, i]
                else:
                    outs[half][k, i] = src[rel % 8, i]


def small_call(body, shapes, dtype, *ins, mib=32):
    return pl.pallas_call(
        body,
        in_specs=[pl.BlockSpec(memory_space=pltpu.VMEM)] * len(ins),
        out_specs=[pl.BlockSpec(memory_space=pltpu.VMEM)] * len(shapes),
        out_shape=[sds(shape, dtype) for shape in shapes],
        cost_estimate=cost(2),
        compiler_params=params(mib),
    )(*ins)


def halve(parts, split, mib=32):
    n, r, c = parts[0].shape

    def body(*refs):
        first, second = refs[-2:]
        for k, ref in enumerate(refs[:-2]):
            first[k] = ref[:split]
            second[k] = ref[split:]

    return small_call(body, [(len(parts), split, r, c), (len(parts), n - split, r, c)], parts[0].dtype, *parts, mib=mib)


def double(halves, got):
    def body(a, b, a_got, b_got, a_out, b_out):
        for mine, other, out in ((a, a_got, a_out), (b, b_got, b_out)):
            m = mine.shape[0]
            out[:m] = mine[...]
            out[m:] = other[...]

    shapes = [(2 * h.shape[0],) + h.shape[1:] for h in halves]
    return small_call(body, shapes, halves[0].dtype, *halves, *got)


def parcels(attention, expand, contract, small):
    r, F = expand.shape
    V = small.shape[0]
    C = F // FC
    G = attention.shape[2] // GC

    def near_body(att_ref, small_ref, out, pad):
        pad[...] = jnp.zeros_like(pad)
        pad[0:V, 0:r] = small_ref[...]
        turned = pad[...].T
        for g in range(G):
            for i, m in ((0, 0), (G, 1), (2 * G + 1, 2), (3 * G + 1, 3)):
                out[i + g] = att_ref[m, :, g * GC : (g + 1) * GC].astype(BF)
        out[2 * G] = jnp.concatenate([turned[0:r, :], jnp.zeros((r, GC - 128), F32)], axis=1).astype(BF)

    def wide_body(att_ref, exp_ref, con_ref, out):
        for i in range(C):
            out[i] = exp_ref[:, i * FC : (i + 1) * FC].astype(BF)
            out[C + 1 + i] = con_ref[i * r : (i + 1) * r, :].astype(BF)
        out[C] = att_ref[4].astype(BF)

    near = pl.pallas_call(
        near_body,
        in_specs=[pl.BlockSpec(memory_space=pltpu.VMEM)] * 2,
        out_specs=pl.BlockSpec(memory_space=pltpu.VMEM),
        out_shape=sds((4 * G + 1, r, GC), BF),
        scratch_shapes=[pltpu.VMEM((128, 128), F32)],
        cost_estimate=cost(1),
        compiler_params=params(58),
    )(attention, small)
    far = lambda gate: small_call(wide_body, [(2 * C + 1, r, FC)], BF, after(attention, gate), expand, contract, mib=58)[0]
    return near, far


class Gather:
    def __init__(self, me, part, split, stacked=(True, True)):
        self.me, self.part, self.split, self.stacked = me, part, split, stacked
        self.along = [part]

    def far(self, *ks, then=()):
        part = after(self.part, then) if then else self.part
        self.along += [swap(part, k * Z) for k in ks]
        return self.along[-1]

    def plane(self, *earlier):
        along = after(self.along, *earlier) if earlier else self.along
        self.halves = halve(along, self.split, 32 if self.part.shape[2] == GC else 58)
        self.got = [swap(h, HALVES[i][0]) for i, h in enumerate(self.halves)]
        return self.halves

    def plane_again(self, *earlier):
        halves, got = after((self.halves, self.got), *earlier) if earlier else (self.halves, self.got)
        self.firsts = double(halves, got)
        self.seconds = [swap(h, HALVES[i][1]) for i, h in enumerate(self.firsts)]
        return self.firsts

    def cores(self, *earlier):
        firsts, seconds = after((self.firsts, self.seconds), *earlier) if earlier else (self.firsts, self.seconds)
        self.pieces = []
        for f, s in zip(firsts, seconds):
            self.pieces += [f, s, swap(f, CORE), swap(s, CORE)]
        return firsts, seconds

    def result(self, *earlier):
        pieces = after(self.pieces, *earlier) if earlier else self.pieces
        n, r, c = self.part.shape
        wide = 128 if c == GC else 384
        counts = [self.split, n - self.split]
        specs = [pl.BlockSpec((8, m, r, wide), lambda j: (0, 0, 0, j)) for m in counts for _ in range(4)]
        shapes, outs = [], []
        for m, stacked in zip(counts, self.stacked):
            lead = (m, 32) if stacked else (32, m)
            shapes.append(sds(lead + (r, c), self.part.dtype))
            outs.append(pl.BlockSpec(lead + (r, wide), lambda j: (0, 0, 0, j)))
        out = pl.pallas_call(
            functools.partial(assemble_kernel, self.stacked),
            grid=(c // wide,),
            in_specs=[pl.BlockSpec(memory_space=pltpu.SMEM)] + specs,
            out_specs=outs,
            out_shape=shapes,
            cost_estimate=cost(4),
            compiler_params=params(50 if c > GC else 58),
        )(self.me, *pieces)
        return [o.reshape(m, 32 * r, c) if stacked else o.reshape(32 * m * r, c) for o, m, stacked in zip(out, counts, self.stacked)]


def join_kernel(plan, *refs):
    n = 1 + max(w for blocks in plan for _, terms in blocks for w, _ in terms)
    ins, outs = refs[:n], refs[n:]
    for out, blocks in zip(outs, plan):
        for place, terms in blocks:
            total = None
            for w, at in terms:
                v = ins[w][at].astype(F32)
                total = v if total is None else total + v
            out[place] = total.astype(BF)


def join(plan, shapes, ins):
    return pl.pallas_call(
        functools.partial(join_kernel, plan),
        in_specs=[pl.BlockSpec(memory_space=pltpu.VMEM)] * len(ins),
        out_specs=[pl.BlockSpec(memory_space=pltpu.VMEM)] * len(shapes),
        out_shape=[sds(shape, BF) for shape in shapes],
        cost_estimate=cost(1),
        compiler_params=params(32),
    )(*ins)


def settle(terms):
    def body(*refs):
        total = refs[0][...].astype(F32)
        for ref in refs[1:-1]:
            total += ref[...].astype(F32)
        refs[-1][...] = total

    return small_call(body, [terms[0].shape], F32, *terms)[0]


class Reduction:
    def __init__(self, *halves):
        self.halves = []
        for h, parts in enumerate(halves):
            self.halves.append([(k, swap(s, CORE)) for k, s in parts])
        self.token = None

    def add(self, *halves):
        for mine, parts in zip(self.halves, halves):
            mine += [(k, swap(s, CORE)) for k, s in parts]

    def flat(self, earlier):
        halves = after(self.halves, *earlier) if earlier else self.halves
        ins, at = [], []
        for parts in halves:
            blocks = []
            for terms in parts:
                blocks += [[(len(ins) + t, b) for t in range(len(terms))] for b in range(terms[0].shape[1])]
                ins += terms
            at.append(blocks)
        return ins, at, ins[0].shape[2:]

    def cross(self, *earlier):
        ins, at, tail = self.flat(earlier)
        n = ins[0].shape[0] // 2
        bit = 1 if n == 8 else 0
        plan, shapes = [], []
        for blocks in at:
            for far in range(2):
                plan.append([((j, b), [(w, (far * n + j, i)) for w, i in terms]) for j in range(n) for b, terms in enumerate(blocks)])
                shapes.append((n, len(blocks)) + tail)
        out = join(plan, shapes, ins)
        self.halves = [[(out[2 * h], swap(out[2 * h + 1], HALVES[h][bit]))] for h in range(2)]
        self.token = out

    def direct(self, *earlier):
        ins, at, tail = self.flat(earlier)
        count = sum(len(blocks) for blocks in at)
        plan = []
        for q in range(4):
            places = []
            b = 0
            for h, blocks in enumerate(at):
                lead = 4 * (q if h == 0 else (q >> 1) + 2 * (q & 1))
                for terms in blocks:
                    places += [((j, b), [(w, (lead + j, i)) for w, i in terms]) for j in range(4)]
                    b += 1
            plan.append(places)
        out = join(plan, [(4, count) + tail] * 4, ins)
        self.halves = [[tuple([out[0]] + [swap(out[q], (q & 1) * X + (q >> 1) * Y) for q in range(1, 4)])]]
        self.token = out

    def along(self, *earlier, also=()):
        groups = [r.flat(earlier) for r in (self,) + tuple(also)]
        ins, places, tail = [], [[] for _ in range(4)], groups[0][2]
        b = 0
        for more, at, _ in groups:
            base = len(ins)
            ins += more
            for blocks in at:
                for terms in blocks:
                    for k in range(4):
                        places[k].append((b, [(base + w, (k, i)) for w, i in terms]))
                    b += 1
        out = join(places, [(b,) + tail] * 4, ins)
        self.terms = [out[0]] + [swap(out[k], k * Z) for k in range(1, 4)]
        self.token = out


def prepare_kernel(lengths_ref, hidden_ref, key_ref, pooled_ref, low_ref, hidt_ref, lowt_ref, bias_ref, mask_ref, wide):
    hid = hidden_ref[0]
    half, L = pooled_ref.shape[1], hid.shape[0]
    hidt_ref[0] = hid.T
    columns = []
    for i in range(wide.shape[0]):
        wide[i] = hid[:, i * 128 : (i + 1) * 128].astype(F32)
        columns.append((wide[i, pl.ds(0, half, stride=2), :] + wide[i, pl.ds(1, half, stride=2), :]) * 0.5)
    pooled = jnp.concatenate(columns, axis=1)
    pooled_ref[0] = pooled
    low = pooled.astype(BF)
    low_ref[0] = low
    lowt_ref[0] = low.T
    place = lax.broadcasted_iota(jnp.int32, (1, L), 1)
    valid = (key_ref[pl.ds(pl.program_id(0), 1), :] == 1) & (place < lengths_ref[pl.program_id(0)])
    bias_ref[0] = jnp.where(valid, 0.0, MASK_FILL)
    twice = 2 * lax.broadcasted_iota(jnp.int32, (half, L), 0)
    token = lax.broadcasted_iota(jnp.int32, (half, L), 1)
    of = ((token == twice) | (token == twice + 1)).astype(F32).astype(BF)
    rows = jnp.broadcast_to(valid.astype(F32), (16, L)).astype(BF)
    mask_ref[0] = jnp.minimum(dot_nt(of, rows)[:, 0:1], 1.0)


def prepare(hidden, lengths, key_mask):
    B, L, D = hidden.shape
    R = L // 2
    return pl.pallas_call(
        prepare_kernel,
        grid=(B,),
        in_specs=[pl.BlockSpec(memory_space=pltpu.SMEM), seqs(L, D), whole(B, L)],
        out_specs=[seqs(R, D), seqs(R, D), seqs(D, L), seqs(D, R), seqs(1, L), seqs(R, 1)],
        out_shape=[sds((B, R, D), F32), sds((B, R, D), BF), sds((B, D, L), BF), sds((B, D, R), BF), sds((B, 1, L), F32),
                   sds((B, R, 1), F32)],
        scratch_shapes=[pltpu.VMEM((D // 128, L, 128), F32)],
        cost_estimate=cost(6),
        compiler_params=params(58),
    )(lengths, hidden, key_mask)


def attend_kernel(start, per, hidden_ref, pooled_ref, wq_ref, wk_ref, wv_ref, wr_ref, table_ref, small_ref, bias_ref, *refs):
    ctx_ref, probs_ref, qu_ref, qw_ref, keys_ref, values_ref, rel_out, rel_ref = refs[-8:]
    half = hidden_ref.shape[1] // 2
    blk = half // 2
    step = pl.program_id(0)

    @pl.when((step == 0) | (lax.rem(start + step, per) == 0))
    def _():
        rel = dot(table_ref[...], wr_ref[0]).astype(BF)
        rel_ref[...] = rel
        rel_out[...] = rel

    hid = hidden_ref[0]
    small_ref = small_ref[0, :, 0:128].astype(F32).T
    q = dot(pooled_ref[0], wq_ref[0])
    qu = (q + small_ref[0:1, :]).astype(BF)
    qw = (q + small_ref[1:2, :]).astype(BF)
    qu_ref[0] = qu
    qw_ref[0] = qw
    keys_ref[0] = dot(hid, wk_ref[0]).astype(BF)
    values_ref[0] = (dot(hid, wv_ref[0]) + small_ref[2:3, :]).astype(BF)
    bias = bias_ref[0]
    lane = lax.broadcasted_iota(jnp.int32, (1, GC), 1)
    masks = [(lane >= h * HEAD) & (lane < (h + 1) * HEAD) for h in range(GH)]
    qu8 = qu.astype(F32) * 0.125
    qw8 = qw.astype(F32) * 0.125
    wide = 2 * half + 128
    for b in range(2):
        rows = slice(b * blk, (b + 1) * blk)
        m0 = half * (1 - b)
        quh = jnp.concatenate([jnp.where(m, qu8[rows], 0.0).astype(BF) for m in masks], axis=0)
        qwh = jnp.concatenate([jnp.where(m, qw8[rows], 0.0).astype(BF) for m in masks], axis=0)
        content = dot_nt(quh, keys_ref[0])
        placed = dot_nt(qwh, rel_ref[m0 : m0 + 3 * half, :])
        lows = []
        for h in range(GH):
            for r in range(0, blk, TILE):
                hr = slice(h * blk + r, h * blk + r + TILE)
                at = half - 128 - 2 * r // 128 * 128
                moved = pltpu.roll(placed[hr, at : at + wide], 2 * r % 128, 1, stride=2, stride_axis=0)[:, 128:]
                s = content[hr] + moved + bias
                top = jnp.max(s, axis=-1, keepdims=True)
                e = jnp.exp(s - top)
                p = e * (1.0 / jnp.sum(e, axis=-1, keepdims=True))
                probs_ref[0, 0, h, b * blk + r : b * blk + r + TILE, :] = p
                lows.append(p.astype(BF))
        c = dot(jnp.concatenate(lows, axis=0), values_ref[0])
        total = c[0:blk]
        for h in range(1, GH):
            total = jnp.where(masks[h], c[h * blk : (h + 1) * blk], total)
        ctx_ref[0, rows, :] = total.astype(BF)


def attend(start, stop, hidden, pooled_low, weights, table, bias, held=None):
    B, L, D = hidden.shape
    R = L // 2
    G = D // GC
    g = lambda i: (start + i) // B
    s = lambda i: lax.rem(start + i, B)
    seq = lambda r: pl.BlockSpec((1, r, D), lambda i: (s(i), 0, 0))
    mat = lambda base: pl.BlockSpec((1, D, GC), lambda i: (base + g(i), 0, 0))
    so = lambda r: pl.BlockSpec((1, r, GC), lambda i: (s(i), 0, g(i)))
    a, b = weights
    ins = [hidden, pooled_low, a, a, b, b, table, a, bias]
    specs = [seq(L), seq(R), mat(0), mat(G), mat(0), mat(G), whole(2 * L, D),
             pl.BlockSpec((1, GC, GC), lambda i: (2 * G, g(i), 0)), pl.BlockSpec((1, 1, L), lambda i: (s(i), 0, 0))]
    aliases = {}
    if held is not None:
        aliases = {len(ins) + i: i for i in range(7)}
        ins += list(held)
        specs += [pl.BlockSpec(memory_space=pl.ANY)] * 7
    return pl.pallas_call(
        functools.partial(attend_kernel, start, B),
        grid=(stop - start,),
        in_specs=specs,
        out_specs=[so(R), pl.BlockSpec((1, 1, GH, R, L), lambda i: (s(i), g(i), 0, 0, 0)), so(R), so(R), so(L), so(L),
                   pl.BlockSpec((2 * L, GC), lambda i: (0, g(i)))],
        out_shape=[sds((B, R, D), BF), sds((B, G, GH, R, L), F32), sds((B, R, D), BF), sds((B, R, D), BF),
                   sds((B, L, D), BF), sds((B, L, D), BF), sds((2 * L, D), BF)],
        scratch_shapes=[pltpu.VMEM((2 * L, GC), BF)],
        input_output_aliases=aliases,
        cost_estimate=cost(4 * (stop - start)),
        compiler_params=params(58),
    )(*ins)


def phi_and_slope(z):
    e = jnp.exp(z * z * (-0.5))
    t = 1.0 / (1.0 + (0.3275911 * 0.7071067811865476) * jnp.abs(z))
    poly = t * (0.127414796 + t * (-0.142248368 + t * (0.7107068705 + t * (-0.7265760135 + t * 0.5307027145))))
    tail = poly * e
    phi = jnp.where(z >= 0, 1.0 - tail, tail)
    return phi, phi + z * e * 0.3989422804014327


def norm(x):
    center = x - jnp.mean(x, axis=-1, keepdims=True)
    inv = lax.rsqrt(jnp.mean(center * center, axis=-1, keepdims=True) + EPSILON)
    return center * inv, inv


def norm_back(e, n, inv):
    return inv * (e - jnp.mean(e, axis=-1, keepdims=True) - n * jnp.mean(e * n, axis=-1, keepdims=True))


def add_rows(ref, *values):
    for k, v in enumerate(values):
        ref[k : k + 1, :] += jnp.sum(v, axis=0, keepdims=True)


def mlp_kernel(dealt, *refs):
    me_ref, ctx_ref, pooled_ref, cot_ref, mask_ref, exp_ref, w2_ref, turned_ref = refs[:8]
    out_ref, y1_ref, n1_ref, s1_ref, slope_ref, dx2_ref, e2_ref, sums_ref = refs[8:16]
    grads, (small_ref, inner_ref, e2_all, total) = refs[16:-4], refs[-4:]
    rows_here = pooled_ref.shape[1]
    mine = pl.ds(pl.multiple_of(pl.program_id(0) * rows_here, 16), rows_here)
    @pl.when(pl.program_id(0) == 0)
    def _():
        sums_ref[...] = jnp.zeros_like(sums_ref)
        small_ref[...] = turned_ref[0, :, 0:128].astype(F32).T

    row = lambda k: small_ref[k : k + 1, :]
    chunks = exp_ref.shape[0] - 1
    x1 = pooled_ref[0] + dot(ctx_ref[0], exp_ref[chunks]) + row(3)
    n1, inv1 = norm(x1)
    n1_ref[0] = n1
    s1_ref[0] = inv1
    y1 = n1 * row(4) + row(5)
    y1l = y1.astype(BF)
    y1_ref[0] = y1l
    x2 = y1 + row(6)
    for c in range(chunks):
        cs = slice(c * FC, (c + 1) * FC)
        z = dot(y1l, exp_ref[c]) + row(9 + c)
        phi, slope = phi_and_slope(z)
        inner = (z * phi).astype(BF)
        inner_ref[mine, cs] = inner
        slope_ref[0, :, cs] = slope
        x2 += dot(inner, w2_ref[cs, :])
    n2, inv2 = norm(x2)
    m = mask_ref[0]
    out_ref[0] = ((n2 * row(7) + row(8)) * m).astype(BF)
    dy2 = cot_ref[0].astype(F32) * m
    dx2 = norm_back(dy2 * row(7), n2, inv2)
    dx2_ref[0] = dx2
    e2 = dx2.astype(BF)
    e2_ref[0] = e2
    add_rows(sums_ref, dx2, dy2 * n2, dy2)
    e2_all[mine, :] = e2

    @pl.when(pl.program_id(0) == pl.num_programs(0) - 1)
    def _():
        for c in range(chunks):
            cs = slice(c * FC, (c + 1) * FC)
            v = dot_tn(inner_ref[:, cs], e2_all[...])
            if not dealt:
                grads[0][cs, :] = v
            else:
                total[cs, :] = v
        if dealt:
            r = grads[0].shape[2]
            for half in range(2):
                for rel in range(32):
                    k = jnp.bitwise_xor(me_ref[0], flat_of(rel, half))
                    at = pl.multiple_of(k * (2 * r) + half * r, 8)
                    grads[2 * half + rel // 16][rel % 16, 0] = total[pl.ds(at, r), :].astype(BF)


def mlp(me, ctx, pooled, cot, mask, expand, w2, small, dealt):
    B, R, D = pooled.shape
    F = w2.shape[0]
    grads = [sds((16, 1, F // 64, D), BF)] * 4 if dealt else [sds((F, D), F32)]
    return pl.pallas_call(
        functools.partial(mlp_kernel, dealt),
        grid=(B,),
        in_specs=[pl.BlockSpec(memory_space=pltpu.SMEM), seqs(R, D), seqs(R, D), seqs(R, D), seqs(R, 1), whole(*expand.shape), whole(F, D),
                  turned_small(D)],
        out_specs=[seqs(R, D), seqs(R, D), seqs(R, D), seqs(R, 1), seqs(R, F), seqs(R, D), seqs(R, D),
                   pl.BlockSpec((8, D), lambda s: (0, 0))] + [whole(*g.shape) for g in grads],
        out_shape=[sds((B, R, D), BF), sds((B, R, D), BF), sds((B, R, D), F32), sds((B, R, 1), F32),
                   sds((B, R, F), F32), sds((B, R, D), F32), sds((B, R, D), BF), sds((8, D), F32)] + grads,
        scratch_shapes=[pltpu.VMEM((128, D), F32), pltpu.VMEM((B * R, F), BF), pltpu.VMEM((B * R, D), BF), pltpu.VMEM((F, D), F32)],
        cost_estimate=cost(38),
        compiler_params=params(50),
    )(me, ctx, pooled, cot, mask, expand, w2, small)


def mlp_back_kernel(dx2_ref, e2_ref, slope_ref, n1_ref, s1_ref, exp_ref, w2_ref, turned_ref,
                    e1_ref, dx1_ref, ea_ref, dctx_ref, sums_ref, db1_ref, small_ref):
    @pl.when(pl.program_id(0) == 0)
    def _():
        small_ref[...] = turned_ref[0, :, 0:128].astype(F32).T
        sums_ref[...] = jnp.zeros_like(sums_ref)
        db1_ref[...] = jnp.zeros_like(db1_ref)

    chunks = exp_ref.shape[0] - 1
    e2 = e2_ref[0]
    dy1 = dx2_ref[0]
    for c in range(chunks):
        cs = slice(c * FC, (c + 1) * FC)
        dz = dot_nt(e2, w2_ref[cs, :]) * slope_ref[0, :, cs]
        db1_ref[:, cs] += jnp.sum(dz, axis=0, keepdims=True)
        e1 = dz.astype(BF)
        e1_ref[0, :, cs] = e1
        dy1 += dot_nt(e1, exp_ref[c])
    n1 = n1_ref[0]
    dx1 = norm_back(dy1 * small_ref[4:5, :], n1, s1_ref[0])
    dx1_ref[0] = dx1
    ea = dx1.astype(BF)
    ea_ref[0] = ea
    dctx_ref[0] = dot_nt(ea, exp_ref[chunks]).astype(BF)
    add_rows(sums_ref, dx1, dy1 * n1, dy1)


def mlp_back(dx2, e2, slope, n1, s1, expand, w2, small):
    B, R, D = dx2.shape
    F = w2.shape[0]
    return pl.pallas_call(
        mlp_back_kernel,
        grid=(B,),
        in_specs=[seqs(R, D), seqs(R, D), seqs(R, F), seqs(R, D), seqs(R, 1), whole(*expand.shape), whole(F, D),
                  turned_small(D)],
        out_specs=[seqs(R, F), seqs(R, D), seqs(R, D), seqs(R, D), pl.BlockSpec((8, D), lambda s: (0, 0)),
                   pl.BlockSpec((1, F), lambda s: (0, 0))],
        out_shape=[sds((B, R, F), BF), sds((B, R, D), F32), sds((B, R, D), BF), sds((B, R, D), BF), sds((8, D), F32),
                   sds((1, F), F32)],
        scratch_shapes=[pltpu.VMEM((128, D), F32)],
        cost_estimate=cost(21),
        compiler_params=params(50),
    )(dx2, e2, slope, n1, s1, expand, w2, small)


def deal(half, me, total_ref, put):
    r = total_ref.shape[0] // 32
    for rel in range(32):
        k = jnp.bitwise_xor(me, flat_of(rel, half))
        put(rel // 16, rel % 16, total_ref[pl.ds(pl.multiple_of(k * r, 8), r), :].astype(BF))


def outer_kernel(half, me_ref, a_ref, b_ref, keep_ref, send_ref, turned, total):
    B, R, M = a_ref.shape

    @pl.when(pl.program_id(0) == 0)
    def _():
        turned[...] = a_ref[...].reshape(B * R, M).T

    total[...] = dot(turned[...], b_ref[...].reshape(B * R, b_ref.shape[2]))

    def put(sent, i, v):
        for j in range(v.shape[1] // GC):
            (send_ref if sent else keep_ref)[i, j] = v[:, j * GC : (j + 1) * GC]

    deal(half, me_ref[0], total, put)


def outer_plain_kernel(a_ref, b_ref, out_ref):
    B, R, M = a_ref.shape
    out_ref[...] = dot_tn(a_ref[...].reshape(B * R, M), b_ref[...].reshape(B * R, b_ref.shape[2]))


def outer(me, a, b, cols, half=None, blocks=None):
    B, R, M = a.shape
    N = b.shape[2]
    first, count = blocks or (0, N // cols)
    specs = [pl.BlockSpec((B, R, M), lambda j: (0, 0, 0)), pl.BlockSpec((B, R, cols), lambda j: (0, 0, first + j))]
    price = cost(2.0 * count)
    if half is None:
        return pl.pallas_call(
            outer_plain_kernel, grid=(count,), in_specs=specs,
            out_specs=pl.BlockSpec((M, cols), lambda j: (0, j)),
            out_shape=sds((M, N), F32), cost_estimate=price, compiler_params=params(32))(a, b)
    return pl.pallas_call(
        functools.partial(outer_kernel, half),
        grid=(count,),
        in_specs=[pl.BlockSpec(memory_space=pltpu.SMEM)] + specs,
        out_specs=[pl.BlockSpec((16, cols // GC, M // 32, GC), lambda j: (0, j, 0, 0))] * 2,
        out_shape=[sds((16, count * cols // GC, M // 32, GC), BF)] * 2,
        scratch_shapes=[pltpu.VMEM((M, B * R), BF), pltpu.VMEM((M, cols), F32)],
        cost_estimate=price,
        compiler_params=params(32),
    )(me, a, b)


def wide_outer_kernel(chunks, me_ref, y1_ref, e1_ref, ctx_ref, ea_ref, keep0, send0, keep1, send1, turned, total):
    B, R, D = y1_ref.shape
    j = pl.program_id(0)
    flat = lambda ref: ref[...].reshape(B * R, D)

    def dealt(half, base):
        def put(sent, i, v):
            ref = ((keep0, send0), (keep1, send1))[half][sent]
            for b in range(D // GC):
                ref[i, base + b] = v[:, b * GC : (b + 1) * GC]

        deal(half, me_ref[0], total, put)

    @pl.when(j == 0)
    def _():
        turned[...] = flat(y1_ref).T

    @pl.when(j < chunks)
    def _():
        total[...] = dot(turned[...], flat(e1_ref))

    @pl.when(j == chunks)
    def _():
        total[...] = dot_tn(flat(ctx_ref), flat(ea_ref))
        dealt(0, chunks // 2 * (D // GC))

    @pl.when(j < chunks // 2)
    def _():
        dealt(0, j * (D // GC))

    @pl.when((j >= chunks // 2) & (j < chunks))
    def _():
        dealt(1, (j - chunks // 2) * (D // GC))


def wide_outer(me, y1, e1, ctx, ea):
    B, R, D = y1.shape
    F = e1.shape[2]
    chunks = F // D
    n = D // GC
    shapes = [(16, m, D // 32, GC) for m in (chunks // 2 * n + n, chunks // 2 * n) for _ in range(2)]
    out = pl.pallas_call(
        functools.partial(wide_outer_kernel, chunks),
        grid=(chunks + 1,),
        in_specs=[pl.BlockSpec(memory_space=pltpu.SMEM), whole(B, R, D),
                  pl.BlockSpec((B, R, D), lambda j: (0, 0, jnp.minimum(j, chunks - 1))), whole(B, R, D), whole(B, R, D)],
        out_specs=[whole(*shape) for shape in shapes],
        out_shape=[sds(shape, BF) for shape in shapes],
        scratch_shapes=[pltpu.VMEM((D, B * R), BF), pltpu.VMEM((D, D), F32)],
        cost_estimate=cost(12),
        compiler_params=params(40),
    )(me, y1, e1, ctx, ea)
    return tuple(out[:2]), tuple(out[2:])


def small_deal_kernel(me_ref, *refs):
    sums, (sums1, sums2, db1, keep_ref, send_ref, total, turned) = refs[:-7], refs[-7:]
    D = sums1.shape[1]
    total[...] = jnp.zeros_like(total)
    for g, s in enumerate(sums):
        total[0:3, g * GC : (g + 1) * GC] = s[0:3, :]
    total[3:6, :] = sums1[0:3, :]
    total[6:9, :] = sums2[0:3, :]
    for i in range(db1.shape[1] // D):
        total[9 + i : 10 + i, :] = db1[0:1, i * D : (i + 1) * D]
    turned[...] = jnp.concatenate([total[...].T, jnp.zeros((D, GC - total.shape[0]), F32)], axis=1)

    def put(sent, i, v):
        (send_ref if sent else keep_ref)[i, 0] = v

    deal(0, me_ref[0], turned, put)


def small_deal(me, sums, sums1, sums2, db1):
    D = sums1.shape[1]
    n = 4 + len(sums)
    return pl.pallas_call(
        small_deal_kernel,
        in_specs=[pl.BlockSpec(memory_space=pltpu.SMEM)] + [pl.BlockSpec(memory_space=pltpu.VMEM)] * (n - 1),
        out_specs=[pl.BlockSpec(memory_space=pltpu.VMEM)] * 2,
        out_shape=[sds((16, 1, D // 32, GC), BF)] * 2,
        scratch_shapes=[pltpu.VMEM((128, D), F32), pltpu.VMEM((D, GC), F32)],
        cost_estimate=cost(2),
        compiler_params=params(24),
    )(me, *sums, sums1, sums2, db1)


def attend_back_kernel(plan, *refs):
    (me_ref, probs_ref, dctx_ref, qu_ref, qw_ref, keys_ref, values_ref, rel_ref, hidt_ref, lowt_ref, tablet_ref) = refs[:11]
    outs = refs[11 : 14]
    dq_ref, dk_ref, dv_ref = outs
    grads = refs[14 : -8]
    sums_ref = refs[-8]
    acc_q, acc_k, acc_v, acc_r, acc_dv, dkt, dvt = refs[-7:]
    step = pl.program_id(0)
    half, L = probs_ref.shape[3], probs_ref.shape[4]
    blk = half // 2

    @pl.when(step == 0)
    def _():
        for a in (acc_q, acc_k, acc_v, acc_r, acc_dv, sums_ref):
            a[...] = jnp.zeros_like(a)

    across = lax.broadcasted_iota(jnp.int32, (half, half), 0) + lax.broadcasted_iota(jnp.int32, (half, half), 1)
    flip = (across == half - 1).astype(F32).astype(BF)
    lane = lax.broadcasted_iota(jnp.int32, (1, GC), 1)
    dctx = dctx_ref[0]
    dctx_t = dctx.T
    qu_t = qu_ref[0].T
    qwr_t = dot(flip, qw_ref[0]).astype(BF).T
    keys = keys_ref[0]
    values = values_ref[0]
    masks = [(lane >= h * HEAD) & (lane < (h + 1) * HEAD) for h in range(GH)]
    dctx_wide = dctx.astype(F32)
    dp = dot_nt(jnp.concatenate([jnp.where(m, dctx_wide, 0.0).astype(BF) for m in masks], axis=0), values)
    backs = []
    moved = [[], []]
    for h in range(GH):
        sel = slice(h * HEAD, (h + 1) * HEAD)
        draws, lows = [], []
        for r in range(0, half, TILE):
            p = probs_ref[0, 0, h, r : r + TILE, :]
            t = p * dp[h * half + r : h * half + r + TILE]
            draws.append((t - p * jnp.sum(t, axis=-1, keepdims=True)).astype(BF))
            lows.append(p.astype(BF))
        draw = jnp.concatenate(draws, axis=0)
        dvt[sel, :] = dot(dctx_t[sel], jnp.concatenate(lows, axis=0))
        both = dot(jnp.concatenate([qu_t[sel], flip], axis=0), draw)
        dkt[sel, :] = both[:HEAD] * 0.125
        back = both[HEAD:]
        backs.append(back.astype(BF))
        for b in range(2):
            tiles = []
            for r in range(0, blk, TILE):
                x = jnp.concatenate([back[b * blk + r : b * blk + r + TILE], jnp.zeros((TILE, 128), F32)], axis=1)
                x = pltpu.roll(x, 2 + 2 * r % 128, 1, stride=2, stride_axis=0).astype(BF)
                none = jnp.zeros((TILE, 128), BF)
                tiles.append(jnp.concatenate([x, none] if r < blk // 2 else [none, x], axis=1))
            x = jnp.concatenate(tiles, axis=0)
            m0 = half * b
            acc_r[sel, m0 : m0 + 3 * half] += dot(qwr_t[sel, b * blk : (b + 1) * blk], x)
            moved[b].append(x)
    alone = lambda v, n: functools.reduce(lambda t, h: jnp.where(masks[h], v[h * n : (h + 1) * n], t), range(1, GH), v[0:n])
    dqu = alone(dot(jnp.concatenate(backs, axis=0), keys), half)
    dqw = jnp.concatenate(
        [alone(dot(jnp.concatenate(moved[b], axis=0), rel_ref[half * b : half * b + 3 * half, :]), blk) for b in range(2)], axis=0
    )
    dqu = dqu * 0.125
    dqw = dqw * 0.125
    dq = dot(flip, (dqu + dqw).astype(BF)).astype(BF)
    dk = dkt[...].astype(BF).T
    dvf = dvt[...]
    dv = dvf.astype(BF).T
    dq_ref[0] = dq
    dk_ref[0] = dk
    dv_ref[0] = dv
    acc_dv[...] += dvf
    add_rows(sums_ref, dqu, dqw)
    acc_q[...] += dot(lowt_ref[0], dq)
    acc_k[...] += dot(hidt_ref[0], dk)
    acc_v[...] += dot(hidt_ref[0], dv)

    @pl.when(step == pl.num_programs(0) - 1)
    def _():
        sums_ref[2:3, :] = jnp.sum(acc_dv[...].T, axis=0, keepdims=True)
        dr = acc_r[...] * 0.125
        hi = dr.astype(BF)
        lo = (dr - hi.astype(F32)).astype(BF)
        tt = tablet_ref[...]
        if plan is None:
            for i, a in enumerate((acc_q, acc_k, acc_v)):
                grads[0][i] = a[...]
            grads[0][3] = dot_nt(tt, hi) + dot_nt(tt, lo)
        else:
            for i in range(4):
                half = plan[i]
                at = plan[:i].count(half)
                base = 2 * sorted(set(plan)).index(half)
                acc = (acc_q, acc_k, acc_v, acc_q)[i]
                if i == 3:
                    acc_q[...] = dot_nt(tt, hi) + dot_nt(tt, lo)

                def put(sent, j, v):
                    grads[base + sent][j, at] = v

                deal(half, me_ref[0], acc, put)


def attend_back(me, g, probs, dctx, qu, qw, keys, values, rel, hid_t, low_t, table_t, plan=None):
    B, R, D = qu.shape
    L = 2 * R
    so = lambda r: pl.BlockSpec((1, r, GC), lambda s: (s, 0, g))
    if plan is None:
        grad_specs = [pl.BlockSpec((4, D, GC), lambda s: (0, 0, 0))]
        grad_shapes = [sds((4, D, GC), F32)]
    else:
        sizes = [(16, plan.count(h), D // 32, GC) for h in sorted(set(plan)) for _ in range(2)]
        grad_specs = [whole(*size) for size in sizes]
        grad_shapes = [sds(size, BF) for size in sizes]
    return pl.pallas_call(
        functools.partial(attend_back_kernel, plan),
        grid=(B,),
        in_specs=[pl.BlockSpec(memory_space=pltpu.SMEM),
                  pl.BlockSpec((1, 1, GH, R, L), lambda s: (s, g, 0, 0, 0)), so(R), so(R), so(R), so(L), so(L),
                  pl.BlockSpec((2 * L, GC), lambda s: (0, g)), seqs(D, L), seqs(D, R), whole(D, 2 * L)],
        out_specs=[seqs(R, GC), seqs(L, GC), seqs(L, GC)] + grad_specs + [pl.BlockSpec((8, GC), lambda s: (0, 0))],
        out_shape=[sds((B, R, GC), BF), sds((B, L, GC), BF), sds((B, L, GC), BF)] + grad_shapes + [sds((8, GC), F32)],
        scratch_shapes=[pltpu.VMEM((D, GC), F32)] * 3 + [pltpu.VMEM((GC, 2 * L), F32)] + [pltpu.VMEM((GC, L), F32)] * 3,
        cost_estimate=cost(22),
        compiler_params=params(34),
    )(me, probs, dctx, qu, qw, keys, values, rel, hid_t, low_t, table_t)


def input_grad_kernel(at, *refs):
    groups = len(at)
    dqs, dks, dvs = refs[:groups], refs[groups : 2 * groups], refs[2 * groups : 3 * groups]
    dx1_ref, weights, out_ref, wide = refs[3 * groups], refs[3 * groups + 1 : -2], refs[-2], refs[-1]
    half = dx1_ref.shape[1]
    shared = dx1_ref[0]
    total = None
    for g in range(groups):
        wq, wk, wv = (weights[a][i] for a, i in at[g])
        shared += dot_nt(dqs[g][0], wq)
        t = dot_nt(dks[g][0], wk) + dot_nt(dvs[g][0], wv)
        total = t if total is None else total + t
    shared = shared * 0.5
    for i in range(wide.shape[0]):
        cs = slice(i * 128, (i + 1) * 128)
        wide[i, pl.ds(0, half, stride=2), :] = shared[:, cs]
        wide[i, pl.ds(1, half, stride=2), :] = shared[:, cs]
        out_ref[0, :, cs] = (total[:, cs] + wide[i]).astype(BF)


def input_grad(dqs, dks, dvs, dx1, weights, at):
    B, R, D = dx1.shape
    L = 2 * R
    G = len(dqs)
    return pl.pallas_call(
        functools.partial(input_grad_kernel, at),
        grid=(B,),
        in_specs=[seqs(R, GC)] * G + [seqs(L, GC)] * (2 * G) + [seqs(R, D)] + [whole(*w.shape) for w in weights],
        out_specs=seqs(L, D),
        out_shape=sds((B, L, D), BF),
        scratch_shapes=[pltpu.VMEM((D // 128, L, 128), F32)],
        cost_estimate=cost(10),
        compiler_params=params(40),
    )(*dqs, *dks, *dvs, dx1, *weights)


def adamw(weight, moment, second, gradient, rates):
    new_moment = rates[1] * moment + (1.0 - rates[1]) * gradient
    new_second = rates[2] * second + (1.0 - rates[2]) * gradient * gradient
    moment_hat = new_moment / rates[4]
    second_hat = new_second / rates[5]
    new_weight = weight - rates[0] * (moment_hat / (jnp.sqrt(second_hat) + 1e-08) + rates[3] * weight)
    return (new_weight, new_moment, new_second)


def update_kernel(plan, rates_ref, w_ref, m_ref, v_ref, *refs):
    terms, (grad_ref, w_out, m_out, v_out) = refs[:-4], refs[-4:]
    rates = [rates_ref[i] for i in range(6)]
    for first, count, block, dest in plan:
        g = None
        for t in terms[first : first + count]:
            v = (t[...] if block is None else t[block]).astype(F32)
            g = v if g is None else g + v
        grad_ref[dest] = g
        w_out[dest], m_out[dest], v_out[dest] = adamw(w_ref[dest], m_ref[dest], v_ref[dest], g, rates)


def update(rates, w, m, v, terms, plan=None):
    plan = plan or [(0, len(terms), None, (slice(None),) * w.ndim)]
    return pl.pallas_call(
        functools.partial(update_kernel, plan),
        in_specs=[pl.BlockSpec(memory_space=pltpu.SMEM)] + [pl.BlockSpec(memory_space=pltpu.VMEM)] * (3 + len(terms)),
        out_specs=[pl.BlockSpec(memory_space=pltpu.VMEM)] * 4,
        out_shape=[sds(w.shape, F32)] * 4,
        cost_estimate=cost(2),
        compiler_params=params(24),
    )(rates, w, m, v, *terms)


def last_update_kernel(plan, small_at, rates_ref, *refs):
    ins, (pad, *_) = refs[:-9], refs[-1:]
    att, small, terms = ins[:3], ins[3:6], ins[6:]
    outs = refs[-9:-1]
    update_kernel(plan, rates_ref, *att, *terms, *outs[:4])
    first, count, block = small_at
    g = sum(t[block].astype(F32) for t in terms[first : first + count])
    V, r = small[0].shape
    pad[...] = jnp.zeros_like(pad)
    pad[0:r, :] = g[:, 0:128]
    pad[...] = pad[...].T
    rates = [rates_ref[i] for i in range(6)]
    g = pad[0:V, 0:r]
    outs[4][...] = g
    outs[5][...], outs[6][...], outs[7][...] = adamw(small[0][...], small[1][...], small[2][...], g, rates)


def last_update(rates, attention, small, terms, plan, small_at):
    like = [attention[0]] * 4 + [small[0]] * 4
    out = pl.pallas_call(
        functools.partial(last_update_kernel, plan, small_at),
        in_specs=[pl.BlockSpec(memory_space=pltpu.SMEM)] + [pl.BlockSpec(memory_space=pltpu.VMEM)] * (6 + len(terms)),
        out_specs=[pl.BlockSpec(memory_space=pltpu.VMEM)] * 8,
        out_shape=[sds(a.shape, F32) for a in like],
        scratch_shapes=[pltpu.VMEM((128, 128), F32)],
        cost_estimate=cost(3),
        compiler_params=params(24),
    )(rates, *attention, *small, *terms)
    return out[:4], out[4:]


def shards(fast, hidden, lengths, key_mask, cotangent, attention_weight, expand_weight, contract_weight, small_params,
           mean_attention, mean_expand, mean_contract, mean_small,
           square_attention, square_expand, square_contract, square_small, update_step, update_rates):
    B, L, D = hidden.shape
    R = L // 2
    F = expand_weight.shape[1]
    G = D // GC
    C = F // FC
    H = C // 2
    r = attention_weight.shape[1]
    V = small_params.shape[0]
    me = (lax.axis_index("dp") * lax.axis_size("fsdp") + lax.axis_index("fsdp")).astype(jnp.int32).reshape(1)

    table = rel_table(L, D)
    table, table_t = jnp.asarray(table), jnp.asarray(np.ascontiguousarray(table.T))

    def correction():
        return jnp.concatenate([update_rates, 1.0 - jnp.power(update_rates[1:3], update_step[0].astype(F32))])

    at = tuple(((0, g), (0, G + g), (1, g)) for g in range(G))
    if fast:
        first, third = parcels(attention_weight, expand_weight, contract_weight, small_params)
        gate1 = Gather(me, first, 2 * G + 1)
        gate1.far(1, 2, 3)
        pooled, pooled_low, hid_t, low_t, bias, mask = prepare(hidden, lengths, key_mask)
        rates = correction()
        third = third(pooled_low)
        token = gate1.plane(pooled_low, rates, third)
        gate2 = Gather(me, third, C + 1, (True, False))
        near = (gate2.far(1, then=token), gate2.far(2, then=token))
        token = gate1.plane_again(near)
        last = gate2.far(3, then=token)
        token = gate1.cores(last)
        token = gate2.plane(token)
        weights = gate1.result()
        low = after(pooled_low, token)
        steps = B * G
        stops = (steps // 4, steps - 1, steps)
        held = attend(0, stops[0], hidden, low, weights, table, bias)
        low = after(low, gate2.plane_again(held[0]))
        held = attend(stops[0], stops[1], hidden, low, weights, table, bias, held)
        low = after(low, gate2.cores(held[0]))
        held = attend(stops[1], stops[2], hidden, low, weights, table, bias, held)
        w_eo, w2 = gate2.result(held[0])
    else:
        cut = lambda a, c: a.astype(BF).reshape(r, -1, c).transpose(1, 0, 2)
        small_t = jnp.pad(small_params.T, ((0, 0), (0, GC - V))).astype(BF)[None]
        cols = [cut(attention_weight[i], GC) for i in range(4)]
        full = lambda a: lax.all_gather(a, ALL, axis=1, tiled=True)
        first = full(jnp.concatenate(cols[:2] + [small_t] + cols[2:], axis=0))
        w_eo = full(jnp.concatenate([cut(expand_weight, FC), cut(attention_weight[4], FC)], axis=0))
        w2 = lax.all_gather(contract_weight.astype(BF), ALL, axis=0, tiled=True)
        weights = (first[: 2 * G + 1], first[2 * G + 1 :])
        pooled, pooled_low, hid_t, low_t, bias, mask = prepare(hidden, lengths, key_mask)
        rates = correction()
        held = attend(0, B * G, hidden, pooled_low, weights, table, bias)
    ctx, probs, qu, qw, keys, values, rel = held
    small = weights[0]
    out, y1, n1, s1, slope, dx2, e2, sums2, *d_contract = mlp(me, ctx, pooled, cotangent, mask, w_eo, w2, small, fast)

    def backward(g, dctx, plan=None):
        return attend_back(me, g, probs, dctx, qu, qw, keys, values, rel, hid_t, low_t, table_t, plan)

    def hidden_grad(back, dx1):
        return input_grad([b[0] for b in back], [b[1] for b in back], [b[2] for b in back], dx1, weights, at)

    if not fast:
        scatter = lambda a, d: lax.psum_scatter(a, ALL, scatter_dimension=d, tiled=True)
        e1, dx1, ea, dctx, sums1, db1 = mlp_back(dx2, e2, slope, n1, s1, w_eo, w2, small)
        back = [backward(g, dctx) for g in range(G)]
        in_grad = hidden_grad(back, dx1)
        d_att = jnp.concatenate([b[3] for b in back], axis=2)
        d_att = jnp.concatenate([d_att, outer(me, ctx, ea, 384)[None]], axis=0)
        d_small = jnp.concatenate([b[-1][0:3] for b in back], axis=1)
        d_small = jnp.concatenate([d_small, sums1[0:3], sums2[0:3], db1.reshape(-1, D)], axis=0)
        attention_terms, attention_plan = [scatter(d_att, 1)], None
        expand_terms, expand_plan = [scatter(outer(me, y1, e1, FC), 0)], None
        contract_terms = [scatter(d_contract[0], 0)]
        contract_up = update(rates, contract_weight, mean_contract, square_contract, contract_terms)
        small_grad = scatter(d_small, 1)
    else:
        half0, half1 = tuple(d_contract[:2]), tuple(d_contract[2:])
        sum1 = Reduction([half0], [half1])
        e1, dx1, ea, dctx, sums1, db1 = mlp_back(dx2, e2, slope, n1, s1, w_eo, w2, small)
        sum1.cross(e1)
        wide0, wide1 = wide_outer(me, after(y1, sum1.token), e1, ctx, ea)
        sum1.cross(wide0)
        wide0, wide1 = after((wide0, wide1), sum1.token)
        sum2 = Reduction([wide0], [wide1])
        sum2.cross()
        back = [backward(0, after(dctx, sum1.token, sum2.token), (0, 0, 0, 0))]
        sum2.cross(back[0][0])
        sum1.along(sum2.token)
        back.append(backward(1, after(dctx, sum1.token, sum2.token), (1, 1, 1, 1)))
        sum2.along(back[1][0])
        every = slice(None)
        r2 = contract_weight.shape[0] // 2
        contract_plan = [(0, 1, i, (slice(i * r2, (i + 1) * r2), every)) for i in range(2)]
        terms1 = settle(after(sum1.terms, sum2.token))
        grads0, grads1 = after((tuple(back[0][3:5]), tuple(back[1][3:5])), terms1)
        sum3 = Reduction([grads0], [grads1])
        sum3.cross()
        back.append(backward(2, after(dctx, sum3.token), (0, 0, 1, 1)))
        terms2 = settle(after(sum2.terms, back[2][0]))
        sum3.cross(terms2)
        d_small = small_deal(me, [b[-1] for b in back], sums1, sums2, after(db1, sum3.token))
        sum4 = Reduction([tuple(back[2][3:5]), tuple(d_small)], [tuple(back[2][5:7])])
        sum4.cross()
        contract_up = update(rates, contract_weight, mean_contract, square_contract, [after(terms1, sum4.token)], contract_plan)
        sum3.along(sum4.token, contract_up[0])
        sum4.cross(sum3.token)
        expand_weight, dx1 = after((expand_weight, dx1), sum4.token)
        in_grad = hidden_grad(back, dx1)
        terms3 = settle(after(sum3.terms, in_grad))
        sum4.along(terms3)
        expand_terms = [terms2]
        per = F // GC // 2
        narrow = lambda j: slice(j * GC, (j + 1) * GC)
        expand_plan = [(0, 1, j + (G if j >= per else 0), (every, narrow(j))) for j in range(2 * per)]
        attention_terms = [terms2, terms3] + sum4.terms
        attention_plan = [(0, 1, per + j, (4, every, narrow(j))) for j in range(G)]
        attention_plan += [(1, 1, 4 * g + m, (m, every, narrow(g))) for g in range(2) for m in range(4)]
        attention_plan += [(2, 4, m + (m > 1), (m, every, narrow(2))) for m in range(4)]
        attention_up, small_up = last_update(
            rates, (attention_weight, mean_attention, square_attention), (small_params, mean_small, square_small),
            attention_terms, attention_plan, (2, 4, 2))
    expand_up = update(rates, expand_weight, mean_expand, square_expand, expand_terms, expand_plan)
    if not fast:
        attention_up = update(rates, attention_weight, mean_attention, square_attention, attention_terms, attention_plan)
        small_up = update(rates, small_params, mean_small, square_small, [small_grad])
    ups = (attention_up, expand_up, contract_up, small_up)
    return (out, in_grad) + tuple(u[i] for i in range(4) for u in ups)


def solution(mesh):
    outer_rows = P(ALL, None)
    middle = P(None, ALL, None)
    inner_cols = P(None, ALL)
    table = (middle, outer_rows, outer_rows, inner_cols)
    tokens = P(ALL, None, None)
    in_specs = (tokens, P(ALL), outer_rows, tokens) + table * 3 + (P(), P())
    out_specs = (tokens, tokens) + table * 4
    fast = mesh.shape["dp"] == 8 and mesh.shape["fsdp"] == 4
    return jax.shard_map(
        functools.partial(shards, fast), mesh=mesh, in_specs=in_specs, out_specs=out_specs, check_vma=False
    )
```
